256 devices in a mesh: dp: 8 (over y, x_hi), tm: 32 (over z, x_lo, core).
Axes of the slice: x: 4 (x_hi: 2, x_lo: 2; x = x_hi * 2 + x_lo), y: 4, z: 8, core: 2. Of those that a mesh axis runs over, the one named last changes fastest.
Arguments:
- features: bfloat16 [8, 4096, 1024], P('dp', 'tm'), may hold values from -20 to 20
- context: bfloat16 [8, 4096, 1024], P('dp', 'tm'), may hold values from -20 to 20
- predictor: bfloat16 [1024, 2, 1024], replicated, may hold values from -0.1875 to 0.1875
- projection: bfloat16 [1024, 1024], replicated, may hold values from -0.1875 to 0.1875
- lengths: int32 [8, 32], P('dp', 'tm'), may hold values from 128 to 128, as said below
- frame_mask: int32 [8, 4096], P('dp', 'tm'), may hold values 0 or 1
Outputs:
- loss: float32 [], replicated
- grad_pred: float32 [1024, 2, 1024], P(('dp', 'tm'))
- grad_proj: float32 [1024, 1024], P(('dp', 'tm'))
The draws below stay inside these ranges and needn't reach their ends.
Inputs may be any that keep to these rules, and one draw needn't show every extreme that they name: `lengths`: every entry is a multiple of 128; some entry equals 128.
All inputs are finite; a program needn't handle non-finite values. No bound on the sum of `frame_mask` on one device may be relied on, other than what follows from the above.
Results may differ from the reference program's by a relative error of at most 0.014.
The reference program's roundings to bfloat16 on the way count: a program that leaves them out, or rounds other values in their place, can miss the bound.
Values may be sent and summed in bfloat16 or wider, within the bound.
No kernel may reach another device: no remote copies, remote signals or barrier semaphores. Data moves between devices by JAX's collectives and lax.ppermute only.
A program may use at most 128 MiB of HBM per device.

```python
import jax
import jax.numpy as jnp
from jax import lax

D = 1024
K = 2
GRAIN = 128
F = 128
FRAMES = 4096
N_DP = 8
N_TM = 32


def rough_rows(key):
    first = jax.random.fold_in(key, 0)
    return jnp.clip(jax.random.normal(first, (N_DP, FRAMES, D), jnp.float32), -6.0, 6.0)


def draw_features(key, part):
    key = jax.random.fold_in(key, 11)
    return rough_rows(key).astype(jnp.bfloat16)


def draw_context(key, part):
    key = jax.random.fold_in(key, 23)
    return rough_rows(key).astype(jnp.bfloat16)


def draw_lengths(key, part):
    key = jax.random.fold_in(key, 37)
    first, second = jax.random.split(key)
    picked = GRAIN * jax.random.randint(first, (N_DP * N_TM,), 1, F // GRAIN + 1)
    chosen = jax.random.randint(second, (), 0, N_DP * N_TM)
    places = jnp.arange(N_DP * N_TM, dtype=jnp.int32)
    filled = jnp.where(places == chosen, F, picked)
    return filled.reshape(N_DP, N_TM).astype(jnp.int32)


def set_ends(drawn, rng, smallest, top_value):
    longest = drawn.shape.index(max(drawn.shape))
    spots = []
    for shift in (0, 1):
        where = [jax.random.randint(jax.random.fold_in(rng, axis), (), 0, length) for axis, length in enumerate(drawn.shape)]
        where[longest] = (where[longest] + shift) % drawn.shape[longest]
        spots.append(tuple(where))
    return drawn.at[spots[0]].set(smallest).at[spots[1]].set(top_value)


def scatter_about(own_key, dims, scale, most, held_as=jnp.bfloat16):
    array = jax.random.normal(own_key, dims, jnp.float32) * scale
    return jnp.minimum(jnp.maximum(array, -most), most).astype(held_as)


def setup_inputs(seed: int = 0) -> dict:
    keys = jax.random.split(jax.random.key(seed), 7)
    features = draw_features(jax.random.fold_in(keys[6], 71), 0)
    context = draw_context(jax.random.fold_in(keys[6], 71), 0)
    predictor = scatter_about(keys[2], (D, K, D), D ** -0.5, 0.1875)
    projection = scatter_about(keys[3], (D, D), D ** -0.5, 0.1875)
    lengths = draw_lengths(jax.random.fold_in(keys[6], 71), 0)
    frame_mask = set_ends((jax.random.randint(keys[5], (N_DP, FRAMES), 0, 8) < 7).astype(jnp.int32), jax.random.fold_in(keys[5], 1), 0, 1)
    return {"features": features, "context": context, "predictor": predictor, "projection": projection, "lengths": lengths, "frame_mask": frame_mask}


def window_math(query, negatives, neg_usable, extended, ext_usable, inv_count, horizons, model_width):
    frames = query.shape[0]
    own_usable = ext_usable[:frames]
    logit_scale = model_width ** -0.5
    loss_sum = jnp.zeros((), jnp.float32)
    neg_grad = jnp.zeros((negatives.shape[0], model_width), jnp.float32)
    ext_grad = jnp.zeros((2 * frames, model_width), jnp.float32)
    pred_parts = []
    for horizon in range(1, horizons + 1):
        query_k = query[:, (horizon - 1) * model_width:horizon * model_width]
        positive_codes = extended[horizon:horizon + frames]
        active = own_usable * ext_usable[horizon:horizon + frames]
        positive = jnp.sum(query_k.astype(jnp.float32) * positive_codes.astype(jnp.float32), axis=1) * logit_scale
        scores = lax.dot_general(query_k, negatives, (((1,), (1,)), ((), ())), preferred_element_type=jnp.float32) * logit_scale
        scores = jnp.where(neg_usable[None, :] > 0, scores, -1e30)
        row_max = jnp.maximum(positive, jnp.max(scores, axis=1))
        log_total = row_max + jnp.log(jnp.exp(positive - row_max) + jnp.sum(jnp.exp(scores - row_max[:, None]), axis=1))
        loss_sum = loss_sum + jnp.sum(active * (log_total - positive))
        weight = inv_count * logit_scale * active
        neg_coef = (weight[:, None] * jnp.exp(scores - log_total[:, None])).astype(jnp.bfloat16)
        pos_coef = (weight * (jnp.exp(positive - log_total) - 1.0)).astype(jnp.bfloat16)
        pred_k = jnp.dot(neg_coef, negatives, preferred_element_type=jnp.float32)
        pred_k = pred_k + pos_coef.astype(jnp.float32)[:, None] * positive_codes.astype(jnp.float32)
        pred_parts.append(pred_k.astype(jnp.bfloat16))
        neg_grad = neg_grad + lax.dot_general(neg_coef, query_k, (((0,), (0,)), ((), ())), preferred_element_type=jnp.float32)
        shifted = pos_coef.astype(jnp.float32)[:, None] * query_k.astype(jnp.float32)
        ext_grad = ext_grad + jnp.pad(shifted, ((horizon, frames - horizon), (0, 0)))
    return loss_sum, jnp.concatenate(pred_parts, axis=1), neg_grad, ext_grad


def reference(features, context, predictor, projection, lengths, frame_mask):
    flat_features = features.reshape(N_DP * FRAMES, D)
    flat_context = context.reshape(N_DP * FRAMES, D)
    encoded = jnp.dot(flat_features, projection, preferred_element_type=jnp.float32).astype(jnp.bfloat16).reshape(N_DP, FRAMES, D)
    predicted = jnp.dot(flat_context, predictor.reshape(D, K * D), preferred_element_type=jnp.float32).astype(jnp.bfloat16).reshape(N_DP, FRAMES, K * D)
    positions = jnp.arange(FRAMES, dtype=jnp.int32)
    limits = jnp.repeat(lengths, F, axis=1)
    usable = ((frame_mask == 1) & ((positions % F)[None, :] < limits)).astype(jnp.float32)
    count = jnp.zeros((), jnp.float32)
    for horizon in range(1, K + 1):
        count = count + jnp.sum(usable[:, :FRAMES - horizon] * usable[:, horizon:])
    inv_count = 1.0 / jnp.maximum(count, 1.0)
    padded_codes = jnp.pad(encoded, ((0, 0), (2 * F, 2 * F), (0, 0)))
    padded_usable = jnp.pad(usable, ((0, 0), (2 * F, 2 * F)))

    def one_window(grads, index):
        group = index // N_TM
        window = index % N_TM
        base = window * F
        zero = jnp.zeros((), jnp.int32)
        block = lax.dynamic_slice(padded_codes, (group, base, zero), (1, 5 * F, D))[0]
        block_usable = lax.dynamic_slice(padded_usable, (group, base), (1, 5 * F))[0]
        query = lax.dynamic_slice(predicted, (group, base, zero), (1, F, K * D))[0]
        negatives = jnp.concatenate([block[:2 * F], block[3 * F:]], axis=0)
        neg_usable = jnp.concatenate([block_usable[:2 * F], block_usable[3 * F:]], axis=0)
        extended = block[2 * F:4 * F]
        ext_usable = block_usable[2 * F:4 * F]
        loss_sum, pred_grad, neg_grad, ext_grad = window_math(query, negatives, neg_usable, extended, ext_usable, inv_count, K, D)
        block_grad = jnp.concatenate([neg_grad[:2 * F], ext_grad[:F], ext_grad[F:] + neg_grad[2 * F:3 * F], neg_grad[3 * F:]], axis=0)
        current = lax.dynamic_slice(grads, (group, base, zero), (1, 5 * F, D))
        grads = lax.dynamic_update_slice(grads, current + block_grad[None], (group, base, zero))
        return grads, (loss_sum, pred_grad)

    indices = jnp.arange(N_DP * N_TM, dtype=jnp.int32)
    start_grads = jnp.zeros((N_DP, FRAMES + 4 * F, D), jnp.float32)
    grads, (losses, pred_grads) = lax.scan(one_window, start_grads, indices)
    code_grad = grads[:, 2 * F:2 * F + FRAMES].astype(jnp.bfloat16).reshape(N_DP * FRAMES, D)
    pred_flat = pred_grads.reshape(N_DP * FRAMES, K * D)
    grad_pred = lax.dot_general(flat_context, pred_flat, (((0,), (0,)), ((), ())), preferred_element_type=jnp.float32).reshape(D, K, D)
    grad_proj = lax.dot_general(flat_features, code_grad, (((0,), (0,)), ((), ())), preferred_element_type=jnp.float32)
    loss = jnp.sum(losses) * inv_count
    return loss, grad_pred, grad_proj
```

```python
import jax
import jax.numpy as jnp
from jax import lax
from jax.sharding import Mesh, PartitionSpec as P

DP = ("y", "xh")
TM = ("z", "xl", "core")
ALL = DP + TM
F32 = jnp.float32
BF16 = jnp.bfloat16


def shifted(block, distance):
    size = 1
    for name in TM:
        size *= lax.axis_size(name)
    route = [(i - distance, i) for i in range(size) if 0 <= i - distance < size]
    return lax.ppermute(block, TM, route)


def other_core(block):
    return lax.ppermute(block, "core", [(0, 1), (1, 0)])


def to_bf16_grid(value):
    return lax.reduce_precision(value, 8, 7)


def rows_dot(a, b):
    return lax.dot_general(a, b, (((1,), (1,)), ((), ())), preferred_element_type=F32)


def cols_dot(a, b):
    return lax.dot_general(a, b, (((0,), (0,)), ((), ())), preferred_element_type=F32)


def per_device(features, context, predictor, projection, lengths, frame_mask):
    frames, width = features.shape[1], features.shape[2]
    horizons = predictor.shape[1]
    scale = width ** (-0.5)
    feat, ctx = features[0], context[0]
    windows = 1
    for name in TM:
        windows *= lax.axis_size(name)
    recordings = lax.axis_size("y") * lax.axis_size("xh")
    devices = windows * recordings
    tm = lax.axis_index(TM)
    rec = lax.axis_index(DP)
    core = lax.axis_index("core")

    encoded = jnp.dot(feat, projection, preferred_element_type=F32).astype(BF16)
    enc_near = {d: shifted(encoded, d) for d in (2, 1, -1, -2)}
    ctx_near = {d: shifted(ctx, d) for d in (2, 1, -1, -2)}
    ctx_ring = lax.all_gather(ctx, "y")
    feat_ring = lax.all_gather(feat, "y")

    positions = jnp.arange(frames, dtype=jnp.int32)
    usable = ((frame_mask[0] == 1) & (positions < lengths[0, 0])).astype(F32)
    flags = lax.all_to_all(
        jnp.broadcast_to(usable[None], (devices, frames)), ALL, 0, 0, tiled=True
    )
    whole = flags.reshape(recordings, windows * frames)
    count = jnp.zeros((), F32)
    for horizon in range(1, horizons + 1):
        count = count + jnp.sum(whole[:, :-horizon] * whole[:, horizon:])
    inv_count = 1.0 / jnp.maximum(count, 1.0)
    mine = lax.dynamic_slice(flags, (rec * windows, 0), (windows, frames))
    mine = jnp.pad(mine, ((2, 3), (0, 0)))
    near = lax.dynamic_slice(mine, (tm, 0), (6, frames))
    line = near.reshape(-1)
    active_near = [
        (line[: 5 * frames] * line[h : h + 5 * frames]).reshape(5, frames)
        for h in range(1, horizons + 1)
    ]
    neg_usable = jnp.concatenate([near[0], near[1], near[3], near[4]])

    weights = predictor.reshape(width, horizons * width)
    predicted = jnp.dot(ctx, weights, preferred_element_type=F32).astype(BF16)
    negatives = jnp.concatenate([enc_near[2], enc_near[1], enc_near[-1], enc_near[-2]], axis=0)
    extended = jnp.concatenate([encoded, enc_near[-1][:horizons]], axis=0)
    loss_sum = jnp.zeros((), F32)
    stats, pred_delta, pos_coefs = [], [], []
    for h in range(1, horizons + 1):
        query = predicted[:, (h - 1) * width : h * width]
        codes = extended[h : h + frames].astype(F32)
        active = active_near[h - 1][2]
        positive = jnp.sum(query.astype(F32) * codes, axis=1) * scale
        scores = rows_dot(query, negatives) * scale
        scores = jnp.where(neg_usable[None, :] > 0, scores, -1e30)
        row_max = jnp.maximum(positive, jnp.max(scores, axis=1))
        log_total = row_max + jnp.log(
            jnp.exp(positive - row_max) + jnp.sum(jnp.exp(scores - row_max[:, None]), axis=1)
        )
        loss_sum = loss_sum + jnp.sum(active * (log_total - positive))
        weight = inv_count * scale * active
        neg_coef = (weight[:, None] * jnp.exp(scores - log_total[:, None])).astype(BF16)
        pos_coef = to_bf16_grid(weight * (jnp.exp(positive - log_total) - 1.0))
        delta = jnp.dot(neg_coef, negatives, preferred_element_type=F32)
        pred_delta.append((delta + pos_coef[:, None] * codes).astype(BF16))
        stats.append(log_total)
        pos_coefs.append(pos_coef)

    packet = jnp.stack(stats + pos_coefs)
    packet_near = {d: shifted(packet, d) for d in (2, 1, -1, -2)}
    ctx_beside = jnp.concatenate([ctx_near[2], ctx_near[1], ctx_near[-1], ctx_near[-2]], axis=0)
    pred_beside = jnp.dot(ctx_beside, weights, preferred_element_type=F32).astype(BF16)
    code_delta = jnp.zeros((frames, width), F32)
    for h in range(1, horizons + 1):
        query = pred_beside[:, (h - 1) * width : h * width]
        act = active_near[h - 1]
        weight = inv_count * scale * jnp.concatenate([act[0], act[1], act[3], act[4]])
        log_total = jnp.concatenate([packet_near[d][h - 1] for d in (2, 1, -1, -2)])
        scores = rows_dot(encoded, query) * scale
        scores = jnp.where(usable[:, None] > 0, scores, -1e30)
        neg_coef = (weight[None, :] * jnp.exp(scores - log_total[None, :])).astype(BF16)
        code_delta = code_delta + jnp.dot(neg_coef, query, preferred_element_type=F32)
        before = packet_near[1][horizons + h - 1][frames - h :]
        own = pos_coefs[h - 1][: frames - h]
        pos_rows = jnp.concatenate([before, own])
        query_rows = jnp.concatenate(
            [
                query[2 * frames - h : 2 * frames],
                predicted[: frames - h, (h - 1) * width : h * width],
            ]
        )
        code_delta = code_delta + pos_rows[:, None] * query_rows.astype(F32)
    code_delta = code_delta.astype(BF16)

    ring = ("y", "core")
    parts = lax.axis_size("y") * lax.axis_size("core")
    pred_cols, code_cols = horizons * width // parts, width // parts
    pd = jnp.concatenate(pred_delta, axis=1).reshape(frames, parts, pred_cols)
    cd = code_delta.reshape(frames, parts, code_cols)
    deltas = jnp.concatenate([pd, cd], axis=2).transpose(1, 0, 2)
    deltas = lax.all_to_all(deltas, ring, 0, 0, tiled=True)
    deltas = deltas.reshape(lax.axis_size("y"), 2, frames, pred_cols + code_cols)
    same = jnp.where(core == 0, deltas[:, 0], deltas[:, 1])
    cross = jnp.where(core == 0, deltas[:, 1], deltas[:, 0])
    deltas = jnp.concatenate([same, cross], axis=0).reshape(parts * frames, pred_cols + code_cols)
    ctx_all = jnp.concatenate([ctx_ring, other_core(ctx_ring)], axis=0).reshape(parts * frames, width)
    feat_all = jnp.concatenate([feat_ring, other_core(feat_ring)], axis=0).reshape(
        parts * frames, width
    )
    pred_term = cols_dot(ctx_all, deltas[:, :pred_cols])
    code_term = cols_dot(feat_all, deltas[:, pred_cols:])

    owned = width // devices
    lanes = pred_cols + code_cols
    terms = jnp.concatenate([pred_term, code_term], axis=1).astype(BF16)
    terms = terms.reshape(devices, owned * lanes // 128, 128)
    high = to_bf16_grid(loss_sum)
    middle = to_bf16_grid(loss_sum - high)
    low = loss_sum - high - middle
    loss_row = jnp.zeros((1, 1, 128), F32).at[0, 0, :3].set(jnp.stack([high, middle, low]))
    loss_row = jnp.broadcast_to(loss_row.astype(BF16), (devices, 1, 128))
    sent = jnp.concatenate([terms, loss_row], axis=1)
    got = lax.all_to_all(sent, ALL, 0, 0, tiled=True).astype(F32)
    loss = jnp.sum(got[:, -1, :3]) * inv_count
    got = got[:, :-1].reshape(
        *(lax.axis_size(name) for name in ALL), owned, lanes
    )
    got = jnp.sum(got, axis=(1, 2, 3)).reshape(parts, owned, lanes).transpose(1, 0, 2)
    grad_pred = got[:, :, :pred_cols].reshape(owned, horizons, width)
    grad_proj = got[:, :, pred_cols:].reshape(owned, width)
    return (loss, grad_pred, grad_proj)


def solution(mesh):
    fine = Mesh(mesh.devices.reshape(4, 2, 8, 2, 2), ALL)
    placed = (P(DP, TM, None), P(DP, TM, None), P(), P(), P(DP, TM), P(DP, TM))
    return jax.shard_map(
        per_device,
        mesh=fine,
        in_specs=placed,
        out_specs=(P(), P(ALL, None, None), P(ALL, None)),
        check_vma=False,
    )
```

```python
import functools

import jax
import jax.numpy as jnp
from jax import lax
from jax.experimental import pallas as pl
from jax.experimental.pallas import tpu as pltpu
from jax.sharding import Mesh, PartitionSpec as P

DP = ("y", "xh")
TM = ("z", "xl", "core")
ALL = DP + TM
PLANE = ("xh", "z", "xl")
RING = ("y", "core")
F32 = jnp.float32
BF16 = jnp.bfloat16
REACH = 2


def size_of(names):
    size = 1
    for name in names:
        size *= lax.axis_size(name)
    return size


def window_at(block, offset):
    size = size_of(TM)
    return lax.ppermute(block, TM, [((i + offset) % size, i) for i in range(size)])


def other_core(block):
    return lax.ppermute(block, "core", [(0, 1), (1, 0)])


def rows_dot(a, b):
    return lax.dot_general(a, b, (((1,), (1,)), ((), ())), preferred_element_type=F32)


def cols_dot(a, b):
    return lax.dot_general(a, b, (((0,), (0,)), ((), ())), preferred_element_type=F32)


def delta_kernel(
    horizons, inv_ref, flags_ref, act_ref, own, low2, high2, low4, high4, odd,
    pred_m2, pred_m1, pred_0, pred_p1, pred_p2, out_ref, loss_ref, codes, code_acc,
):
    frames, width = own.shape
    scale = width ** (-0.5)
    parts = out_ref.shape[0]
    pred_cols, code_cols = horizons * width // parts, width // parts

    def put(window, block):
        codes[(window + 4) * frames : (window + 5) * frames] = block

    put(-4, low4[...])
    put(-3, odd[:frames])
    put(-2, low2[:frames])
    put(-1, odd[frames : 2 * frames])
    put(0, own[...])
    put(1, odd[2 * frames : 3 * frames])
    put(2, high2[:frames])
    put(3, odd[3 * frames : 4 * frames])
    put(4, high4[...])
    row = lax.broadcasted_iota(jnp.int32, (frames, frames), 0)
    col = lax.broadcasted_iota(jnp.int32, (frames, frames), 1)
    preds = {-2: pred_m2, -1: pred_m1, 0: pred_0, 1: pred_p1, 2: pred_p2}
    factor = inv_ref[0, 0] * scale
    loss = jnp.zeros((frames, 1), F32)
    first = True
    for window in (-2, -1, 1, 2, 0):
        base = (window + 2) * frames
        for step in range(horizons):
            ahead = step + 1
            query = preds[window][:, step * width : (step + 1) * width]
            scores = rows_dot(query, codes[base : base + 5 * frames]) * scale
            block = {
                d: scores[:, (d + 2) * frames : (d + 3) * frames] for d in range(-REACH, REACH + 1)
            }
            here, after = col == row + ahead, col == row + ahead - frames
            positive = jnp.sum(
                jnp.where(here, block[0], 0.0) + jnp.where(after, block[1], 0.0),
                axis=1,
                keepdims=True,
            )
            for d in (-2, -1, 1, 2):
                usable = flags_ref[window + d + 4 : window + d + 5, :]
                block[d] = jnp.where(usable > 0, block[d], -1e30)
            top = jnp.maximum(
                jnp.maximum(block[-2], block[-1]), jnp.maximum(block[1], block[2])
            )
            top = jnp.maximum(positive, jnp.max(top, axis=1, keepdims=True))
            total = sum(jnp.exp(block[d] - top) for d in (-2, -1, 1, 2))
            total = jnp.sum(total, axis=1, keepdims=True)
            log_total = top + jnp.log(jnp.exp(positive - top) + total)
            spot = (window + 2) * horizons + step
            active = act_ref[:, spot : spot + 1]
            weight = factor * active
            pos_coef = weight * (jnp.exp(positive - log_total) - 1.0)
            pos_here = jnp.where(here, pos_coef, 0.0).astype(BF16)
            pos_after = jnp.where(after, pos_coef, 0.0).astype(BF16)
            if window != 0:
                coef = (weight * jnp.exp(block[-window] - log_total)).astype(BF16)
                term = cols_dot(coef, query)
                if window == -1:
                    term = term + cols_dot(pos_after, query)
            else:
                coefs = {
                    d: (weight * jnp.exp(block[d] - log_total)).astype(BF16) for d in (-2, -1, 1, 2)
                }
                coefs[0] = pos_here
                wide = jnp.concatenate([coefs[d] for d in range(-REACH, REACH + 1)], axis=1)
                delta = jnp.dot(
                    wide, codes[base : base + 5 * frames], preferred_element_type=F32
                ) + jnp.dot(
                    pos_after, codes[base + 3 * frames : base + 4 * frames],
                    preferred_element_type=F32,
                )
                delta = delta.astype(BF16)
                for part in range(parts // horizons):
                    spot = step * (parts // horizons) + part
                    out_ref[spot, :, :pred_cols] = delta[:, part * pred_cols : (part + 1) * pred_cols]
                term = cols_dot(pos_here, query)
                loss = loss + active * (log_total - positive)
            if first:
                code_acc[...] = term
                first = False
            else:
                code_acc[...] += term
    for part in range(parts):
        out_ref[part, :, pred_cols:] = code_acc[:, part * code_cols : (part + 1) * code_cols].astype(
            BF16
        )
    loss_ref[...] = jnp.broadcast_to(jnp.sum(loss, axis=0, keepdims=True), loss_ref.shape)


def per_device(features, context, predictor, projection, lengths, frame_mask):
    frames, width = features.shape[1], features.shape[2]
    horizons = predictor.shape[1]
    feat, ctx = features[0], context[0]
    windows, recordings = size_of(TM), size_of(DP)
    devices = windows * recordings
    parts, plane = size_of(RING), size_of(PLANE)
    tm = lax.axis_index(TM)
    core = lax.axis_index("core")

    encoded = jnp.dot(feat, projection, preferred_element_type=F32).astype(BF16)
    both = jnp.concatenate([encoded, ctx], axis=0)
    low2, high2 = window_at(both, -2), window_at(both, 2)
    low4, high4 = window_at(encoded, -4), window_at(encoded, 4)
    slots = [low4, low2[:frames], encoded, high2[:frames], high4]
    side = [low2[frames:], ctx, high2[frames:]]
    swap = jnp.concatenate(
        [jnp.where(core == 0, b, a) for a, b in zip(slots, slots[1:])]
        + [jnp.where(core == 0, b, a) for a, b in zip(side, side[1:])],
        axis=0,
    )
    odd = other_core(swap)
    ctx_ring = lax.all_gather(ctx, "y")
    feat_ring = lax.all_gather(feat, "y")

    positions = jnp.arange(frames, dtype=jnp.int32)
    usable = ((frame_mask[0] == 1) & (positions < lengths[0, 0])).astype(F32)
    flags = lax.all_to_all(
        jnp.broadcast_to(usable[None], (windows, frames)), TM, 0, 0, tiled=True
    )
    line = flags.reshape(-1)
    count = jnp.zeros((), F32)
    for h in range(1, horizons + 1):
        count = count + jnp.sum(line[:-h] * line[h:])
    count = lax.all_to_all(jnp.broadcast_to(count, (recordings, 128)), DP, 0, 0, tiled=True)
    inv_count = 1.0 / jnp.maximum(jnp.sum(count[:, 0]), 1.0)
    near = lax.dynamic_slice(jnp.pad(flags, ((4, 5), (0, 0))), (tm, 0), (10, frames))
    line = near[2:8].reshape(-1)
    act = jnp.stack(
        [(line[: 5 * frames] * line[h : h + 5 * frames]).reshape(5, frames) for h in range(1, horizons + 1)],
        axis=1,
    ).reshape(5 * horizons, frames)
    act = jnp.pad(act, ((0, 16 - 5 * horizons), (0, 0))).T
    near = jnp.pad(near, ((0, 6), (0, 0)))

    weights = predictor.reshape(width, horizons * width)
    contexts = [low2[frames:], odd[4 * frames : 5 * frames], ctx, odd[5 * frames :], high2[frames:]]
    preds = [jnp.dot(c, weights, preferred_element_type=F32).astype(BF16) for c in contexts]
    pred_cols, code_cols = horizons * width // parts, width // parts
    lanes = pred_cols + code_cols
    vmem = pl.BlockSpec(memory_space=pltpu.VMEM)
    deltas, loss_part = pl.pallas_call(
        functools.partial(delta_kernel, horizons),
        out_shape=(
            jax.ShapeDtypeStruct((parts, frames, lanes), BF16),
            jax.ShapeDtypeStruct((8, 128), F32),
        ),
        in_specs=[pl.BlockSpec(memory_space=pltpu.SMEM)] + [vmem] * 13,
        out_specs=(vmem, vmem),
        scratch_shapes=[
            pltpu.VMEM((9 * frames, width), BF16),
            pltpu.VMEM((frames, width), F32),
        ],
        compiler_params=pltpu.CompilerParams(vmem_limit_bytes=40 * 2**20),
        cost_estimate=pl.CostEstimate(
            flops=2600000000, bytes_accessed=6000000, transcendentals=900000
        ),
    )(inv_count.reshape(1, 1), near, act, encoded, low2, high2, low4, high4, odd, *preds)
    loss_plane = lax.all_to_all(
        jnp.broadcast_to(loss_part[:1], (plane, 128)), PLANE, 0, 0, tiled=True
    )
    loss_plane = jnp.sum(loss_plane[:, 0])

    deltas = lax.all_to_all(deltas, RING, 0, 0, tiled=True)
    deltas = deltas.reshape(lax.axis_size("y"), 2, frames, lanes)
    same = jnp.where(core == 0, deltas[:, 0], deltas[:, 1]).reshape(-1, lanes)
    cross = jnp.where(core == 0, deltas[:, 1], deltas[:, 0]).reshape(-1, lanes)
    ctx_ring, feat_ring = ctx_ring.reshape(-1, width), feat_ring.reshape(-1, width)
    ctx_cross, feat_cross = other_core(ctx_ring), other_core(feat_ring)
    pred_term = cols_dot(ctx_ring, same[:, :pred_cols]) + cols_dot(ctx_cross, cross[:, :pred_cols])
    code_term = cols_dot(feat_ring, same[:, pred_cols:]) + cols_dot(feat_cross, cross[:, pred_cols:])

    owned = width // devices
    terms = jnp.concatenate([pred_term, code_term], axis=1).astype(BF16)
    terms = terms.reshape(lax.axis_size("y"), plane, 2 * owned, lanes).transpose(1, 0, 2, 3)
    terms = terms.reshape(plane, parts * owned, lanes)
    terms = lax.all_to_all(terms, PLANE, 0, 0, tiled=True)
    terms = jnp.sum(terms.astype(F32), axis=0).reshape(parts, owned, lanes)
    tail = jnp.broadcast_to(loss_plane, (parts, owned, lanes))
    got = lax.all_to_all(jnp.concatenate([terms, tail], axis=1), RING, 0, 0, tiled=True)
    loss = jnp.sum(got[:, owned, 0]) * inv_count
    got = got[:, :owned].transpose(1, 0, 2)
    grad_pred = got[:, :, :pred_cols].reshape(owned, horizons, width)
    grad_proj = got[:, :, pred_cols:].reshape(owned, width)
    return (loss, grad_pred, grad_proj)


def solution(mesh):
    fine = Mesh(mesh.devices.reshape(4, 2, 8, 2, 2), ALL)
    placed = (P(DP, TM, None), P(DP, TM, None), P(), P(), P(DP, TM), P(DP, TM))
    return jax.shard_map(
        per_device,
        mesh=fine,
        in_specs=placed,
        out_specs=(P(), P(ALL, None, None), P(ALL, None)),
        check_vma=False,
    )
```

```python
import functools

import jax
import jax.numpy as jnp
from jax import lax
from jax.experimental import pallas as pl
from jax.experimental.pallas import tpu as pltpu
from jax.sharding import Mesh, PartitionSpec as P

DP = ("y", "xh")
TM = ("z", "xl", "core")
ALL = DP + TM
PLANE = ("xh", "z", "xl")
RING = ("y", "core")
F32 = jnp.float32
BF16 = jnp.bfloat16
REACH = 2


def size_of(names):
    size = 1
    for name in names:
        size *= lax.axis_size(name)
    return size


def ring_shift(block, axes, offset):
    size = size_of(axes)
    return lax.ppermute(block, axes, [((i + offset) % size, i) for i in range(size)])


def window_at(block, offset):
    return ring_shift(block, TM, offset)


def other_core(block):
    return lax.ppermute(block, "core", [(0, 1), (1, 0)])


def ring_sum(value, axes):
    step = 1
    while step < size_of(axes):
        value = value + ring_shift(value, axes, step)
        step *= 2
    return value


def rows_dot(a, b):
    return lax.dot_general(a, b, (((1,), (1,)), ((), ())), preferred_element_type=F32)


def cols_dot(a, b):
    return lax.dot_general(a, b, (((0,), (0,)), ((), ())), preferred_element_type=F32)


def delta_kernel(
    horizons, core_ref, count_ref, flags_ref, act_ref, low4, low2, own, high2, high4,
    pred_m2, pred_0, pred_p2, feat_own, feat_low, feat_high, feat_side, ctx_own, ctx_low,
    ctx_high, projection, weights, out_ref, loss_ref, codes, code_acc, odd_feat, odd_ctx, odd_pred,
):
    frames, width = own.shape
    scale = width ** (-0.5)
    parts = out_ref.shape[0]
    pred_cols, code_cols = horizons * width // parts, width // parts
    core = core_ref[0, 0]

    @pl.when(core == 0)
    def _():
        for slot, block in enumerate((feat_side, feat_low, feat_own, feat_high)):
            odd_feat[slot * frames : (slot + 1) * frames] = block[...]
        odd_ctx[:frames] = ctx_low[...]
        odd_ctx[frames:] = ctx_own[...]

    @pl.when(core != 0)
    def _():
        for slot, block in enumerate((feat_low, feat_own, feat_high, feat_side)):
            odd_feat[slot * frames : (slot + 1) * frames] = block[...]
        odd_ctx[:frames] = ctx_own[...]
        odd_ctx[frames:] = ctx_high[...]

    for slot, block in enumerate((low4, low2, own, high2, high4)):
        codes[2 * slot * frames : (2 * slot + 1) * frames] = block[...]
    tile = 512
    for at in range(0, width, tile):
        part = jnp.dot(
            odd_feat[...], projection[:, at : at + tile], preferred_element_type=F32
        ).astype(BF16)
        for slot in range(4):
            base = (2 * slot + 1) * frames
            codes[base : base + frames, at : at + tile] = part[slot * frames : (slot + 1) * frames]
    for at in range(0, horizons * width, tile):
        odd_pred[:, at : at + tile] = jnp.dot(
            odd_ctx[...], weights[:, at : at + tile], preferred_element_type=F32
        ).astype(BF16)
    row = lax.broadcasted_iota(jnp.int32, (frames, frames), 0)
    col = lax.broadcasted_iota(jnp.int32, (frames, frames), 1)
    preds = {
        -2: pred_m2, -1: odd_pred.at[:frames], 0: pred_0, 1: odd_pred.at[frames:], 2: pred_p2
    }
    factor = (1.0 / jnp.maximum(count_ref[:, :1], 1.0)) * scale
    loss = jnp.zeros((frames, 1), F32)
    first = True
    for window in (-2, -1, 1, 2, 0):
        base = (window + 2) * frames
        for step in range(horizons):
            ahead = step + 1
            query = preds[window][:, step * width : (step + 1) * width]
            scores = rows_dot(query, codes[base : base + 5 * frames]) * scale
            block = {
                d: scores[:, (d + 2) * frames : (d + 3) * frames] for d in range(-REACH, REACH + 1)
            }
            here, after = col == row + ahead, col == row + ahead - frames
            positive = jnp.sum(
                jnp.where(here, block[0], 0.0) + jnp.where(after, block[1], 0.0),
                axis=1,
                keepdims=True,
            )
            for d in (-2, -1, 1, 2):
                usable = flags_ref[window + d + 4 : window + d + 5, :]
                block[d] = jnp.where(usable > 0, block[d], -1e30)
            top = jnp.maximum(
                jnp.maximum(block[-2], block[-1]), jnp.maximum(block[1], block[2])
            )
            top = jnp.maximum(positive, jnp.max(top, axis=1, keepdims=True))
            total = sum(jnp.exp(block[d] - top) for d in (-2, -1, 1, 2))
            total = jnp.sum(total, axis=1, keepdims=True)
            log_total = top + jnp.log(jnp.exp(positive - top) + total)
            spot = (window + 2) * horizons + step
            active = act_ref[:, spot : spot + 1]
            weight = factor * active
            pos_coef = weight * (jnp.exp(positive - log_total) - 1.0)
            pos_here = jnp.where(here, pos_coef, 0.0).astype(BF16)
            pos_after = jnp.where(after, pos_coef, 0.0).astype(BF16)
            if window != 0:
                coef = (weight * jnp.exp(block[-window] - log_total)).astype(BF16)
                term = cols_dot(coef, query)
                if window == -1:
                    term = term + cols_dot(pos_after, query)
            else:
                coefs = {
                    d: (weight * jnp.exp(block[d] - log_total)).astype(BF16) for d in (-2, -1, 1, 2)
                }
                coefs[0] = pos_here
                wide = jnp.concatenate([coefs[d] for d in range(-REACH, REACH + 1)], axis=1)
                delta = jnp.dot(
                    wide, codes[base : base + 5 * frames], preferred_element_type=F32
                ) + jnp.dot(
                    pos_after, codes[base + 3 * frames : base + 4 * frames],
                    preferred_element_type=F32,
                )
                delta = delta.astype(BF16)
                for part in range(parts // horizons):
                    spot = step * (parts // horizons) + part
                    out_ref[spot, :, :pred_cols] = delta[:, part * pred_cols : (part + 1) * pred_cols]
                term = cols_dot(pos_here, query)
                loss = loss + active * (log_total - positive)
            if first:
                code_acc[...] = term
                first = False
            else:
                code_acc[...] += term
    for part in range(parts):
        out_ref[part, :, pred_cols:] = code_acc[:, part * code_cols : (part + 1) * code_cols].astype(
            BF16
        )
    loss_ref[...] = jnp.broadcast_to(jnp.sum(loss, axis=0, keepdims=True), loss_ref.shape)


def term_kernel(pred_cols, core_ref, deltas, ctx_same, feat_same, ctx_cross, feat_cross, out_ref, held):
    parts, frames, _ = deltas.shape
    plane = out_ref.shape[0]
    core = core_ref[0, 0]
    for spot in range(parts // 2):
        rows = slice(spot * frames, (spot + 1) * frames)
        held[0, rows] = deltas[2 * spot + core]
        held[1, rows] = deltas[2 * spot + 1 - core]
    rows = 2 * ctx_same.shape[0] * 2 // parts
    for half in range(parts // 4):
        blocks = slice(half * rows, (half + 1) * rows)
        for same, cross, lanes in (
            (ctx_same, ctx_cross, slice(0, pred_cols)),
            (feat_same, feat_cross, slice(pred_cols, deltas.shape[2])),
        ):
            term = jnp.dot(same[blocks], held[0, :, lanes], preferred_element_type=F32)
            term = term + jnp.dot(cross[blocks], held[1, :, lanes], preferred_element_type=F32)
            term = term.reshape(2, plane, rows // plane // 2, -1)
            term = jnp.concatenate([term[0], term[1]], axis=1).astype(BF16)
            span = rows // plane
            out_ref[:, half * span : (half + 1) * span, lanes] = term


def per_device(features, context, predictor, projection, lengths, frame_mask):
    frames, width = features.shape[1], features.shape[2]
    horizons = predictor.shape[1]
    feat, ctx = features[0], context[0]
    windows, recordings = size_of(TM), size_of(DP)
    devices = windows * recordings
    parts, plane = size_of(RING), size_of(PLANE)
    tm = lax.axis_index(TM)
    core = lax.axis_index("core")

    feat_low, feat_high = window_at(feat, -2), window_at(feat, 2)
    ctx_low, ctx_high = window_at(ctx, -2), window_at(ctx, 2)
    feat_low4, feat_high4 = window_at(feat, -4), window_at(feat, 4)
    feat_side = jnp.where(core == 0, feat_high4, feat_low4)
    feat_x, ctx_x = other_core(feat), other_core(ctx)
    feat_low_x, feat_high_x = other_core(feat_low), other_core(feat_high)
    ctx_low_x, ctx_high_x = other_core(ctx_low), other_core(ctx_high)
    feat_side_x = other_core(feat_side)
    ctx_ring = lax.all_gather(ctx, "y")
    feat_ring = lax.all_gather(feat, "y")

    positions = lax.broadcasted_iota(jnp.int32, (1, frames), 1)
    usable = ((frame_mask == 1) & (positions < lengths)).astype(F32)
    usable_x = other_core(usable)
    chip = jnp.concatenate(
        [jnp.where(core == 0, usable, usable_x), jnp.where(core == 0, usable_x, usable)], axis=0
    )
    near = jnp.concatenate(
        [window_at(chip, -4), window_at(chip, -2), chip, window_at(chip, 2), window_at(chip, 4)]
    )
    place = tm - core - 4 + lax.broadcasted_iota(jnp.int32, (10, 1), 0)
    near = jnp.where((place >= 0) & (place < windows), near, 0.0)
    line = near.reshape(1, -1)
    acts = [line[:, : 9 * frames] * line[:, h : h + 9 * frames] for h in range(1, horizons + 1)]
    count = sum(jnp.sum(a[:, 4 * frames : 6 * frames]) for a in acts)
    count = jnp.broadcast_to(count, (1, 128))
    for axes in (("z",), ("xh", "xl"), ("y",)):
        count = ring_sum(count, axes)
    near = jnp.where(core == 0, near[:9], near[1:])
    acts = [
        jnp.where(core == 0, a[:, 2 * frames : 7 * frames], a[:, 3 * frames : 8 * frames]) for a in acts
    ]
    act = jnp.stack([a.reshape(5, frames) for a in acts], axis=1).reshape(5 * horizons, frames)
    act = jnp.pad(act, ((0, 16 - 5 * horizons), (0, 0))).T
    near = jnp.pad(near, ((0, 7), (0, 0)))

    weights = predictor.reshape(width, horizons * width)
    codes = [
        jnp.dot(f, projection, preferred_element_type=F32).astype(BF16)
        for f in (feat_low4, feat_low, feat, feat_high, feat_high4)
    ]
    preds = [
        jnp.dot(c, weights, preferred_element_type=F32).astype(BF16)
        for c in (ctx_low, ctx, ctx_high)
    ]
    pred_cols, code_cols = horizons * width // parts, width // parts
    lanes = pred_cols + code_cols
    smem = pl.BlockSpec(memory_space=pltpu.SMEM)
    vmem = pl.BlockSpec(memory_space=pltpu.VMEM)
    core_word = jnp.reshape(core, (1, 1)).astype(jnp.int32)
    deltas, loss_part = pl.pallas_call(
        functools.partial(delta_kernel, horizons),
        out_shape=(
            jax.ShapeDtypeStruct((parts, frames, lanes), BF16),
            jax.ShapeDtypeStruct((1, 128), F32),
        ),
        in_specs=[smem] + [vmem] * 20,
        out_specs=(vmem, vmem),
        scratch_shapes=[
            pltpu.VMEM((9 * frames, width), BF16),
            pltpu.VMEM((frames, width), F32),
            pltpu.VMEM((4 * frames, width), BF16),
            pltpu.VMEM((2 * frames, width), BF16),
            pltpu.VMEM((2 * frames, horizons * width), BF16),
        ],
        compiler_params=pltpu.CompilerParams(vmem_limit_bytes=32 * 2**20),
        cost_estimate=pl.CostEstimate(
            flops=5000000000, bytes_accessed=12000000, transcendentals=900000
        ),
    )(
        core_word, count, near, act, *codes, *preds, feat_x, feat_low_x, feat_high_x, feat_side_x,
        ctx_x, ctx_low_x, ctx_high_x, projection, weights,
    )

    deltas = lax.all_to_all(deltas, RING, 0, 0, tiled=True)
    ring_rows = [block.reshape(-1, width) for block in (ctx_ring, feat_ring)]
    ring_rows = ring_rows + [other_core(block) for block in ring_rows]
    terms = pl.pallas_call(
        functools.partial(term_kernel, pred_cols),
        out_shape=jax.ShapeDtypeStruct((plane, width // plane, lanes), BF16),
        in_specs=[smem] + [vmem] * 5,
        out_specs=vmem,
        scratch_shapes=[pltpu.VMEM((2, parts // 2 * frames, lanes), BF16)],
        compiler_params=pltpu.CompilerParams(vmem_limit_bytes=32 * 2**20),
        cost_estimate=pl.CostEstimate(flops=800000000, bytes_accessed=6000000, transcendentals=0),
    )(core_word, deltas, *[block.T for block in ring_rows])

    owned = width // devices
    loss_part = ring_sum(ring_sum(loss_part, ("z",)), ("xh", "xl"))
    terms = lax.all_to_all(terms, PLANE, 0, 0, tiled=True)
    terms = jnp.sum(terms.astype(F32), axis=0).reshape(parts, owned, lanes)
    tail = jnp.broadcast_to(loss_part[0, 0], (parts, owned, lanes))
    got = lax.all_to_all(jnp.concatenate([terms, tail], axis=1), RING, 0, 0, tiled=True)
    loss = jnp.sum(got[:, owned, 0]) * (1.0 / jnp.maximum(count[0, 0], 1.0))
    got = got[:, :owned].transpose(1, 0, 2)
    grad_pred = got[:, :, :pred_cols].reshape(owned, horizons, width)
    grad_proj = got[:, :, pred_cols:].reshape(owned, width)
    return (loss, grad_pred, grad_proj)


def solution(mesh):
    fine = Mesh(mesh.devices.reshape(4, 2, 8, 2, 2), ALL)
    placed = (P(DP, TM, None), P(DP, TM, None), P(), P(), P(DP, TM), P(DP, TM))
    return jax.shard_map(
        per_device,
        mesh=fine,
        in_specs=placed,
        out_specs=(P(), P(ALL, None, None), P(ALL, None)),
        check_vma=False,
    )
```

```python
import functools

import jax
import jax.numpy as jnp
from jax import lax
from jax.experimental import pallas as pl
from jax.experimental.pallas import tpu as pltpu
from jax.sharding import Mesh, PartitionSpec as P

DP = ("y", "xh")
TM = ("z", "xl", "core")
ALL = DP + TM
PLANE = ("xh", "z", "xl")
RING = ("y", "core")
F32 = jnp.float32
BF16 = jnp.bfloat16
REACH = 2


def size_of(names):
    size = 1
    for name in names:
        size *= lax.axis_size(name)
    return size


def ring_shift(block, axes, offset):
    size = size_of(axes)
    return lax.ppermute(block, axes, [((i + offset) % size, i) for i in range(size)])


def window_at(block, offset):
    return ring_shift(block, TM, offset)


def other_core(block):
    return lax.ppermute(block, "core", [(0, 1), (1, 0)])


def gathered_terms(value, axes):
    high = to_bf16_grid(value)
    middle = to_bf16_grid(value - high)
    terms = jnp.concatenate([high, middle, value - high - middle], axis=0).astype(BF16)
    return lax.all_gather(terms, axes)


def to_bf16_grid(value):
    return lax.reduce_precision(value, 8, 7)


def rows_dot(a, b):
    return lax.dot_general(a, b, (((1,), (1,)), ((), ())), preferred_element_type=F32)


def cols_dot(a, b):
    return lax.dot_general(a, b, (((0,), (0,)), ((), ())), preferred_element_type=F32)


def flags_kernel(horizons, windows, spot_ref, flags_ref, count_ref, near_ref, act_ref):
    devices, frames = flags_ref.shape
    device, tm = spot_ref[0, 0], spot_ref[0, 1]
    flags = flags_ref[...]
    row = lax.broadcasted_iota(jnp.int32, flags.shape, 0)
    lane = lax.broadcasted_iota(jnp.int32, flags.shape, 1)
    following = jnp.where(row % windows == windows - 1, 0.0, pltpu.roll(flags, devices - 1, 0))
    slot = lax.broadcasted_iota(jnp.int32, (devices, 16), 1)
    source = lax.broadcasted_iota(jnp.int32, (devices, 16), 0)
    total = jnp.zeros((1, frames), F32)
    act = jnp.zeros((frames, 16), F32)
    for h in range(1, horizons + 1):
        ahead = jnp.where(
            lane < frames - h,
            pltpu.roll(flags, frames - h, 1),
            pltpu.roll(following, frames - h, 1),
        )
        pairs = flags * ahead
        total = total + jnp.sum(pairs, axis=0, keepdims=True)
        window = slot // horizons - REACH
        pick = (source == device + window) & (slot % horizons == h - 1) & (window <= REACH)
        pick = pick & (tm + window >= 0) & (tm + window < windows)
        act = act + cols_dot(pairs.astype(BF16), jnp.where(pick, 1.0, 0.0).astype(BF16))
    act_ref[...] = act
    count_ref[...] = jnp.broadcast_to(jnp.sum(total, axis=1, keepdims=True), count_ref.shape)
    window = slot - 2 * REACH
    pick = (source == device + window) & (tm + window >= 0) & (tm + window < windows)
    near_ref[...] = cols_dot(jnp.where(pick, 1.0, 0.0).astype(BF16), flags.astype(BF16))


def pred_kernel(low2, ctx, high2, weights, out_ref, rows, sems):
    frames = ctx.shape[0]
    copies = [
        pltpu.make_async_copy(block, rows.at[pl.ds(slot * frames, frames)], sems.at[slot])
        for slot, block in enumerate(
            (low2.at[pl.ds(frames, frames)], ctx, high2.at[pl.ds(frames, frames)])
        )
    ]
    for copy in copies:
        copy.start()
    for copy in copies:
        copy.wait()
    tile = 512
    for at in range(0, weights.shape[1], tile):
        out_ref[:, at : at + tile] = jnp.dot(
            rows[...], weights[:, at : at + tile], preferred_element_type=F32
        ).astype(BF16)


def delta_kernel(
    horizons, core_ref, count_ref, flags_ref, act_ref, preds_ref, weights,
    both, low2, high2, low4, high4, both_x, low2_x, high2_x, side_x,
    out_ref, loss_ref, codes, code_acc, odd_ctx, odd_pred, sems,
):
    frames, width = low4.shape
    scale = width ** (-0.5)
    parts = out_ref.shape[0]
    pred_cols, code_cols = horizons * width // parts, width // parts
    core = core_ref[0, 0]

    def put(sem, block, start, held, slot):
        at = slot * frames
        if not isinstance(slot, int):
            at = pl.multiple_of(at, frames)
        return pltpu.make_async_copy(
            block.at[pl.ds(start, frames)], held.at[pl.ds(at, frames)], sems.at[sem]
        )

    ctx_copies = [
        put(0, low2_x, frames, odd_ctx, 1 - core),
        put(1, both_x, frames, odd_ctx, 2 - core),
        put(2, high2_x, frames, odd_ctx, 3 - core),
    ]
    code_copies = [
        put(3, low4, 0, codes, 0),
        put(4, low2, 0, codes, 2),
        put(5, both, 0, codes, 4),
        put(6, high2, 0, codes, 6),
        put(7, high4, 0, codes, 8),
        put(8, low2_x, 0, codes, 3 - 2 * core),
        put(9, both_x, 0, codes, 5 - 2 * core),
        put(10, high2_x, 0, codes, 7 - 2 * core),
        put(11, side_x, 0, codes, 1 + 6 * core),
    ]
    for copy in ctx_copies + code_copies:
        copy.start()
    for copy in ctx_copies:
        copy.wait()
    tile = 512
    for at in range(0, horizons * width, tile):
        odd_pred[:, at : at + tile] = jnp.dot(
            odd_ctx[frames : 3 * frames], weights[:, at : at + tile], preferred_element_type=F32
        ).astype(BF16)
    for copy in code_copies:
        copy.wait()
    row = lax.broadcasted_iota(jnp.int32, (frames, frames), 0)
    col = lax.broadcasted_iota(jnp.int32, (frames, frames), 1)
    preds = {
        -2: preds_ref.at[:frames],
        -1: odd_pred.at[:frames],
        0: preds_ref.at[frames : 2 * frames],
        1: odd_pred.at[frames:],
        2: preds_ref.at[2 * frames :],
    }
    factor = (1.0 / jnp.maximum(count_ref[:, :1], 1.0)) * scale
    loss = jnp.zeros((frames, 1), F32)
    first = True
    for window in (-2, -1, 1, 2, 0):
        base = (window + 2) * frames
        for step in range(horizons):
            ahead = step + 1
            query = preds[window][:, step * width : (step + 1) * width]
            scores = rows_dot(query, codes[base : base + 5 * frames]) * scale
            block = {
                d: scores[:, (d + 2) * frames : (d + 3) * frames] for d in range(-REACH, REACH + 1)
            }
            here, after = col == row + ahead, col == row + ahead - frames
            positive = jnp.sum(
                jnp.where(here, block[0], 0.0) + jnp.where(after, block[1], 0.0),
                axis=1,
                keepdims=True,
            )
            for d in (-2, -1, 1, 2):
                usable = flags_ref[window + d + 4 : window + d + 5, :]
                block[d] = jnp.where(usable > 0, block[d], -1e30)
            top = jnp.maximum(
                jnp.maximum(block[-2], block[-1]), jnp.maximum(block[1], block[2])
            )
            top = jnp.maximum(positive, jnp.max(top, axis=1, keepdims=True))
            total = sum(jnp.exp(block[d] - top) for d in (-2, -1, 1, 2))
            total = jnp.sum(total, axis=1, keepdims=True)
            log_total = top + jnp.log(jnp.exp(positive - top) + total)
            spot = (window + 2) * horizons + step
            active = act_ref[:, spot : spot + 1]
            weight = factor * active
            pos_coef = weight * (jnp.exp(positive - log_total) - 1.0)
            pos_here = jnp.where(here, pos_coef, 0.0).astype(BF16)
            pos_after = jnp.where(after, pos_coef, 0.0).astype(BF16)
            if window != 0:
                coef = (weight * jnp.exp(block[-window] - log_total)).astype(BF16)
                term = cols_dot(coef, query)
                if window == -1:
                    term = term + cols_dot(pos_after, query)
            else:
                coefs = {
                    d: (weight * jnp.exp(block[d] - log_total)).astype(BF16) for d in (-2, -1, 1, 2)
                }
                coefs[0] = pos_here
                wide = jnp.concatenate([coefs[d] for d in range(-REACH, REACH + 1)], axis=1)
                delta = jnp.dot(
                    wide, codes[base : base + 5 * frames], preferred_element_type=F32
                ) + jnp.dot(
                    pos_after, codes[base + 3 * frames : base + 4 * frames],
                    preferred_element_type=F32,
                )
                delta = delta.astype(BF16)
                for part in range(parts // horizons):
                    spot = step * (parts // horizons) + part
                    out_ref[spot, :, :pred_cols] = delta[:, part * pred_cols : (part + 1) * pred_cols]
                term = cols_dot(pos_here, query)
                loss = loss + active * (log_total - positive)
            if first:
                code_acc[...] = term
                first = False
            else:
                code_acc[...] += term
    for part in range(parts):
        out_ref[part, :, pred_cols:] = code_acc[:, part * code_cols : (part + 1) * code_cols].astype(
            BF16
        )
    loss_ref[...] = jnp.broadcast_to(jnp.sum(loss, axis=0, keepdims=True), loss_ref.shape)


def term_kernel(pred_cols, core_ref, deltas, ctx_same, feat_same, ctx_cross, feat_cross, out_ref, held):
    parts, frames, _ = deltas.shape
    plane = out_ref.shape[0]
    core, place = core_ref[0, 0], core_ref[0, 1]
    for spot in range(parts // 2):
        rows = slice(spot * frames, (spot + 1) * frames)
        onward = (place + spot) % (parts // 2)
        held[0, rows, :pred_cols] = deltas[2 * spot + core, :, :pred_cols]
        held[1, rows, :pred_cols] = deltas[2 * spot + 1 - core, :, :pred_cols]
        held[0, rows, pred_cols:] = deltas[2 * onward + core, :, pred_cols:]
        held[1, rows, pred_cols:] = deltas[2 * onward + 1 - core, :, pred_cols:]
    rows = 2 * ctx_same.shape[1] * 2 // parts
    for half in range(parts // 4):
        blocks = slice(half * rows, (half + 1) * rows)
        for same, cross, lanes in (
            (ctx_same, ctx_cross, slice(0, pred_cols)),
            (feat_same, feat_cross, slice(pred_cols, deltas.shape[2])),
        ):
            term = cols_dot(same[:, blocks], held[0, :, lanes])
            term = term + cols_dot(cross[:, blocks], held[1, :, lanes])
            term = term.reshape(2, plane, rows // plane // 2, -1)
            term = jnp.concatenate([term[0], term[1]], axis=1).astype(BF16)
            span = rows // plane
            out_ref[:, half * span : (half + 1) * span, lanes] = term


def per_device(features, context, predictor, projection, lengths, frame_mask):
    frames, width = features.shape[1], features.shape[2]
    horizons = predictor.shape[1]
    feat, ctx = features[0], context[0]
    windows, recordings = size_of(TM), size_of(DP)
    devices = windows * recordings
    parts, plane = size_of(RING), size_of(PLANE)
    tm = lax.axis_index(TM)
    core = lax.axis_index("core")

    encoded = jnp.dot(feat, projection, preferred_element_type=F32).astype(BF16)
    both = jnp.concatenate([encoded, ctx], axis=0)
    low2, high2 = window_at(both, -2), window_at(both, 2)
    positions = jnp.arange(frames, dtype=jnp.int32)
    usable = ((frame_mask[0] == 1) & (positions < lengths[0, 0])).astype(F32)
    flags = lax.all_to_all(
        jnp.broadcast_to(usable[None], (devices, frames)), ALL, 0, 0, tiled=True
    )
    flags, outer = lax.optimization_barrier((flags, encoded))
    low4, high4 = window_at(outer, -4), window_at(outer, 4)
    both_x, low2_x, high2_x = other_core(both), other_core(low2), other_core(high2)
    side_x = other_core(jnp.where(core == 0, high4, low4))
    ctx_ring = lax.all_gather(ctx, "y")
    feat_ring = [feat] + [ring_shift(feat, ("y",), step) for step in range(1, lax.axis_size("y"))]

    smem = pl.BlockSpec(memory_space=pltpu.SMEM)
    vmem = pl.BlockSpec(memory_space=pltpu.VMEM)
    anywhere = pl.BlockSpec(memory_space=pl.ANY)
    limit = pltpu.CompilerParams(vmem_limit_bytes=16 * 2**20)

    spot = jnp.stack([lax.axis_index(ALL), tm]).reshape(1, 2).astype(jnp.int32)
    count, near, act = pl.pallas_call(
        functools.partial(flags_kernel, horizons, windows),
        out_shape=(
            jax.ShapeDtypeStruct((1, 128), F32),
            jax.ShapeDtypeStruct((16, frames), F32),
            jax.ShapeDtypeStruct((frames, 16), F32),
        ),
        in_specs=[smem, vmem],
        out_specs=(vmem, vmem, vmem),
    )(spot, flags)

    weights = predictor.reshape(width, horizons * width)
    preds = pl.pallas_call(
        pred_kernel,
        out_shape=jax.ShapeDtypeStruct((3 * frames, horizons * width), BF16),
        in_specs=[anywhere, anywhere, anywhere, vmem],
        out_specs=vmem,
        scratch_shapes=[pltpu.VMEM((3 * frames, width), BF16), pltpu.SemaphoreType.DMA((3,))],
        compiler_params=limit,
        cost_estimate=pl.CostEstimate(flops=1600000000, bytes_accessed=6500000, transcendentals=0),
    )(low2, ctx, high2, weights)
    pred_cols, code_cols = horizons * width // parts, width // parts
    lanes = pred_cols + code_cols
    core_word = jnp.stack([core, lax.axis_index("y")]).reshape(1, 2).astype(jnp.int32)
    deltas, loss_part = pl.pallas_call(
        functools.partial(delta_kernel, horizons),
        out_shape=(
            jax.ShapeDtypeStruct((parts, frames, lanes), BF16),
            jax.ShapeDtypeStruct((1, 128), F32),
        ),
        in_specs=[smem] + [vmem] * 5 + [anywhere] * 9,
        out_specs=(vmem, vmem),
        scratch_shapes=[
            pltpu.VMEM((9 * frames, width), BF16),
            pltpu.VMEM((frames, width), F32),
            pltpu.VMEM((4 * frames, width), BF16),
            pltpu.VMEM((2 * frames, horizons * width), BF16),
            pltpu.SemaphoreType.DMA((12,)),
        ],
        compiler_params=pltpu.CompilerParams(vmem_limit_bytes=20 * 2**20),
        cost_estimate=pl.CostEstimate(
            flops=4000000000, bytes_accessed=12000000, transcendentals=900000
        ),
    )(
        core_word, count, near, act, preds, weights,
        both, low2, high2, low4, high4, both_x, low2_x, high2_x, side_x,
    )

    feat_ring = jnp.concatenate(feat_ring, axis=0)
    deltas, ctx_ring, feat_ring = lax.optimization_barrier((deltas, ctx_ring, feat_ring))
    loss_part = gathered_terms(loss_part, "z")
    deltas = lax.all_to_all(deltas, RING, 0, 0, tiled=True)
    deltas, loss_part = lax.optimization_barrier((deltas, loss_part))
    loss_part = jnp.sum(loss_part.astype(F32), axis=(0, 1)).reshape(1, -1)
    loss_part = gathered_terms(loss_part, ("xh", "xl"))
    ring_rows = [block.reshape(-1, width) for block in (ctx_ring, feat_ring)]
    ring_rows = ring_rows + [other_core(block) for block in ring_rows]
    terms = pl.pallas_call(
        functools.partial(term_kernel, pred_cols),
        out_shape=jax.ShapeDtypeStruct((plane, width // plane, lanes), BF16),
        in_specs=[smem] + [vmem] * 5,
        out_specs=vmem,
        scratch_shapes=[pltpu.VMEM((2, parts // 2 * frames, lanes), BF16)],
        compiler_params=limit,
        cost_estimate=pl.CostEstimate(flops=800000000, bytes_accessed=6000000, transcendentals=0),
    )(core_word, deltas, *ring_rows)

    owned = width // devices
    terms = lax.all_to_all(terms, PLANE, 0, 0, tiled=True)
    terms, loss_part = lax.optimization_barrier((terms, loss_part))
    loss_part = jnp.sum(loss_part[:, :, 0].astype(F32))
    terms = jnp.sum(terms.astype(F32), axis=0).reshape(parts, owned, lanes)
    tail = jnp.broadcast_to(loss_part, (parts, owned, lanes))
    got = lax.all_to_all(jnp.concatenate([terms, tail], axis=1), RING, 0, 0, tiled=True)
    loss = jnp.sum(got[:, owned, 0]) * (1.0 / jnp.maximum(count[0, 0], 1.0))
    got = got[:, :owned].transpose(1, 0, 2)
    grad_pred = got[:, :, :pred_cols].reshape(owned, horizons, width)
    grad_proj = got[:, :, pred_cols:].reshape(owned, width)
    return (loss, grad_pred, grad_proj)


def solution(mesh):
    fine = Mesh(mesh.devices.reshape(4, 2, 8, 2, 2), ALL)
    placed = (P(DP, TM, None), P(DP, TM, None), P(), P(), P(DP, TM), P(DP, TM))
    return jax.shard_map(
        per_device,
        mesh=fine,
        in_specs=placed,
        out_specs=(P(), P(ALL, None, None), P(ALL, None)),
        check_vma=False,
    )
```

```python
import functools

import jax
import jax.numpy as jnp
from jax import lax
from jax.experimental import pallas as pl
from jax.experimental.pallas import tpu as pltpu
from jax.sharding import Mesh, PartitionSpec as P

DP = ("y", "xh")
TM = ("z", "xl", "core")
ALL = DP + TM
PLANE = ("xh", "z", "xl")
RING = ("y", "core")
F32 = jnp.float32
BF16 = jnp.bfloat16
REACH = 2


def size_of(names):
    size = 1
    for name in names:
        size *= lax.axis_size(name)
    return size


def ring_shift(block, axes, offset):
    size = size_of(axes)
    return lax.ppermute(block, axes, [((i + offset) % size, i) for i in range(size)])


def window_at(block, offset):
    return ring_shift(block, TM, offset)


def other_core(block):
    return lax.ppermute(block, "core", [(0, 1), (1, 0)])


def gathered_terms(value, axes):
    high = to_bf16_grid(value)
    middle = to_bf16_grid(value - high)
    terms = jnp.concatenate([high, middle, value - high - middle], axis=0).astype(BF16)
    return lax.all_gather(terms, axes)


def to_bf16_grid(value):
    return lax.reduce_precision(value, 8, 7)


def rows_dot(a, b):
    return lax.dot_general(a, b, (((1,), (1,)), ((), ())), preferred_element_type=F32)


def cols_dot(a, b):
    return lax.dot_general(a, b, (((0,), (0,)), ((), ())), preferred_element_type=F32)


def flags_kernel(horizons, windows, spot_ref, flags_ref, count_ref, near_ref, act_ref):
    devices, frames = flags_ref.shape
    device, tm = spot_ref[0, 0], spot_ref[0, 1]
    flags = flags_ref[...]
    row = lax.broadcasted_iota(jnp.int32, flags.shape, 0)
    lane = lax.broadcasted_iota(jnp.int32, flags.shape, 1)
    following = jnp.where(row % windows == windows - 1, 0.0, pltpu.roll(flags, devices - 1, 0))
    slot = lax.broadcasted_iota(jnp.int32, (devices, 16), 1)
    source = lax.broadcasted_iota(jnp.int32, (devices, 16), 0)
    window = slot - REACH
    pick = (source == device + window) & (tm + window >= 0) & (tm + window < windows)
    pick = jnp.where(pick, 1.0, 0.0).astype(BF16)
    total = jnp.zeros((1, frames), F32)
    for h in range(1, horizons + 1):
        ahead = jnp.where(
            lane < frames - h,
            pltpu.roll(flags, frames - h, 1),
            pltpu.roll(following, frames - h, 1),
        )
        pairs = flags * ahead
        total = total + jnp.sum(pairs, axis=0, keepdims=True)
        act_ref[(h - 1) * frames : h * frames] = cols_dot(pairs.astype(BF16), pick)
    count_ref[...] = jnp.broadcast_to(jnp.sum(total, axis=1, keepdims=True), count_ref.shape)
    window = slot - 2 * REACH
    pick = (source == device + window) & (tm + window >= 0) & (tm + window < windows)
    near_ref[...] = cols_dot(jnp.where(pick, 1.0, 0.0).astype(BF16), flags.astype(BF16))


def stacked_dot(rows, weights, out_ref):
    windows, stacked, width = out_ref.shape
    tile = 512
    frames = stacked * width // weights.shape[1]
    for at in range(0, weights.shape[1], tile):
        part = jnp.dot(rows, weights[:, at : at + tile], preferred_element_type=F32).astype(BF16)
        step, lane = divmod(at, width)
        for w in range(windows):
            out_ref[w, step * frames : (step + 1) * frames, lane : lane + tile] = part[
                w * frames : (w + 1) * frames
            ]


def pred_kernel(low2, ctx, high2, weights, out_ref, rows, sems):
    frames = ctx.shape[0]
    copies = [
        pltpu.make_async_copy(block, rows.at[pl.ds(slot * frames, frames)], sems.at[slot])
        for slot, block in enumerate(
            (low2.at[pl.ds(frames, frames)], ctx, high2.at[pl.ds(frames, frames)])
        )
    ]
    for copy in copies:
        copy.start()
    for copy in copies:
        copy.wait()
    stacked_dot(rows[...], weights, out_ref)


def delta_kernel(
    horizons, core_ref, count_ref, flags_ref, act_ref, preds_ref, weights,
    both, low2, high2, low4, high4, both_x, low2_x, high2_x, side_x,
    out_0, out_1, out_2, out_3, loss_ref, codes, code_acc, odd_ctx, odd_pred, blocks, sems,
):
    frames, width = low4.shape
    scale = width ** (-0.5)
    ring, cores = blocks.shape[:2]
    parts = ring * cores
    pred_cols, code_cols = horizons * width // parts, width // parts
    core, place = core_ref[0, 0], core_ref[0, 1]

    def put(sem, block, start, held, slot):
        at = slot * frames
        if not isinstance(slot, int):
            at = pl.multiple_of(at, frames)
        return pltpu.make_async_copy(
            block.at[pl.ds(start, frames)], held.at[pl.ds(at, frames)], sems.at[sem]
        )

    ctx_copies = [
        put(0, low2_x, frames, odd_ctx, 1 - core),
        put(1, both_x, frames, odd_ctx, 2 - core),
        put(2, high2_x, frames, odd_ctx, 3 - core),
    ]
    code_copies = [
        put(3, low4, 0, codes, 0),
        put(4, low2, 0, codes, 2),
        put(5, both, 0, codes, 4),
        put(6, high2, 0, codes, 6),
        put(7, high4, 0, codes, 8),
        put(8, low2_x, 0, codes, 3 - 2 * core),
        put(9, both_x, 0, codes, 5 - 2 * core),
        put(10, high2_x, 0, codes, 7 - 2 * core),
        put(11, side_x, 0, codes, 1 + 6 * core),
    ]
    for copy in ctx_copies + code_copies:
        copy.start()
    for copy in ctx_copies:
        copy.wait()
    stacked_dot(odd_ctx[frames : 3 * frames], weights, odd_pred)
    for copy in code_copies:
        copy.wait()
    shape = (horizons * frames, frames)
    row = lax.broadcasted_iota(jnp.int32, shape, 0)
    ahead = row % frames + row // frames + 1
    col = lax.broadcasted_iota(jnp.int32, shape, 1)
    here, after = col == ahead, col == ahead - frames
    preds = {-2: preds_ref[0], -1: odd_pred[0], 0: preds_ref[1], 1: odd_pred[1], 2: preds_ref[2]}
    factor = (1.0 / jnp.maximum(count_ref[:, :1], 1.0)) * scale
    beside = (-2, -1, 1, 2)
    for window in (-2, -1, 1, 2, 0):
        base = (window + 2) * frames
        query = preds[window]
        scores = rows_dot(query, codes[base : base + 5 * frames]) * scale
        block = {
            d: scores[:, (d + 2) * frames : (d + 3) * frames] for d in range(-REACH, REACH + 1)
        }
        positive = jnp.sum(
            jnp.where(here, block[0], 0.0) + jnp.where(after, block[1], 0.0),
            axis=1,
            keepdims=True,
        )
        for d in beside:
            usable = flags_ref[window + d + 4 : window + d + 5, :]
            block[d] = jnp.where(usable > 0, block[d], -1e30)
        top = jnp.maximum(jnp.maximum(block[-2], block[-1]), jnp.maximum(block[1], block[2]))
        top = jnp.maximum(positive, jnp.max(top, axis=1, keepdims=True))
        total = sum(jnp.exp(block[d] - top) for d in beside)
        total = jnp.sum(total, axis=1, keepdims=True)
        log_total = top + jnp.log(jnp.exp(positive - top) + total)
        active = act_ref[:, window + 2 : window + 3]
        weight = factor * active
        pos_coef = weight * (jnp.exp(positive - log_total) - 1.0)
        pos_after = jnp.where(after, pos_coef, 0.0).astype(BF16)
        if window != 0:
            coef = (weight * jnp.exp(block[-window] - log_total)).astype(BF16)
            term = cols_dot(coef, query)
            if window == -1:
                term = term + cols_dot(pos_after, query)
            if window == -2:
                code_acc[...] = term
            else:
                code_acc[...] += term
        else:
            coefs = {d: (weight * jnp.exp(block[d] - log_total)).astype(BF16) for d in beside}
            coefs[0] = jnp.where(here, pos_coef, 0.0).astype(BF16)
            wide = jnp.concatenate([coefs[d] for d in range(-REACH, REACH + 1)], axis=1)
            delta = jnp.dot(
                wide, codes[base : base + 5 * frames], preferred_element_type=F32
            ) + jnp.dot(
                pos_after, codes[base + 3 * frames : base + 4 * frames], preferred_element_type=F32
            )
            delta = delta.astype(BF16)
            for part in range(parts):
                step, at = divmod(part * pred_cols, width)
                blocks[part // cores, part % cores, :, :pred_cols] = delta[
                    step * frames : (step + 1) * frames, at : at + pred_cols
                ]
            code_delta = (code_acc[...] + cols_dot(coefs[0], query)).astype(BF16)
            for part in range(parts):
                blocks[part // cores, part % cores, :, pred_cols:] = code_delta[
                    :, part * code_cols : (part + 1) * code_cols
                ]
            loss = jnp.sum(active * (log_total - positive), axis=0, keepdims=True)
            loss_ref[...] = jnp.broadcast_to(loss, loss_ref.shape)
    for back, out in enumerate((out_0, out_1, out_2, out_3)):
        out[...] = blocks[(place + ring - back) % ring]


def term_kernel(
    pred_cols, core_ref, same_0, same_1, same_2, same_3, cross_0, cross_1, cross_2, cross_3,
    ctx_same, feat_same, ctx_cross, feat_cross, out_ref, held,
):
    cores, frames, lanes_all = same_0.shape
    plane = out_ref.shape[0]
    core, place = core_ref[0, 0], core_ref[0, 1]
    both = ((same_0, same_1, same_2, same_3), (cross_0, cross_1, cross_2, cross_3))
    parts = cores * len(both[0])
    for side, blocks in enumerate(both):
        for spot, block in enumerate(blocks):
            start = pl.multiple_of((place + spot) % len(blocks) * frames, frames)
            held[side, pl.ds(start, frames)] = block[core]
    rows = 2 * ctx_same.shape[1] * 2 // parts
    for half in range(parts // 4):
        blocks = slice(half * rows, (half + 1) * rows)
        for same, cross, lanes in (
            (ctx_same, ctx_cross, slice(0, pred_cols)),
            (feat_same, feat_cross, slice(pred_cols, lanes_all)),
        ):
            term = cols_dot(same[:, blocks], held[0, :, lanes])
            term = term + cols_dot(cross[:, blocks], held[1, :, lanes])
            term = term.reshape(2, plane, rows // plane // 2, -1)
            term = jnp.concatenate([term[0], term[1]], axis=1).astype(BF16)
            span = rows // plane
            out_ref[:, half * span : (half + 1) * span, lanes] = term


def per_device(features, context, predictor, projection, lengths, frame_mask):
    frames, width = features.shape[1], features.shape[2]
    horizons = predictor.shape[1]
    feat, ctx = features[0], context[0]
    windows, recordings = size_of(TM), size_of(DP)
    devices = windows * recordings
    parts, plane = size_of(RING), size_of(PLANE)
    tm = lax.axis_index(TM)
    core = lax.axis_index("core")

    encoded = jnp.dot(feat, projection, preferred_element_type=F32).astype(BF16)
    both = jnp.concatenate([encoded, ctx], axis=0)
    low2, high2 = window_at(both, -2), window_at(both, 2)
    both_x = other_core(both)
    positions = jnp.arange(frames, dtype=jnp.int32)
    usable = ((frame_mask[0] == 1) & (positions < lengths[0, 0])).astype(F32)
    usable, both_x = lax.optimization_barrier((usable, both_x))
    flags = lax.all_to_all(
        jnp.broadcast_to(usable[None], (devices, frames)), ALL, 0, 0, tiled=True
    )
    low4, high4 = window_at(encoded, -4), window_at(encoded, 4)
    weights = predictor.reshape(width, horizons * width)
    low2, high2, weights, flags = lax.optimization_barrier((low2, high2, weights, flags))
    low2_x, high2_x = other_core(low2), other_core(high2)
    side_x = other_core(jnp.where(core == 0, high4, low4))
    ctx_ring = lax.all_gather(ctx, "y")
    feat_ring = lax.all_gather(feat, "y")

    smem = pl.BlockSpec(memory_space=pltpu.SMEM)
    vmem = pl.BlockSpec(memory_space=pltpu.VMEM)
    anywhere = pl.BlockSpec(memory_space=pl.ANY)
    limit = pltpu.CompilerParams(vmem_limit_bytes=16 * 2**20)

    spot = jnp.stack([lax.axis_index(ALL), tm]).reshape(1, 2).astype(jnp.int32)
    count, near, act = pl.pallas_call(
        functools.partial(flags_kernel, horizons, windows),
        out_shape=(
            jax.ShapeDtypeStruct((1, 128), F32),
            jax.ShapeDtypeStruct((16, frames), F32),
            jax.ShapeDtypeStruct((horizons * frames, 16), F32),
        ),
        in_specs=[smem, vmem],
        out_specs=(vmem, vmem, vmem),
    )(spot, flags)

    preds = pl.pallas_call(
        pred_kernel,
        out_shape=jax.ShapeDtypeStruct((3, horizons * frames, width), BF16),
        in_specs=[anywhere, anywhere, anywhere, vmem],
        out_specs=vmem,
        scratch_shapes=[pltpu.VMEM((3 * frames, width), BF16), pltpu.SemaphoreType.DMA((3,))],
        compiler_params=limit,
        cost_estimate=pl.CostEstimate(flops=1600000000, bytes_accessed=6500000, transcendentals=0),
    )(low2, ctx, high2, weights)
    pred_cols, code_cols = horizons * width // parts, width // parts
    lanes = pred_cols + code_cols
    core_word = jnp.stack([core, lax.axis_index("y")]).reshape(1, 2).astype(jnp.int32)
    ring = lax.axis_size("y")
    *deltas, loss_part = pl.pallas_call(
        functools.partial(delta_kernel, horizons),
        out_shape=[jax.ShapeDtypeStruct((2, frames, lanes), BF16)] * ring
        + [jax.ShapeDtypeStruct((1, 128), F32)],
        in_specs=[smem] + [vmem] * 5 + [anywhere] * 9,
        out_specs=[vmem] * (ring + 1),
        scratch_shapes=[
            pltpu.VMEM((9 * frames, width), BF16),
            pltpu.VMEM((frames, width), F32),
            pltpu.VMEM((4 * frames, width), BF16),
            pltpu.VMEM((2, horizons * frames, width), BF16),
            pltpu.VMEM((ring, 2, frames, lanes), BF16),
            pltpu.SemaphoreType.DMA((12,)),
        ],
        compiler_params=pltpu.CompilerParams(vmem_limit_bytes=20 * 2**20),
        cost_estimate=pl.CostEstimate(
            flops=4000000000, bytes_accessed=12000000, transcendentals=900000
        ),
    )(
        core_word, count, near, act, preds, weights,
        both, low2, high2, low4, high4, both_x, low2_x, high2_x, side_x,
    )

    deltas, ctx_ring = lax.optimization_barrier((deltas, ctx_ring))
    loss_part = gathered_terms(loss_part, ("xh", "xl"))
    same = [deltas[0]] + [ring_shift(deltas[step], ("y",), step) for step in range(1, ring)]
    *_, feat_ring = lax.optimization_barrier((*same[1:], feat_ring))
    cross = [other_core(block) for block in same]
    ring_rows = [block.reshape(-1, width) for block in (ctx_ring, feat_ring)]
    ring_rows = ring_rows + [other_core(block) for block in ring_rows]
    terms = pl.pallas_call(
        functools.partial(term_kernel, pred_cols),
        out_shape=jax.ShapeDtypeStruct((plane, width // plane, lanes), BF16),
        in_specs=[smem] + [vmem] * 12,
        out_specs=vmem,
        scratch_shapes=[pltpu.VMEM((2, parts // 2 * frames, lanes), BF16)],
        compiler_params=limit,
        cost_estimate=pl.CostEstimate(flops=800000000, bytes_accessed=6000000, transcendentals=0),
    )(core_word, *same, *cross, *ring_rows)

    owned = width // devices
    terms, loss_part = lax.optimization_barrier((terms, loss_part))
    loss_part = jnp.sum(loss_part.astype(F32), axis=(0, 1)).reshape(1, -1)
    loss_part = gathered_terms(loss_part, "z")
    terms = lax.all_to_all(terms, PLANE, 0, 0, tiled=True)
    terms, loss_part = lax.optimization_barrier((terms, loss_part))
    loss_part = jnp.sum(loss_part[:, :, 0].astype(F32))
    terms = jnp.sum(terms.astype(F32), axis=0).reshape(parts, owned, lanes)
    tail = jnp.broadcast_to(loss_part, (parts, owned, lanes))
    got = lax.all_to_all(jnp.concatenate([terms, tail], axis=1), RING, 0, 0, tiled=True)
    loss = jnp.sum(got[:, owned, 0]) * (1.0 / jnp.maximum(count[0, 0], 1.0))
    got = got[:, :owned].transpose(1, 0, 2)
    grad_pred = got[:, :, :pred_cols].reshape(owned, horizons, width)
    grad_proj = got[:, :, pred_cols:].reshape(owned, width)
    return (loss, grad_pred, grad_proj)


def solution(mesh):
    fine = Mesh(mesh.devices.reshape(4, 2, 8, 2, 2), ALL)
    placed = (P(DP, TM, None), P(DP, TM, None), P(), P(), P(DP, TM), P(DP, TM))
    return jax.shard_map(
        per_device,
        mesh=fine,
        in_specs=placed,
        out_specs=(P(), P(ALL, None, None), P(ALL, None)),
        check_vma=False,
    )
```

```python
import functools

import jax
import jax.numpy as jnp
from jax import lax
from jax.experimental import pallas as pl
from jax.experimental.pallas import tpu as pltpu
from jax.sharding import Mesh, PartitionSpec as P

DP = ("y", "xh")
TM = ("z", "xl", "core")
ALL = DP + TM
PLANE = ("xh", "z", "xl")
RING = ("y", "core")
CHIPS = ("y", "xh", "z", "xl")
F32 = jnp.float32
BF16 = jnp.bfloat16
REACH = 2


def size_of(names):
    size = 1
    for name in names:
        size *= lax.axis_size(name)
    return size


def ring_shift(block, axes, offset):
    size = size_of(axes)
    return lax.ppermute(block, axes, [((i + offset) % size, i) for i in range(size)])


def window_at(block, offset):
    return ring_shift(block, TM, offset)


def other_core(block):
    return lax.ppermute(block, "core", [(0, 1), (1, 0)])


def rows_dot(a, b):
    return lax.dot_general(a, b, (((1,), (1,)), ((), ())), preferred_element_type=F32)


def cols_dot(a, b):
    return lax.dot_general(a, b, (((0,), (0,)), ((), ())), preferred_element_type=F32)


def flags_kernel(horizons, windows, spot_ref, flags_ref, count_ref, near_ref, act_ref):
    chips, span = flags_ref.shape
    frames = span // 2
    device, tm = spot_ref[0, 0], spot_ref[0, 1]
    flags = flags_ref[...]
    row = lax.broadcasted_iota(jnp.int32, flags.shape, 0)
    lane = lax.broadcasted_iota(jnp.int32, flags.shape, 1)
    last = row % (windows // 2) == windows // 2 - 1
    following = jnp.where(last, 0.0, pltpu.roll(flags, chips - 1, 0))
    slot = lax.broadcasted_iota(jnp.int32, (chips, 16), 1)
    source = lax.broadcasted_iota(jnp.int32, (chips, 16), 0)

    def picked(values, reach, transposed):
        window = slot - reach
        inside = (tm + window >= 0) & (tm + window < windows)
        out = 0.0
        for half in range(2):
            pick = (2 * source + half == device + window) & inside
            pick = jnp.where(pick, 1.0, 0.0).astype(BF16)
            part = values[:, half * frames : (half + 1) * frames].astype(BF16)
            out = out + (cols_dot(part, pick) if transposed else cols_dot(pick, part))
        return out

    total = jnp.zeros((1, span), F32)
    for h in range(1, horizons + 1):
        ahead = jnp.where(
            lane < span - h, pltpu.roll(flags, span - h, 1), pltpu.roll(following, span - h, 1)
        )
        pairs = flags * ahead
        total = total + jnp.sum(pairs, axis=0, keepdims=True)
        act_ref[(h - 1) * frames : h * frames] = picked(pairs, REACH, True)
    count_ref[...] = jnp.broadcast_to(jnp.sum(total, axis=1, keepdims=True), count_ref.shape)
    near_ref[...] = picked(flags, 2 * REACH, False)


def stacked_dot(rows, weights, out_ref, ready=None):
    windows, stacked, width = out_ref.shape
    tile = 512
    frames = stacked * width // weights.shape[1]
    for at in range(0, weights.shape[1], tile):
        if ready is not None:
            ready[at // tile].wait()
        part = jnp.dot(rows, weights[:, at : at + tile], preferred_element_type=F32).astype(BF16)
        step, lane = divmod(at, width)
        for w in range(windows):
            out_ref[w, step * frames : (step + 1) * frames, lane : lane + tile] = part[
                w * frames : (w + 1) * frames
            ]


def pred_kernel(low2, ctx, high2, weights, out_ref, rows, held, sems):
    frames = ctx.shape[0]
    copies = [
        pltpu.make_async_copy(block, rows.at[pl.ds(slot * frames, frames)], sems.at[slot])
        for slot, block in enumerate(
            (low2.at[pl.ds(frames, frames)], ctx, high2.at[pl.ds(frames, frames)])
        )
    ]
    tile = 512
    ready = [
        pltpu.make_async_copy(
            weights.at[:, pl.ds(at, tile)], held.at[:, pl.ds(at, tile)], sems.at[3 + at // tile]
        )
        for at in range(0, weights.shape[1], tile)
    ]
    for copy in copies + ready:
        copy.start()
    for copy in copies:
        copy.wait()
    stacked_dot(rows[...], held, out_ref, ready)


def delta_kernel(
    horizons, core_ref, count_ref, flags_ref, act_ref, preds_ref, weights,
    both, low2, high2, low4, high4, both_x, low2_x, high2_x, low4_x, high4_x,
    out_0, out_1, out_2, out_3, loss_ref, codes, code_acc, odd_ctx, odd_pred, blocks, sems,
):
    frames, width = low4.shape
    scale = width ** (-0.5)
    ring, cores = blocks.shape[:2]
    parts = ring * cores
    pred_cols, code_cols = horizons * width // parts, width // parts
    core, place = core_ref[0, 0], core_ref[0, 1]

    def put(sem, block, start, held, slot):
        at = slot * frames
        if not isinstance(slot, int):
            at = pl.multiple_of(at, frames)
        return pltpu.make_async_copy(
            block.at[pl.ds(start, frames)], held.at[pl.ds(at, frames)], sems.at[sem]
        )

    ctx_copies = [
        put(0, low2_x, frames, odd_ctx, 1 - core),
        put(1, both_x, frames, odd_ctx, 2 - core),
        put(2, high2_x, frames, odd_ctx, 3 - core),
    ]
    code_copies = [
        put(3, low4, 0, codes, 1),
        put(4, low2, 0, codes, 3),
        put(5, both, 0, codes, 5),
        put(6, high2, 0, codes, 7),
        put(7, high4, 0, codes, 9),
        put(8, low4_x, 0, codes, 2 - 2 * core),
        put(9, low2_x, 0, codes, 4 - 2 * core),
        put(10, both_x, 0, codes, 6 - 2 * core),
        put(11, high2_x, 0, codes, 8 - 2 * core),
        put(12, high4_x, 0, codes, 10 - 2 * core),
    ]
    for copy in ctx_copies + code_copies:
        copy.start()
    for copy in ctx_copies:
        copy.wait()
    stacked_dot(odd_ctx[frames : 3 * frames], weights, odd_pred)
    for copy in code_copies:
        copy.wait()
    shape = (horizons * frames, frames)
    row = lax.broadcasted_iota(jnp.int32, shape, 0)
    ahead = row % frames + row // frames + 1
    col = lax.broadcasted_iota(jnp.int32, shape, 1)
    here, after = col == ahead, col == ahead - frames
    preds = {-2: preds_ref[0], -1: odd_pred[0], 0: preds_ref[1], 1: odd_pred[1], 2: preds_ref[2]}
    factor = (1.0 / jnp.maximum(count_ref[:, :1], 1.0)) * scale
    beside = (-2, -1, 1, 2)
    for window in (-2, -1, 1, 2, 0):
        base = (window + 3) * frames
        query = preds[window]
        scores = rows_dot(query, codes[base : base + 5 * frames]) * scale
        block = {
            d: scores[:, (d + 2) * frames : (d + 3) * frames] for d in range(-REACH, REACH + 1)
        }
        positive = jnp.sum(
            jnp.where(here, block[0], 0.0) + jnp.where(after, block[1], 0.0),
            axis=1,
            keepdims=True,
        )
        for d in beside:
            usable = flags_ref[window + d + 4 : window + d + 5, :]
            block[d] = jnp.where(usable > 0, block[d], -1e30)
        top = jnp.maximum(jnp.maximum(block[-2], block[-1]), jnp.maximum(block[1], block[2]))
        top = jnp.maximum(positive, jnp.max(top, axis=1, keepdims=True))
        total = sum(jnp.exp(block[d] - top) for d in beside)
        total = jnp.sum(total, axis=1, keepdims=True)
        log_total = top + jnp.log(jnp.exp(positive - top) + total)
        active = act_ref[:, window + 2 : window + 3]
        weight = factor * active
        pos_coef = weight * (jnp.exp(positive - log_total) - 1.0)
        pos_after = jnp.where(after, pos_coef, 0.0).astype(BF16)
        if window != 0:
            coef = (weight * jnp.exp(block[-window] - log_total)).astype(BF16)
            term = cols_dot(coef, query)
            if window == -1:
                term = term + cols_dot(pos_after, query)
            if window == -2:
                code_acc[...] = term
            else:
                code_acc[...] += term
        else:
            coefs = {d: (weight * jnp.exp(block[d] - log_total)).astype(BF16) for d in beside}
            coefs[0] = jnp.where(here, pos_coef, 0.0).astype(BF16)
            wide = jnp.concatenate([coefs[d] for d in range(-REACH, REACH + 1)], axis=1)
            delta = jnp.dot(
                wide, codes[base : base + 5 * frames], preferred_element_type=F32
            ) + jnp.dot(
                pos_after, codes[base + 3 * frames : base + 4 * frames], preferred_element_type=F32
            )
            delta = delta.astype(BF16)
            for part in range(parts):
                step, at = divmod(part * pred_cols, width)
                blocks[part // cores, part % cores, :, :pred_cols] = delta[
                    step * frames : (step + 1) * frames, at : at + pred_cols
                ]
            code_delta = (code_acc[...] + cols_dot(coefs[0], query)).astype(BF16)
            for part in range(parts):
                blocks[part // cores, part % cores, :, pred_cols:] = code_delta[
                    :, part * code_cols : (part + 1) * code_cols
                ]
            loss = jnp.sum(active * (log_total - positive), axis=0, keepdims=True)
            loss_ref[...] = jnp.broadcast_to(loss, loss_ref.shape)
    for back, out in enumerate((out_0, out_1, out_2, out_3)):
        out[...] = blocks[(place + ring - back) % ring]


def term_kernel(
    pred_cols, core_ref, same_0, same_1, same_2, same_3, cross_0, cross_1, cross_2, cross_3,
    ctx_same, feat_same, ctx_cross, feat_cross, out_ref, held, rows_held, sems,
):
    copies = [
        pltpu.make_async_copy(block, rows_held.at[spot], sems.at[spot])
        for spot, block in enumerate((ctx_same, ctx_cross, feat_same, feat_cross))
    ]
    for copy in copies:
        copy.start()
    cores, frames, lanes_all = same_0.shape
    plane = out_ref.shape[0]
    core, place = core_ref[0, 0], core_ref[0, 1]
    both = ((same_0, same_1, same_2, same_3), (cross_0, cross_1, cross_2, cross_3))
    parts = cores * len(both[0])
    for side, blocks in enumerate(both):
        for spot, block in enumerate(blocks):
            start = pl.multiple_of((place + spot) % len(blocks) * frames, frames)
            held[side, pl.ds(start, frames)] = block[core]
    rows = 2 * ctx_same.shape[1] * 2 // parts
    span = rows // plane
    for first, lanes in ((0, slice(0, pred_cols)), (2, slice(pred_cols, lanes_all))):
        copies[first].wait()
        copies[first + 1].wait()
        for half in range(parts // 4):
            blocks = slice(half * rows, (half + 1) * rows)
            term = cols_dot(rows_held[first, :, blocks], held[0, :, lanes])
            term = term + cols_dot(rows_held[first + 1, :, blocks], held[1, :, lanes])
            term = term.reshape(2, plane, span // 2, -1)
            term = jnp.concatenate([term[0], term[1]], axis=1).astype(BF16)
            out_ref[:, half * span : (half + 1) * span, lanes] = term


def sum_kernel(terms_ref, loss_ref, out_ref):
    total = terms_ref[0].astype(F32)
    for source in range(1, terms_ref.shape[0]):
        total = total + terms_ref[source].astype(F32)
    owned = out_ref.shape[1] // 2
    loss = jnp.sum(loss_ref[:, :1], axis=0, keepdims=True)
    for part in range(out_ref.shape[0]):
        out_ref[part, :owned] = total[part * owned : (part + 1) * owned]
        out_ref[part, owned:] = jnp.broadcast_to(loss, (owned, out_ref.shape[2]))


def per_device(features, context, predictor, projection, lengths, frame_mask):
    frames, width = features.shape[1], features.shape[2]
    horizons = predictor.shape[1]
    feat, ctx = features[0], context[0]
    windows, recordings = size_of(TM), size_of(DP)
    devices = windows * recordings
    parts, plane = size_of(RING), size_of(PLANE)
    tm = lax.axis_index(TM)
    core = lax.axis_index("core")

    encoded = jnp.dot(feat, projection, preferred_element_type=F32).astype(BF16)
    both = jnp.concatenate([encoded, ctx], axis=0)
    low2, high2 = window_at(both, -2), window_at(both, 2)
    both_x = other_core(both)
    positions = lax.broadcasted_iota(jnp.int32, (1, frames), 1)
    usable = ((frame_mask == 1) & (positions < lengths)).astype(F32)
    usable_x = other_core(usable)
    pair = jnp.concatenate(
        [jnp.where(core == 0, usable, usable_x), jnp.where(core == 0, usable_x, usable)], axis=1
    )
    pair, both_x = lax.optimization_barrier((pair, both_x))
    chips = size_of(CHIPS)
    flags = lax.all_to_all(
        jnp.broadcast_to(pair, (chips, 2 * frames)), CHIPS, 0, 0, tiled=True
    )
    low4, high4 = window_at(encoded, -4), window_at(encoded, 4)
    weights = predictor.reshape(width, horizons * width)
    low2, high2, weights, flags = lax.optimization_barrier((low2, high2, weights, flags))
    low2_x, high2_x = other_core(low2), other_core(high2)
    low4_x, high4_x = other_core(low4), other_core(high4)
    ctx_ring = lax.all_gather(ctx, "y")
    feat_ring = lax.all_gather(feat, "y")

    smem = pl.BlockSpec(memory_space=pltpu.SMEM)
    vmem = pl.BlockSpec(memory_space=pltpu.VMEM)
    anywhere = pl.BlockSpec(memory_space=pl.ANY)
    limit = pltpu.CompilerParams(vmem_limit_bytes=16 * 2**20)

    spot = jnp.stack([lax.axis_index(ALL), tm]).reshape(1, 2).astype(jnp.int32)
    count, near, act = pl.pallas_call(
        functools.partial(flags_kernel, horizons, windows),
        out_shape=(
            jax.ShapeDtypeStruct((1, 128), F32),
            jax.ShapeDtypeStruct((16, frames), F32),
            jax.ShapeDtypeStruct((horizons * frames, 16), F32),
        ),
        in_specs=[smem, vmem],
        out_specs=(vmem, vmem, vmem),
    )(spot, flags)

    preds = pl.pallas_call(
        pred_kernel,
        out_shape=jax.ShapeDtypeStruct((3, horizons * frames, width), BF16),
        in_specs=[anywhere] * 4,
        out_specs=vmem,
        scratch_shapes=[
            pltpu.VMEM((3 * frames, width), BF16),
            pltpu.VMEM((width, horizons * width), BF16),
            pltpu.SemaphoreType.DMA((3 + horizons * width // 512,)),
        ],
        compiler_params=limit,
        cost_estimate=pl.CostEstimate(flops=1600000000, bytes_accessed=6500000, transcendentals=0),
    )(low2, ctx, high2, weights)
    pred_cols, code_cols = horizons * width // parts, width // parts
    lanes = pred_cols + code_cols
    core_word = jnp.stack([core, lax.axis_index("y")]).reshape(1, 2).astype(jnp.int32)
    ring = lax.axis_size("y")
    *deltas, loss_part = pl.pallas_call(
        functools.partial(delta_kernel, horizons),
        out_shape=[jax.ShapeDtypeStruct((2, frames, lanes), BF16)] * ring
        + [jax.ShapeDtypeStruct((1, 128), F32)],
        in_specs=[smem] + [vmem] * 5 + [anywhere] * 10,
        out_specs=[vmem] * (ring + 1),
        scratch_shapes=[
            pltpu.VMEM((11 * frames, width), BF16),
            pltpu.VMEM((frames, width), F32),
            pltpu.VMEM((4 * frames, width), BF16),
            pltpu.VMEM((2, horizons * frames, width), BF16),
            pltpu.VMEM((ring, 2, frames, lanes), BF16),
            pltpu.SemaphoreType.DMA((13,)),
        ],
        compiler_params=pltpu.CompilerParams(vmem_limit_bytes=20 * 2**20),
        cost_estimate=pl.CostEstimate(
            flops=4000000000, bytes_accessed=12000000, transcendentals=900000
        ),
    )(
        core_word, count, near, act, preds, weights,
        both, low2, high2, low4, high4, both_x, low2_x, high2_x, low4_x, high4_x,
    )

    deltas, ctx_ring = lax.optimization_barrier((deltas, ctx_ring))
    same = [deltas[0]] + [ring_shift(deltas[step], ("y",), step) for step in range(1, ring)]
    ctx_ring = ctx_ring.reshape(-1, width)
    ctx_cross = other_core(ctx_ring)
    *_, feat_ring = lax.optimization_barrier((*same[1:], feat_ring))
    feat_ring = feat_ring.reshape(-1, width)
    cross = [other_core(block) for block in same]
    ring_rows = [ctx_ring, feat_ring, ctx_cross, other_core(feat_ring)]
    terms = pl.pallas_call(
        functools.partial(term_kernel, pred_cols),
        out_shape=jax.ShapeDtypeStruct((plane, width // plane, lanes), BF16),
        in_specs=[smem] + [vmem] * 8 + [anywhere] * 4,
        out_specs=vmem,
        scratch_shapes=[
            pltpu.VMEM((2, ring * frames, lanes), BF16),
            pltpu.VMEM((4, ring * frames, width), BF16),
            pltpu.SemaphoreType.DMA((4,)),
        ],
        compiler_params=limit,
        cost_estimate=pl.CostEstimate(flops=800000000, bytes_accessed=6000000, transcendentals=0),
    )(core_word, *same, *cross, *ring_rows)

    owned = width // devices
    terms, loss_part = lax.optimization_barrier((terms, loss_part))
    terms = lax.all_to_all(terms, PLANE, 0, 0, tiled=True)
    loss_plane = lax.all_to_all(
        jnp.broadcast_to(loss_part, (plane, 128)), PLANE, 0, 0, tiled=True
    )
    sums = pl.pallas_call(
        sum_kernel,
        out_shape=jax.ShapeDtypeStruct((parts, 2 * owned, lanes), F32),
        in_specs=[vmem, vmem],
        out_specs=vmem,
    )(terms, loss_plane)
    got = lax.all_to_all(sums, RING, 0, 0, tiled=True)
    loss = jnp.sum(got[:, owned, 0]) * (1.0 / jnp.maximum(count[0, 0], 1.0))
    got = got[:, :owned].transpose(1, 0, 2)
    grad_pred = got[:, :, :pred_cols].reshape(owned, horizons, width)
    grad_proj = got[:, :, pred_cols:].reshape(owned, width)
    return (loss, grad_pred, grad_proj)


def solution(mesh):
    fine = Mesh(mesh.devices.reshape(4, 2, 8, 2, 2), ALL)
    placed = (P(DP, TM, None), P(DP, TM, None), P(), P(), P(DP, TM), P(DP, TM))
    return jax.shard_map(
        per_device,
        mesh=fine,
        in_specs=placed,
        out_specs=(P(), P(ALL, None, None), P(ALL, None)),
        check_vma=False,
    )
```

```python
import functools

import jax
import jax.numpy as jnp
from jax import lax
from jax.experimental import pallas as pl
from jax.experimental.pallas import tpu as pltpu
from jax.sharding import Mesh, PartitionSpec as P

DP = ("y", "xh")
TM = ("z", "xl", "core")
ALL = DP + TM
PLANE = ("xh", "z", "xl")
RING = ("y", "core")
CHIPS = ("y", "xh", "z", "xl")
F32 = jnp.float32
BF16 = jnp.bfloat16
REACH = 2


def size_of(names):
    size = 1
    for name in names:
        size *= lax.axis_size(name)
    return size


def ring_shift(block, axes, offset):
    size = size_of(axes)
    return lax.ppermute(block, axes, [((i + offset) % size, i) for i in range(size)])


def window_at(block, offset):
    return ring_shift(block, TM, offset)


def other_core(block):
    return lax.ppermute(block, "core", [(0, 1), (1, 0)])


def to_bf16_grid(value):
    return lax.reduce_precision(value, 8, 7)


def rows_dot(a, b):
    return lax.dot_general(a, b, (((1,), (1,)), ((), ())), preferred_element_type=F32)


def cols_dot(a, b):
    return lax.dot_general(a, b, (((0,), (0,)), ((), ())), preferred_element_type=F32)


def flags_kernel(
    horizons, windows, spot_ref, flags_ref, flags_x_ref, weights, count_ref, near_ref, act_ref, held,
    sem,
):
    copy = pltpu.make_async_copy(weights, held, sem)
    copy.start()
    chips, frames = flags_ref.shape
    span = 2 * frames
    device, tm, core = spot_ref[0, 0], spot_ref[0, 1], spot_ref[0, 2]
    flags, flags_x = flags_ref[...], flags_x_ref[...]
    flags = jnp.concatenate(
        [jnp.where(core == 0, flags, flags_x), jnp.where(core == 0, flags_x, flags)], axis=1
    )
    row = lax.broadcasted_iota(jnp.int32, flags.shape, 0)
    lane = lax.broadcasted_iota(jnp.int32, flags.shape, 1)
    last = row % (windows // 2) == windows // 2 - 1
    following = jnp.where(last, 0.0, pltpu.roll(flags, chips - 1, 0))
    slot = lax.broadcasted_iota(jnp.int32, (chips, 16), 1)
    source = lax.broadcasted_iota(jnp.int32, (chips, 16), 0)

    def picked(values, reach, transposed):
        window = slot - reach
        inside = (tm + window >= 0) & (tm + window < windows)
        out = 0.0
        for half in range(2):
            pick = (2 * source + half == device + window) & inside
            pick = jnp.where(pick, 1.0, 0.0).astype(BF16)
            part = values[:, half * frames : (half + 1) * frames].astype(BF16)
            out = out + (cols_dot(part, pick) if transposed else cols_dot(pick, part))
        return out

    total = jnp.zeros((1, span), F32)
    for h in range(1, horizons + 1):
        ahead = jnp.where(
            lane < span - h, pltpu.roll(flags, span - h, 1), pltpu.roll(following, span - h, 1)
        )
        pairs = flags * ahead
        total = total + jnp.sum(pairs, axis=0, keepdims=True)
        act_ref[(h - 1) * frames : h * frames] = picked(pairs, REACH, True)
    count_ref[...] = jnp.broadcast_to(jnp.sum(total, axis=1, keepdims=True), count_ref.shape)
    near_ref[...] = picked(flags, 2 * REACH, False)
    copy.wait()


def stacked_dot(rows, weights, out_ref):
    windows, stacked, width = out_ref.shape
    tile = 512
    frames = stacked * width // weights.shape[1]
    for at in range(0, weights.shape[1], tile):
        part = jnp.dot(rows, weights[:, at : at + tile], preferred_element_type=F32).astype(BF16)
        step, lane = divmod(at, width)
        for w in range(windows):
            out_ref[w, step * frames : (step + 1) * frames, lane : lane + tile] = part[
                w * frames : (w + 1) * frames
            ]


def pred_kernel(low2, ctx, high2, weights, out_ref, rows, sems):
    frames = ctx.shape[0]
    copies = [
        pltpu.make_async_copy(block, rows.at[pl.ds(slot * frames, frames)], sems.at[slot])
        for slot, block in enumerate(
            (low2.at[pl.ds(frames, frames)], ctx, high2.at[pl.ds(frames, frames)])
        )
    ]
    for copy in copies:
        copy.start()
    for copy in copies:
        copy.wait()
    stacked_dot(rows[...], weights, out_ref)


def delta_kernel(
    horizons, core_ref, count_ref, flags_ref, act_ref, preds_ref, weights,
    both, low2, high2, low4, high4, both_x, low2_x, high2_x, low4_x, high4_x,
    out_0, out_1, out_2, out_3, loss_ref, codes, code_acc, odd_ctx, odd_pred, blocks, sems,
):
    frames, width = low4.shape
    scale = width ** (-0.5)
    ring, cores = blocks.shape[:2]
    parts = ring * cores
    pred_cols, code_cols = horizons * width // parts, width // parts
    core, place = core_ref[0, 0], core_ref[0, 1]

    def put(sem, block, start, held, slot):
        at = slot * frames
        if not isinstance(slot, int):
            at = pl.multiple_of(at, frames)
        return pltpu.make_async_copy(
            block.at[pl.ds(start, frames)], held.at[pl.ds(at, frames)], sems.at[sem]
        )

    ctx_copies = [
        put(0, low2_x, frames, odd_ctx, 1 - core),
        put(1, both_x, frames, odd_ctx, 2 - core),
        put(2, high2_x, frames, odd_ctx, 3 - core),
    ]
    code_copies = [
        put(3, low4, 0, codes, 1),
        put(4, low2, 0, codes, 3),
        put(5, both, 0, codes, 5),
        put(6, high2, 0, codes, 7),
        put(7, high4, 0, codes, 9),
        put(8, low4_x, 0, codes, 2 - 2 * core),
        put(9, low2_x, 0, codes, 4 - 2 * core),
        put(10, both_x, 0, codes, 6 - 2 * core),
        put(11, high2_x, 0, codes, 8 - 2 * core),
        put(12, high4_x, 0, codes, 10 - 2 * core),
    ]
    for copy in ctx_copies + code_copies:
        copy.start()
    for copy in ctx_copies:
        copy.wait()
    stacked_dot(odd_ctx[frames : 3 * frames], weights, odd_pred)
    for copy in code_copies:
        copy.wait()
    shape = (horizons * frames, frames)
    row = lax.broadcasted_iota(jnp.int32, shape, 0)
    ahead = row % frames + row // frames + 1
    col = lax.broadcasted_iota(jnp.int32, shape, 1)
    here, after = col == ahead, col == ahead - frames
    preds = {-2: preds_ref[0], -1: odd_pred[0], 0: preds_ref[1], 1: odd_pred[1], 2: preds_ref[2]}
    factor = (1.0 / jnp.maximum(count_ref[:, :1], 1.0)) * scale
    beside = (-2, -1, 1, 2)
    for window in (-2, -1, 1, 2, 0):
        base = (window + 3) * frames
        query = preds[window]
        scores = rows_dot(query, codes[base : base + 5 * frames]) * scale
        block = {
            d: scores[:, (d + 2) * frames : (d + 3) * frames] for d in range(-REACH, REACH + 1)
        }
        positive = jnp.sum(
            jnp.where(here, block[0], 0.0) + jnp.where(after, block[1], 0.0),
            axis=1,
            keepdims=True,
        )
        for d in beside:
            usable = flags_ref[window + d + 4 : window + d + 5, :]
            block[d] = jnp.where(usable > 0, block[d], -1e30)
        top = jnp.maximum(jnp.maximum(block[-2], block[-1]), jnp.maximum(block[1], block[2]))
        top = jnp.maximum(positive, jnp.max(top, axis=1, keepdims=True))
        total = sum(jnp.exp(block[d] - top) for d in beside)
        total = jnp.sum(total, axis=1, keepdims=True)
        log_total = top + jnp.log(jnp.exp(positive - top) + total)
        active = act_ref[:, window + 2 : window + 3]
        weight = factor * active
        pos_coef = weight * (jnp.exp(positive - log_total) - 1.0)
        pos_after = jnp.where(after, pos_coef, 0.0).astype(BF16)
        if window != 0:
            coef = (weight * jnp.exp(block[-window] - log_total)).astype(BF16)
            term = cols_dot(coef, query)
            if window == -1:
                term = term + cols_dot(pos_after, query)
            if window == -2:
                code_acc[...] = term
            else:
                code_acc[...] += term
        else:
            coefs = {d: (weight * jnp.exp(block[d] - log_total)).astype(BF16) for d in beside}
            coefs[0] = jnp.where(here, pos_coef, 0.0).astype(BF16)
            wide = jnp.concatenate([coefs[d] for d in range(-REACH, REACH + 1)], axis=1)
            delta = jnp.dot(
                wide, codes[base : base + 5 * frames], preferred_element_type=F32
            ) + jnp.dot(
                pos_after, codes[base + 3 * frames : base + 4 * frames], preferred_element_type=F32
            )
            delta = delta.astype(BF16)
            for part in range(parts):
                step, at = divmod(part * pred_cols, width)
                blocks[part // cores, part % cores, :, :pred_cols] = delta[
                    step * frames : (step + 1) * frames, at : at + pred_cols
                ]
            code_delta = (code_acc[...] + cols_dot(coefs[0], query)).astype(BF16)
            for part in range(parts):
                blocks[part // cores, part % cores, :, pred_cols:] = code_delta[
                    :, part * code_cols : (part + 1) * code_cols
                ]
            loss = jnp.sum(active * (log_total - positive), axis=0, keepdims=True)
            loss_ref[...] = jnp.broadcast_to(loss, loss_ref.shape)
    for back, out in enumerate((out_0, out_1, out_2, out_3)):
        out[...] = blocks[(place + ring - back) % ring]


def term_kernel(
    pred_cols, core_ref, same_0, same_1, same_2, same_3, cross_0, cross_1, cross_2, cross_3,
    rows_same, rows_cross, out_ref, held, rows_held, held_sems, rows_sems,
):
    cores, frames, lanes_all = same_0.shape
    plane = out_ref.shape[0]
    core, place = core_ref[0, 0], core_ref[0, 1]
    both = ((same_0, same_1, same_2, same_3), (cross_0, cross_1, cross_2, cross_3))
    ring = len(both[0])
    delta_copies, row_copies = [], [[] for _ in range(4)]
    for side, blocks in enumerate(both):
        for spot, block in enumerate(blocks):
            start = pl.multiple_of((place + spot) % ring * frames, frames)
            delta_copies.append(
                pltpu.make_async_copy(
                    block.at[core], held.at[side, pl.ds(start, frames)], held_sems.at[side, spot]
                )
            )
    for group in range(4):
        source = rows_cross if group % 2 else rows_same
        for spot in range(ring):
            row_copies[group].append(
                pltpu.make_async_copy(
                    source.at[spot, pl.ds((1 - group // 2) * frames, frames)],
                    rows_held.at[group, pl.ds(spot * frames, frames)],
                    rows_sems.at[group, spot],
                )
            )
    for copy in delta_copies + sum(row_copies, []):
        copy.start()
    for copy in delta_copies:
        copy.wait()
    rows = 2 * rows_held.shape[2] // ring
    span = rows // plane
    for first, lanes in ((0, slice(0, pred_cols)), (2, slice(pred_cols, lanes_all))):
        for copy in row_copies[first] + row_copies[first + 1]:
            copy.wait()
        for half in range(ring // 2):
            blocks = slice(half * rows, (half + 1) * rows)
            term = cols_dot(rows_held[first, :, blocks], held[0, :, lanes])
            term = term + cols_dot(rows_held[first + 1, :, blocks], held[1, :, lanes])
            term = term.reshape(2, plane, span // 2, -1)
            term = jnp.concatenate([term[0], term[1]], axis=1).astype(BF16)
            out_ref[:, half * span : (half + 1) * span, lanes] = term


def sum_kernel(terms_ref, loss_ref, out_ref):
    total = terms_ref[0].astype(F32)
    for source in range(1, terms_ref.shape[0]):
        total = total + terms_ref[source].astype(F32)
    owned = out_ref.shape[1] // 2
    loss = jnp.sum(loss_ref[:, :1], axis=0, keepdims=True)
    for part in range(out_ref.shape[0]):
        out_ref[part, :owned] = total[part * owned : (part + 1) * owned]
        out_ref[part, owned:] = jnp.broadcast_to(loss, (owned, out_ref.shape[2]))


def per_device(features, context, predictor, projection, lengths, frame_mask):
    frames, width = features.shape[1], features.shape[2]
    horizons = predictor.shape[1]
    feat, ctx = features[0], context[0]
    windows, recordings = size_of(TM), size_of(DP)
    devices = windows * recordings
    parts, plane = size_of(RING), size_of(PLANE)
    tm = lax.axis_index(TM)
    core = lax.axis_index("core")

    encoded = jnp.dot(feat, projection, preferred_element_type=F32).astype(BF16)
    both = jnp.concatenate([encoded, ctx], axis=0)
    low2, high2 = window_at(both, -2), window_at(both, 2)
    both_x = other_core(both)
    positions = lax.broadcasted_iota(jnp.int32, (1, frames), 1)
    usable = ((frame_mask == 1) & (positions < lengths)).astype(F32)
    usable, both_x = lax.optimization_barrier((usable, both_x))
    chips = size_of(CHIPS)
    flags = lax.all_to_all(jnp.broadcast_to(usable, (chips, frames)), CHIPS, 0, 0, tiled=True)
    flags_x = other_core(flags)
    low4, high4 = window_at(encoded, -4), window_at(encoded, 4)
    weights = predictor.reshape(width, horizons * width)
    low2, high2, weights, flags = lax.optimization_barrier((low2, high2, weights, flags))
    low2_x, high2_x = other_core(low2), other_core(high2)
    low4_x, high4_x = other_core(low4), other_core(high4)
    rows_ring = lax.all_gather(jnp.concatenate([feat, ctx], axis=0), "y")

    smem = pl.BlockSpec(memory_space=pltpu.SMEM)
    vmem = pl.BlockSpec(memory_space=pltpu.VMEM)
    anywhere = pl.BlockSpec(memory_space=pl.ANY)
    limit = pltpu.CompilerParams(vmem_limit_bytes=16 * 2**20)

    spot = jnp.stack([lax.axis_index(ALL), tm, core]).reshape(1, 3).astype(jnp.int32)
    count, near, act, weights = pl.pallas_call(
        functools.partial(flags_kernel, horizons, windows),
        out_shape=(
            jax.ShapeDtypeStruct((1, 128), F32),
            jax.ShapeDtypeStruct((16, frames), F32),
            jax.ShapeDtypeStruct((horizons * frames, 16), F32),
            jax.ShapeDtypeStruct((width, horizons * width), BF16),
        ),
        in_specs=[smem, vmem, vmem, anywhere],
        out_specs=(vmem, vmem, vmem, vmem),
        scratch_shapes=[pltpu.SemaphoreType.DMA],
        compiler_params=limit,
    )(spot, flags, flags_x, weights)

    preds = pl.pallas_call(
        pred_kernel,
        out_shape=jax.ShapeDtypeStruct((3, horizons * frames, width), BF16),
        in_specs=[anywhere] * 3 + [vmem],
        out_specs=vmem,
        scratch_shapes=[pltpu.VMEM((3 * frames, width), BF16), pltpu.SemaphoreType.DMA((3,))],
        compiler_params=limit,
        cost_estimate=pl.CostEstimate(flops=1600000000, bytes_accessed=6500000, transcendentals=0),
    )(low2, ctx, high2, weights)
    pred_cols, code_cols = horizons * width // parts, width // parts
    lanes = pred_cols + code_cols
    core_word = jnp.stack([core, lax.axis_index("y")]).reshape(1, 2).astype(jnp.int32)
    ring = lax.axis_size("y")
    *deltas, loss_part = pl.pallas_call(
        functools.partial(delta_kernel, horizons),
        out_shape=[jax.ShapeDtypeStruct((2, frames, lanes), BF16)] * ring
        + [jax.ShapeDtypeStruct((1, 128), F32)],
        in_specs=[smem] + [vmem] * 5 + [anywhere] * 10,
        out_specs=[vmem] * (ring + 1),
        scratch_shapes=[
            pltpu.VMEM((11 * frames, width), BF16),
            pltpu.VMEM((frames, width), F32),
            pltpu.VMEM((4 * frames, width), BF16),
            pltpu.VMEM((2, horizons * frames, width), BF16),
            pltpu.VMEM((ring, 2, frames, lanes), BF16),
            pltpu.SemaphoreType.DMA((13,)),
        ],
        compiler_params=pltpu.CompilerParams(vmem_limit_bytes=20 * 2**20),
        cost_estimate=pl.CostEstimate(
            flops=4000000000, bytes_accessed=12000000, transcendentals=900000
        ),
    )(
        core_word, count, near, act, preds, weights,
        both, low2, high2, low4, high4, both_x, low2_x, high2_x, low4_x, high4_x,
    )

    same = [deltas[0]] + [ring_shift(deltas[step], ("y",), step) for step in range(1, ring)]
    _, rows_ring = lax.optimization_barrier((same[1], rows_ring))
    rows_cross = other_core(rows_ring)
    loss_part = lax.all_to_all(
        jnp.broadcast_to(loss_part, (lax.axis_size("z"), 128)), "z", 0, 0, tiled=True
    )
    *same[1:], loss_part = lax.optimization_barrier((*same[1:], loss_part))
    cross = [other_core(block) for block in same]
    terms = pl.pallas_call(
        functools.partial(term_kernel, pred_cols),
        out_shape=jax.ShapeDtypeStruct((plane, width // plane, lanes), BF16),
        in_specs=[smem] + [anywhere] * 10,
        out_specs=vmem,
        scratch_shapes=[
            pltpu.VMEM((2, ring * frames, lanes), BF16),
            pltpu.VMEM((4, ring * frames, width), BF16),
            pltpu.SemaphoreType.DMA((2, ring)),
            pltpu.SemaphoreType.DMA((4, ring)),
        ],
        compiler_params=pltpu.CompilerParams(vmem_limit_bytes=16 * 2**20),
        cost_estimate=pl.CostEstimate(flops=800000000, bytes_accessed=6000000, transcendentals=0),
    )(core_word, *same, *cross, rows_ring, rows_cross)

    owned = width // devices
    loss_part = jnp.sum(loss_part, axis=0, keepdims=True)
    terms, loss_part = lax.optimization_barrier((terms, loss_part))
    terms = lax.all_to_all(terms, PLANE, 0, 0, tiled=True)
    high = to_bf16_grid(loss_part)
    middle = to_bf16_grid(loss_part - high)
    loss_part = jnp.concatenate([high, middle, loss_part - high - middle], axis=0).astype(BF16)
    loss_plane = lax.all_gather(loss_part, ("xh", "xl")).reshape(-1, 128).astype(F32)
    sums = pl.pallas_call(
        sum_kernel,
        out_shape=jax.ShapeDtypeStruct((parts, 2 * owned, lanes), F32),
        in_specs=[vmem, vmem],
        out_specs=vmem,
    )(terms, loss_plane)
    got = lax.all_to_all(sums, RING, 0, 0, tiled=True)
    loss = jnp.sum(got[:, owned, 0]) * (1.0 / jnp.maximum(count[0, 0], 1.0))
    got = got[:, :owned].transpose(1, 0, 2)
    grad_pred = got[:, :, :pred_cols].reshape(owned, horizons, width)
    grad_proj = got[:, :, pred_cols:].reshape(owned, width)
    return (loss, grad_pred, grad_proj)


def solution(mesh):
    fine = Mesh(mesh.devices.reshape(4, 2, 8, 2, 2), ALL)
    placed = (P(DP, TM, None), P(DP, TM, None), P(), P(), P(DP, TM), P(DP, TM))
    return jax.shard_map(
        per_device,
        mesh=fine,
        in_specs=placed,
        out_specs=(P(), P(ALL, None, None), P(ALL, None)),
        check_vma=False,
    )
```

```python
import functools

import jax
import jax.numpy as jnp
from jax import lax
from jax.experimental import pallas as pl
from jax.experimental.pallas import tpu as pltpu
from jax.sharding import Mesh, PartitionSpec as P

DP = ("y", "xh")
TM = ("z", "xl", "core")
ALL = DP + TM
PLANE = ("xh", "z", "xl")
RING = ("y", "core")
CHIPS = ("y", "xh", "z", "xl")
F32 = jnp.float32
BF16 = jnp.bfloat16
REACH = 2


def size_of(names):
    size = 1
    for name in names:
        size *= lax.axis_size(name)
    return size


def ring_shift(block, axes, offset):
    size = size_of(axes)
    return lax.ppermute(block, axes, [((i + offset) % size, i) for i in range(size)])


def window_at(block, offset):
    return ring_shift(block, TM, offset)


def other_core(block):
    return lax.ppermute(block, "core", [(0, 1), (1, 0)])


def to_bf16_grid(value):
    return lax.reduce_precision(value, 8, 7)


def rows_dot(a, b):
    return lax.dot_general(a, b, (((1,), (1,)), ((), ())), preferred_element_type=F32)


def cols_dot(a, b):
    return lax.dot_general(a, b, (((0,), (0,)), ((), ())), preferred_element_type=F32)


def prepare_kernel(
    horizons, windows, spot_ref, flags_ref, weights, low2, ctx, high2, count_ref, near_ref, act_ref,
    preds_ref, rows, sems,
):
    chips, span = flags_ref.shape
    frames = span // 2
    copies = [
        pltpu.make_async_copy(block, rows.at[pl.ds(slot * frames, frames)], sems.at[slot])
        for slot, block in enumerate(
            (low2.at[pl.ds(frames, frames)], ctx, high2.at[pl.ds(frames, frames)])
        )
    ]
    for copy in copies:
        copy.start()
    device, tm = spot_ref[0, 0], spot_ref[0, 1]
    flags = flags_ref[...]
    row = lax.broadcasted_iota(jnp.int32, flags.shape, 0)
    lane = lax.broadcasted_iota(jnp.int32, flags.shape, 1)
    last = row % (windows // 2) == windows // 2 - 1
    following = jnp.where(last, 0.0, pltpu.roll(flags, chips - 1, 0))
    slot = lax.broadcasted_iota(jnp.int32, (chips, 16), 1)
    source = lax.broadcasted_iota(jnp.int32, (chips, 16), 0)

    def picked(values, reach, transposed):
        window = slot - reach
        inside = (tm + window >= 0) & (tm + window < windows)
        out = 0.0
        for half in range(2):
            pick = (2 * source + half == device + window) & inside
            pick = jnp.where(pick, 1.0, 0.0).astype(BF16)
            part = values[:, half * frames : (half + 1) * frames].astype(BF16)
            out = out + (cols_dot(part, pick) if transposed else cols_dot(pick, part))
        return out

    total = jnp.zeros((1, span), F32)
    for h in range(1, horizons + 1):
        ahead = jnp.where(
            lane < span - h, pltpu.roll(flags, span - h, 1), pltpu.roll(following, span - h, 1)
        )
        pairs = flags * ahead
        total = total + jnp.sum(pairs, axis=0, keepdims=True)
        act_ref[(h - 1) * frames : h * frames] = picked(pairs, REACH, True)
    count_ref[...] = jnp.broadcast_to(jnp.sum(total, axis=1, keepdims=True), count_ref.shape)
    near_ref[...] = picked(flags, 2 * REACH, False)
    for copy in copies:
        copy.wait()
    stacked_dot(rows[...], weights, preds_ref)


def stacked_dot(rows, weights, out_ref):
    windows, stacked, width = out_ref.shape
    tile = 512
    frames = stacked * width // weights.shape[1]
    for at in range(0, weights.shape[1], tile):
        part = jnp.dot(rows, weights[:, at : at + tile], preferred_element_type=F32).astype(BF16)
        step, lane = divmod(at, width)
        for w in range(windows):
            out_ref[w, step * frames : (step + 1) * frames, lane : lane + tile] = part[
                w * frames : (w + 1) * frames
            ]


def delta_kernel(
    horizons, core_ref, count_ref, flags_ref, act_ref, preds_ref, weights,
    both, low2, high2, low4, high4, both_x, low2_x, high2_x, low4_x, high4_x,
    out_0, out_1, out_2, out_3, loss_ref, codes, code_acc, odd_ctx, odd_pred, blocks, sems,
):
    frames, width = low4.shape
    scale = width ** (-0.5)
    ring, cores = blocks.shape[:2]
    parts = ring * cores
    pred_cols, code_cols = horizons * width // parts, width // parts
    core, place = core_ref[0, 0], core_ref[0, 1]

    def put(sem, block, start, held, slot):
        at = slot * frames
        if not isinstance(slot, int):
            at = pl.multiple_of(at, frames)
        return pltpu.make_async_copy(
            block.at[pl.ds(start, frames)], held.at[pl.ds(at, frames)], sems.at[sem]
        )

    ctx_copies = [
        put(0, low2_x, frames, odd_ctx, 1 - core),
        put(1, both_x, frames, odd_ctx, 2 - core),
        put(2, high2_x, frames, odd_ctx, 3 - core),
    ]
    code_copies = [
        put(3, low4, 0, codes, 1),
        put(4, low2, 0, codes, 3),
        put(5, both, 0, codes, 5),
        put(6, high2, 0, codes, 7),
        put(7, high4, 0, codes, 9),
        put(8, low4_x, 0, codes, 2 - 2 * core),
        put(9, low2_x, 0, codes, 4 - 2 * core),
        put(10, both_x, 0, codes, 6 - 2 * core),
        put(11, high2_x, 0, codes, 8 - 2 * core),
        put(12, high4_x, 0, codes, 10 - 2 * core),
    ]
    for copy in ctx_copies + code_copies:
        copy.start()
    for copy in ctx_copies:
        copy.wait()
    stacked_dot(odd_ctx[frames : 3 * frames], weights, odd_pred)
    for copy in code_copies:
        copy.wait()
    shape = (horizons * frames, frames)
    row = lax.broadcasted_iota(jnp.int32, shape, 0)
    ahead = row % frames + row // frames + 1
    col = lax.broadcasted_iota(jnp.int32, shape, 1)
    here, after = col == ahead, col == ahead - frames
    preds = {-2: preds_ref[0], -1: odd_pred[0], 0: preds_ref[1], 1: odd_pred[1], 2: preds_ref[2]}
    factor = (1.0 / jnp.maximum(count_ref[:, :1], 1.0)) * scale
    beside = (-2, -1, 1, 2)
    for window in (-2, -1, 1, 2, 0):
        base = (window + 3) * frames
        query = preds[window]
        scores = rows_dot(query, codes[base : base + 5 * frames]) * scale
        block = {
            d: scores[:, (d + 2) * frames : (d + 3) * frames] for d in range(-REACH, REACH + 1)
        }
        positive = jnp.sum(
            jnp.where(here, block[0], 0.0) + jnp.where(after, block[1], 0.0),
            axis=1,
            keepdims=True,
        )
        for d in beside:
            usable = flags_ref[window + d + 4 : window + d + 5, :]
            block[d] = jnp.where(usable > 0, block[d], -1e30)
        top = jnp.maximum(jnp.maximum(block[-2], block[-1]), jnp.maximum(block[1], block[2]))
        top = jnp.maximum(positive, jnp.max(top, axis=1, keepdims=True))
        total = sum(jnp.exp(block[d] - top) for d in beside)
        total = jnp.sum(total, axis=1, keepdims=True)
        log_total = top + jnp.log(jnp.exp(positive - top) + total)
        active = act_ref[:, window + 2 : window + 3]
        weight = factor * active
        pos_coef = weight * (jnp.exp(positive - log_total) - 1.0)
        pos_after = jnp.where(after, pos_coef, 0.0).astype(BF16)
        if window != 0:
            coef = (weight * jnp.exp(block[-window] - log_total)).astype(BF16)
            term = cols_dot(coef, query)
            if window == -1:
                term = term + cols_dot(pos_after, query)
            if window == -2:
                code_acc[...] = term
            else:
                code_acc[...] += term
        else:
            coefs = {d: (weight * jnp.exp(block[d] - log_total)).astype(BF16) for d in beside}
            coefs[0] = jnp.where(here, pos_coef, 0.0).astype(BF16)
            wide = jnp.concatenate([coefs[d] for d in range(-REACH, REACH + 1)], axis=1)
            delta = jnp.dot(
                wide, codes[base : base + 5 * frames], preferred_element_type=F32
            ) + jnp.dot(
                pos_after, codes[base + 3 * frames : base + 4 * frames], preferred_element_type=F32
            )
            delta = delta.astype(BF16)
            for part in range(parts):
                step, at = divmod(part * pred_cols, width)
                blocks[part // cores, part % cores, :, :pred_cols] = delta[
                    step * frames : (step + 1) * frames, at : at + pred_cols
                ]
            code_delta = (code_acc[...] + cols_dot(coefs[0], query)).astype(BF16)
            for part in range(parts):
                blocks[part // cores, part % cores, :, pred_cols:] = code_delta[
                    :, part * code_cols : (part + 1) * code_cols
                ]
            loss = jnp.sum(active * (log_total - positive), axis=0, keepdims=True)
            loss_ref[...] = jnp.broadcast_to(loss, loss_ref.shape)
    for back, out in enumerate((out_0, out_1, out_2, out_3)):
        out[...] = blocks[(place + ring - back) % ring]


def term_kernel(
    pred_cols, core_ref, same_0, same_1, same_2, same_3, cross_0, cross_1, cross_2, cross_3,
    rows_same, rows_cross, out_ref, held,
):
    _, frames, lanes = same_0.shape
    plane = out_ref.shape[0]
    core, place = core_ref[0, 0], core_ref[0, 1]
    both = ((same_0, same_1, same_2, same_3), (cross_0, cross_1, cross_2, cross_3))
    ring = len(both[0])
    for side, blocks in enumerate(both):
        for spot, block in enumerate(blocks):
            spot = (place + spot) % ring
            held[side, spot, :frames, :pred_cols] = jnp.zeros((frames, pred_cols), BF16)
            held[side, spot, :frames, pred_cols:] = block[core, :, pred_cols:]
            held[side, spot, frames:, :pred_cols] = block[core, :, :pred_cols]
            held[side, spot, frames:, pred_cols:] = jnp.zeros((frames, lanes - pred_cols), BF16)
    width = rows_same.shape[2]
    rows = 2 * width // ring
    span = rows // plane
    deltas = [held[side].reshape(-1, lanes) for side in range(2)]
    for half in range(ring // 2):
        term = 0.0
        for source, delta in zip((rows_same, rows_cross), deltas):
            term = term + cols_dot(
                source[:, :, half * rows : (half + 1) * rows].reshape(-1, rows), delta
            )
        term = term.reshape(2, plane, span // 2, lanes)
        term = jnp.concatenate([term[0], term[1]], axis=1).astype(BF16)
        out_ref[:, half * span : (half + 1) * span] = term


def sum_kernel(terms_ref, loss_ref, out_ref):
    total = terms_ref[0].astype(F32)
    for source in range(1, terms_ref.shape[0]):
        total = total + terms_ref[source].astype(F32)
    owned = out_ref.shape[1] // 2
    loss = jnp.sum(loss_ref[:, :1], axis=0, keepdims=True)
    for part in range(out_ref.shape[0]):
        out_ref[part, :owned] = total[part * owned : (part + 1) * owned]
        out_ref[part, owned:] = jnp.broadcast_to(loss, (owned, out_ref.shape[2]))


def per_device(features, context, predictor, projection, lengths, frame_mask):
    frames, width = features.shape[1], features.shape[2]
    horizons = predictor.shape[1]
    feat, ctx = features[0], context[0]
    windows, recordings = size_of(TM), size_of(DP)
    devices = windows * recordings
    parts, plane = size_of(RING), size_of(PLANE)
    tm = lax.axis_index(TM)
    core = lax.axis_index("core")

    encoded = jnp.dot(feat, projection, preferred_element_type=F32).astype(BF16)
    both = jnp.concatenate([encoded, ctx], axis=0)
    low2, high2 = window_at(both, -2), window_at(both, 2)
    both_x = other_core(both)
    positions = lax.broadcasted_iota(jnp.int32, (1, frames), 1)
    usable = ((frame_mask == 1) & (positions < lengths)).astype(F32)
    usable_x = other_core(usable)
    pair = jnp.concatenate(
        [jnp.where(core == 0, usable, usable_x), jnp.where(core == 0, usable_x, usable)], axis=1
    )
    pair, both_x = lax.optimization_barrier((pair, both_x))
    chips = size_of(CHIPS)
    flags = lax.all_to_all(
        jnp.broadcast_to(pair, (chips, 2 * frames)), CHIPS, 0, 0, tiled=True
    )
    low4, high4 = window_at(encoded, -4), window_at(encoded, 4)
    weights = predictor.reshape(width, horizons * width)
    low2, high2, weights, flags = lax.optimization_barrier((low2, high2, weights, flags))
    low2_x, high2_x = other_core(low2), other_core(high2)
    low4_x, high4_x = other_core(low4), other_core(high4)
    rows_ring = lax.all_gather(jnp.concatenate([feat, ctx], axis=0), "y")

    smem = pl.BlockSpec(memory_space=pltpu.SMEM)
    vmem = pl.BlockSpec(memory_space=pltpu.VMEM)
    anywhere = pl.BlockSpec(memory_space=pl.ANY)
    limit = pltpu.CompilerParams(vmem_limit_bytes=16 * 2**20)

    spot = jnp.stack([lax.axis_index(ALL), tm]).reshape(1, 2).astype(jnp.int32)
    count, near, act, preds = pl.pallas_call(
        functools.partial(prepare_kernel, horizons, windows),
        out_shape=(
            jax.ShapeDtypeStruct((1, 128), F32),
            jax.ShapeDtypeStruct((16, frames), F32),
            jax.ShapeDtypeStruct((horizons * frames, 16), F32),
            jax.ShapeDtypeStruct((3, horizons * frames, width), BF16),
        ),
        in_specs=[smem, vmem, vmem] + [anywhere] * 3,
        out_specs=(vmem, vmem, vmem, vmem),
        scratch_shapes=[pltpu.VMEM((3 * frames, width), BF16), pltpu.SemaphoreType.DMA((3,))],
        compiler_params=limit,
        cost_estimate=pl.CostEstimate(flops=1700000000, bytes_accessed=6500000, transcendentals=0),
    )(spot, flags, weights, low2, ctx, high2)
    *_, rows_ring = lax.optimization_barrier((low2_x, high2_x, low4_x, high4_x, preds, rows_ring))
    rows_cross = other_core(rows_ring)

    pred_cols, code_cols = horizons * width // parts, width // parts
    lanes = pred_cols + code_cols
    core_word = jnp.stack([core, lax.axis_index("y")]).reshape(1, 2).astype(jnp.int32)
    ring = lax.axis_size("y")
    *deltas, loss_part = pl.pallas_call(
        functools.partial(delta_kernel, horizons),
        out_shape=[jax.ShapeDtypeStruct((2, frames, lanes), BF16)] * ring
        + [jax.ShapeDtypeStruct((1, 128), F32)],
        in_specs=[smem] + [vmem] * 5 + [anywhere] * 10,
        out_specs=[vmem] * (ring + 1),
        scratch_shapes=[
            pltpu.VMEM((11 * frames, width), BF16),
            pltpu.VMEM((frames, width), F32),
            pltpu.VMEM((4 * frames, width), BF16),
            pltpu.VMEM((2, horizons * frames, width), BF16),
            pltpu.VMEM((ring, 2, frames, lanes), BF16),
            pltpu.SemaphoreType.DMA((13,)),
        ],
        compiler_params=pltpu.CompilerParams(vmem_limit_bytes=20 * 2**20),
        cost_estimate=pl.CostEstimate(
            flops=4000000000, bytes_accessed=12000000, transcendentals=900000
        ),
    )(
        core_word, count, near, act, preds, weights,
        both, low2, high2, low4, high4, both_x, low2_x, high2_x, low4_x, high4_x,
    )

    same = [deltas[0]] + [ring_shift(deltas[step], ("y",), step) for step in range(1, ring)]
    loss_part = lax.all_to_all(
        jnp.broadcast_to(loss_part, (lax.axis_size("z"), 128)), "z", 0, 0, tiled=True
    )
    *same[1:], loss_part = lax.optimization_barrier((*same[1:], loss_part))
    cross = [other_core(block) for block in same]
    terms = pl.pallas_call(
        functools.partial(term_kernel, pred_cols),
        out_shape=jax.ShapeDtypeStruct((plane, width // plane, lanes), BF16),
        in_specs=[smem] + [vmem] * 10,
        out_specs=vmem,
        scratch_shapes=[pltpu.VMEM((2, ring, 2 * frames, lanes), BF16)],
        compiler_params=limit,
        cost_estimate=pl.CostEstimate(flops=1600000000, bytes_accessed=6000000, transcendentals=0),
    )(core_word, *same, *cross, rows_ring, rows_cross)

    owned = width // devices
    loss_part = jnp.sum(loss_part, axis=0, keepdims=True)
    terms, loss_part = lax.optimization_barrier((terms, loss_part))
    terms = lax.all_to_all(terms, PLANE, 0, 0, tiled=True)
    high = to_bf16_grid(loss_part)
    middle = to_bf16_grid(loss_part - high)
    loss_part = jnp.concatenate([high, middle, loss_part - high - middle], axis=0).astype(BF16)
    loss_plane = lax.all_gather(loss_part, ("xh", "xl")).reshape(-1, 128).astype(F32)
    sums = pl.pallas_call(
        sum_kernel,
        out_shape=jax.ShapeDtypeStruct((parts, 2 * owned, lanes), F32),
        in_specs=[vmem, vmem],
        out_specs=vmem,
    )(terms, loss_plane)
    got = lax.all_to_all(sums, RING, 0, 0, tiled=True)
    loss = jnp.sum(got[:, owned, 0]) * (1.0 / jnp.maximum(count[0, 0], 1.0))
    got = got[:, :owned].transpose(1, 0, 2)
    grad_pred = got[:, :, :pred_cols].reshape(owned, horizons, width)
    grad_proj = got[:, :, pred_cols:].reshape(owned, width)
    return (loss, grad_pred, grad_proj)


def solution(mesh):
    fine = Mesh(mesh.devices.reshape(4, 2, 8, 2, 2), ALL)
    placed = (P(DP, TM, None), P(DP, TM, None), P(), P(), P(DP, TM), P(DP, TM))
    return jax.shard_map(
        per_device,
        mesh=fine,
        in_specs=placed,
        out_specs=(P(), P(ALL, None, None), P(ALL, None)),
        check_vma=False,
    )
```

```python
import functools

import jax
import jax.numpy as jnp
from jax import lax
from jax.experimental import pallas as pl
from jax.experimental.pallas import tpu as pltpu
from jax.sharding import Mesh, PartitionSpec as P

DP = ("y", "xh")
TM = ("z", "xl", "core")
ALL = DP + TM
PLANE = ("xh", "z", "xl")
RING = ("y", "core")
CHIPS = ("y", "xh", "z", "xl")
F32 = jnp.float32
BF16 = jnp.bfloat16
REACH = 2


def size_of(names):
    size = 1
    for name in names:
        size *= lax.axis_size(name)
    return size


def ring_shift(block, axes, offset):
    size = size_of(axes)
    return lax.ppermute(block, axes, [((i + offset) % size, i) for i in range(size)])


def window_at(block, offset):
    return ring_shift(block, TM, offset)


def other_core(block):
    return lax.ppermute(block, "core", [(0, 1), (1, 0)])


def rows_dot(a, b):
    return lax.dot_general(a, b, (((1,), (1,)), ((), ())), preferred_element_type=F32)


def cols_dot(a, b):
    return lax.dot_general(a, b, (((0,), (0,)), ((), ())), preferred_element_type=F32)


def prepare_kernel(
    horizons, windows, spot_ref, flags_ref, weights, low2, ctx, high2, count_ref, near_ref, act_ref,
    preds_ref, rows, sems,
):
    chips, span = flags_ref.shape
    frames = span // 2
    copies = [
        pltpu.make_async_copy(block, rows.at[pl.ds(slot * frames, frames)], sems.at[slot])
        for slot, block in enumerate(
            (low2.at[pl.ds(frames, frames)], ctx, high2.at[pl.ds(frames, frames)])
        )
    ]
    for copy in copies:
        copy.start()
    device, tm = spot_ref[0, 0], spot_ref[0, 1]
    flags = flags_ref[...]
    row = lax.broadcasted_iota(jnp.int32, flags.shape, 0)
    lane = lax.broadcasted_iota(jnp.int32, flags.shape, 1)
    last = row % (windows // 2) == windows // 2 - 1
    following = jnp.where(last, 0.0, pltpu.roll(flags, chips - 1, 0))
    slot = lax.broadcasted_iota(jnp.int32, (chips, 16), 1)
    source = lax.broadcasted_iota(jnp.int32, (chips, 16), 0)

    def picked(values, reach, transposed):
        window = slot - reach
        inside = (tm + window >= 0) & (tm + window < windows)
        out = 0.0
        for half in range(2):
            pick = (2 * source + half == device + window) & inside
            pick = jnp.where(pick, 1.0, 0.0).astype(BF16)
            part = values[:, half * frames : (half + 1) * frames].astype(BF16)
            out = out + (cols_dot(part, pick) if transposed else cols_dot(pick, part))
        return out

    total = jnp.zeros((1, span), F32)
    for h in range(1, horizons + 1):
        ahead = jnp.where(
            lane < span - h, pltpu.roll(flags, span - h, 1), pltpu.roll(following, span - h, 1)
        )
        pairs = flags * ahead
        total = total + jnp.sum(pairs, axis=0, keepdims=True)
        act_ref[(h - 1) * frames : h * frames] = picked(pairs, REACH, True)
    count_ref[...] = jnp.broadcast_to(jnp.sum(total, axis=1, keepdims=True), count_ref.shape)
    near_ref[...] = picked(flags, 2 * REACH, False)
    for copy in copies:
        copy.wait()
    stacked_dot(rows[...], weights, preds_ref)


def stacked_dot(rows, weights, out_ref):
    windows, stacked, width = out_ref.shape
    tile = 512
    frames = stacked * width // weights.shape[1]
    for at in range(0, weights.shape[1], tile):
        part = jnp.dot(rows, weights[:, at : at + tile], preferred_element_type=F32).astype(BF16)
        step, lane = divmod(at, width)
        for w in range(windows):
            out_ref[w, step * frames : (step + 1) * frames, lane : lane + tile] = part[
                w * frames : (w + 1) * frames
            ]


def delta_kernel(
    horizons, core_ref, count_ref, flags_ref, act_ref, preds_ref, weights,
    both, low2, high2, low4, high4, both_x, low2_x, high2_x, low4_x, high4_x,
    out_0, out_1, out_2, out_3, loss_ref, codes, code_acc, odd_ctx, odd_pred, blocks, sems,
):
    frames, width = low4.shape
    scale = width ** (-0.5)
    ring, cores = blocks.shape[:2]
    parts = ring * cores
    pred_cols, code_cols = horizons * width // parts, width // parts
    core, place = core_ref[0, 0], core_ref[0, 1]

    def put(sem, block, start, held, slot):
        at = slot * frames
        if not isinstance(slot, int):
            at = pl.multiple_of(at, frames)
        return pltpu.make_async_copy(
            block.at[pl.ds(start, frames)], held.at[pl.ds(at, frames)], sems.at[sem]
        )

    ctx_copies = [
        put(0, low2_x, frames, odd_ctx, 1 - core),
        put(1, both_x, frames, odd_ctx, 2 - core),
        put(2, high2_x, frames, odd_ctx, 3 - core),
    ]
    code_copies = [
        put(3, low4, 0, codes, 1),
        put(4, low2, 0, codes, 3),
        put(5, both, 0, codes, 5),
        put(6, high2, 0, codes, 7),
        put(7, high4, 0, codes, 9),
        put(8, low4_x, 0, codes, 2 - 2 * core),
        put(9, low2_x, 0, codes, 4 - 2 * core),
        put(10, both_x, 0, codes, 6 - 2 * core),
        put(11, high2_x, 0, codes, 8 - 2 * core),
        put(12, high4_x, 0, codes, 10 - 2 * core),
    ]
    for copy in ctx_copies + code_copies:
        copy.start()
    for copy in ctx_copies:
        copy.wait()
    stacked_dot(odd_ctx[frames : 3 * frames], weights, odd_pred)
    for copy in code_copies:
        copy.wait()
    shape = (horizons * frames, frames)
    row = lax.broadcasted_iota(jnp.int32, shape, 0)
    ahead = row % frames + row // frames + 1
    col = lax.broadcasted_iota(jnp.int32, shape, 1)
    here, after = col == ahead, col == ahead - frames
    preds = {-2: preds_ref[0], -1: odd_pred[0], 0: preds_ref[1], 1: odd_pred[1], 2: preds_ref[2]}
    factor = (1.0 / jnp.maximum(count_ref[:, :1], 1.0)) * scale
    beside = (-2, -1, 1, 2)
    for window in (-2, -1, 1, 2, 0):
        base = (window + 3) * frames
        query = preds[window]
        scores = rows_dot(query, codes[base : base + 5 * frames]) * scale
        block = {
            d: scores[:, (d + 2) * frames : (d + 3) * frames] for d in range(-REACH, REACH + 1)
        }
        positive = jnp.sum(
            jnp.where(here, block[0], 0.0) + jnp.where(after, block[1], 0.0),
            axis=1,
            keepdims=True,
        )
        for d in beside:
            usable = flags_ref[window + d + 4 : window + d + 5, :]
            block[d] = jnp.where(usable > 0, block[d], -1e30)
        top = jnp.maximum(jnp.maximum(block[-2], block[-1]), jnp.maximum(block[1], block[2]))
        top = jnp.maximum(positive, jnp.max(top, axis=1, keepdims=True))
        total = sum(jnp.exp(block[d] - top) for d in beside)
        total = jnp.sum(total, axis=1, keepdims=True)
        log_total = top + jnp.log(jnp.exp(positive - top) + total)
        active = act_ref[:, window + 2 : window + 3]
        weight = factor * active
        pos_coef = weight * (jnp.exp(positive - log_total) - 1.0)
        pos_after = jnp.where(after, pos_coef, 0.0).astype(BF16)
        if window != 0:
            coef = (weight * jnp.exp(block[-window] - log_total)).astype(BF16)
            term = cols_dot(coef, query)
            if window == -1:
                term = term + cols_dot(pos_after, query)
            if window == -2:
                code_acc[...] = term
            else:
                code_acc[...] += term
        else:
            coefs = {d: (weight * jnp.exp(block[d] - log_total)).astype(BF16) for d in beside}
            coefs[0] = jnp.where(here, pos_coef, 0.0).astype(BF16)
            wide = jnp.concatenate([coefs[d] for d in range(-REACH, REACH + 1)], axis=1)
            delta = jnp.dot(
                wide, codes[base : base + 5 * frames], preferred_element_type=F32
            ) + jnp.dot(
                pos_after, codes[base + 3 * frames : base + 4 * frames], preferred_element_type=F32
            )
            delta = delta.astype(BF16)
            for part in range(parts):
                step, at = divmod(part * pred_cols, width)
                blocks[part // cores, part % cores, :, :pred_cols] = delta[
                    step * frames : (step + 1) * frames, at : at + pred_cols
                ]
            code_delta = (code_acc[...] + cols_dot(coefs[0], query)).astype(BF16)
            for part in range(parts):
                blocks[part // cores, part % cores, :, pred_cols:] = code_delta[
                    :, part * code_cols : (part + 1) * code_cols
                ]
            loss = jnp.sum(active * (log_total - positive), axis=0, keepdims=True)
            loss_ref[...] = jnp.broadcast_to(loss, loss_ref.shape)
    for back, out in enumerate((out_0, out_1, out_2, out_3)):
        out[...] = blocks[(place + ring - back) % ring]


def term_kernel(
    pred_cols, core_ref, loss_ref, same_0, same_1, same_2, same_3, cross_0, cross_1, cross_2, cross_3,
    rows_same, rows_cross, out_ref, held,
):
    _, frames, lanes_all = same_0.shape
    plane = out_ref.shape[0]
    core, place = core_ref[0, 0], core_ref[0, 1]
    both = ((same_0, same_1, same_2, same_3), (cross_0, cross_1, cross_2, cross_3))
    ring = len(both[0])
    for side, blocks in enumerate(both):
        for spot, block in enumerate(blocks):
            start = pl.multiple_of((place + spot) % ring * frames, frames)
            held[side, pl.ds(start, frames)] = block[core]
    width = rows_same.shape[1] // 2
    rows = 2 * width // ring
    span = rows // plane
    depth = ring * span // 2
    for first, lanes in ((width, slice(0, pred_cols)), (0, slice(pred_cols, lanes_all))):
        for half in range(ring // 2):
            blocks = slice(first + half * rows, first + (half + 1) * rows)
            term = cols_dot(rows_same[:, blocks], held[0, :, lanes])
            term = term + cols_dot(rows_cross[:, blocks], held[1, :, lanes])
            term = term.reshape(2, plane, span // 2, -1)
            term = jnp.concatenate([term[0], term[1]], axis=1).astype(BF16)
            for tile in range(term.shape[2] // 128):
                at = (lanes.start // 128 + tile) * depth + half * span
                out_ref[:, at : at + span] = term[:, :, tile * 128 : (tile + 1) * 128]
    loss = loss_ref[...]
    high = loss.astype(BF16).astype(F32)
    middle = (loss - high).astype(BF16).astype(F32)
    row = lax.broadcasted_iota(jnp.int32, (16, 128), 0)
    terms = jnp.where(row == 0, high, jnp.where(row == 1, middle, loss - high - middle))
    terms = jnp.where(row < 3, terms, 0.0).astype(BF16)
    out_ref[:, out_ref.shape[1] - 16 :] = jnp.broadcast_to(terms[None], (plane, 16, 128))


def sum_kernel(terms_ref, out_ref):
    total = terms_ref[0].astype(F32)
    for source in range(1, terms_ref.shape[0]):
        total = total + terms_ref[source].astype(F32)
    parts, owned = out_ref.shape[0], out_ref.shape[1] // 2
    depth = parts * owned
    loss = jnp.sum(total[total.shape[0] - 16 :, :1], axis=0, keepdims=True)
    for part in range(parts):
        for tile in range(out_ref.shape[2] // 128):
            at = tile * depth + part * owned
            out_ref[part, :owned, tile * 128 : (tile + 1) * 128] = total[at : at + owned]
        out_ref[part, owned:] = jnp.broadcast_to(loss, (owned, out_ref.shape[2]))


def per_device(features, context, predictor, projection, lengths, frame_mask):
    frames, width = features.shape[1], features.shape[2]
    horizons = predictor.shape[1]
    feat, ctx = features[0], context[0]
    windows, recordings = size_of(TM), size_of(DP)
    devices = windows * recordings
    parts, plane = size_of(RING), size_of(PLANE)
    tm = lax.axis_index(TM)
    core = lax.axis_index("core")

    encoded = jnp.dot(feat, projection, preferred_element_type=F32).astype(BF16)
    both = jnp.concatenate([encoded, ctx], axis=0)
    low2, high2 = window_at(both, -2), window_at(both, 2)
    both_x = other_core(both)
    positions = lax.broadcasted_iota(jnp.int32, (1, frames), 1)
    usable = ((frame_mask == 1) & (positions < lengths)).astype(F32)
    usable_x = other_core(usable)
    pair = jnp.concatenate(
        [jnp.where(core == 0, usable, usable_x), jnp.where(core == 0, usable_x, usable)], axis=1
    )
    pair, both_x = lax.optimization_barrier((pair, both_x))
    chips = size_of(CHIPS)
    flags = lax.all_to_all(
        jnp.broadcast_to(pair, (chips, 2 * frames)), CHIPS, 0, 0, tiled=True
    )
    low4, high4 = window_at(encoded, -4), window_at(encoded, 4)
    weights = predictor.reshape(width, horizons * width)
    low2, high2, weights, flags = lax.optimization_barrier((low2, high2, weights, flags))
    low2_x, high2_x = other_core(low2), other_core(high2)
    low4_x, high4_x = other_core(low4), other_core(high4)
    rows_ring = lax.all_gather(jnp.concatenate([feat, ctx], axis=1), "y", tiled=True)

    smem = pl.BlockSpec(memory_space=pltpu.SMEM)
    vmem = pl.BlockSpec(memory_space=pltpu.VMEM)
    anywhere = pl.BlockSpec(memory_space=pl.ANY)
    limit = pltpu.CompilerParams(vmem_limit_bytes=16 * 2**20)

    spot = jnp.stack([lax.axis_index(ALL), tm]).reshape(1, 2).astype(jnp.int32)
    count, near, act, preds = pl.pallas_call(
        functools.partial(prepare_kernel, horizons, windows),
        out_shape=(
            jax.ShapeDtypeStruct((1, 128), F32),
            jax.ShapeDtypeStruct((16, frames), F32),
            jax.ShapeDtypeStruct((horizons * frames, 16), F32),
            jax.ShapeDtypeStruct((3, horizons * frames, width), BF16),
        ),
        in_specs=[smem, vmem, vmem] + [anywhere] * 3,
        out_specs=(vmem, vmem, vmem, vmem),
        scratch_shapes=[pltpu.VMEM((3 * frames, width), BF16), pltpu.SemaphoreType.DMA((3,))],
        compiler_params=limit,
        cost_estimate=pl.CostEstimate(flops=1700000000, bytes_accessed=6500000, transcendentals=0),
    )(spot, flags, weights, low2, ctx, high2)

    pred_cols, code_cols = horizons * width // parts, width // parts
    lanes = pred_cols + code_cols
    core_word = jnp.stack([core, lax.axis_index("y")]).reshape(1, 2).astype(jnp.int32)
    ring = lax.axis_size("y")
    *deltas, loss_part = pl.pallas_call(
        functools.partial(delta_kernel, horizons),
        out_shape=[jax.ShapeDtypeStruct((2, frames, lanes), BF16)] * ring
        + [jax.ShapeDtypeStruct((1, 128), F32)],
        in_specs=[smem] + [vmem] * 5 + [anywhere] * 10,
        out_specs=[vmem] * (ring + 1),
        scratch_shapes=[
            pltpu.VMEM((11 * frames, width), BF16),
            pltpu.VMEM((frames, width), F32),
            pltpu.VMEM((4 * frames, width), BF16),
            pltpu.VMEM((2, horizons * frames, width), BF16),
            pltpu.VMEM((ring, 2, frames, lanes), BF16),
            pltpu.SemaphoreType.DMA((13,)),
        ],
        compiler_params=pltpu.CompilerParams(vmem_limit_bytes=20 * 2**20),
        cost_estimate=pl.CostEstimate(
            flops=4000000000, bytes_accessed=12000000, transcendentals=900000
        ),
    )(
        core_word, count, near, act, preds, weights,
        both, low2, high2, low4, high4, both_x, low2_x, high2_x, low4_x, high4_x,
    )

    _, rows_ring = lax.optimization_barrier((loss_part, rows_ring))
    rows_cross = other_core(rows_ring)
    same = [deltas[0]] + [ring_shift(deltas[step], ("y",), step) for step in range(1, ring)]
    cross = [other_core(block) for block in same]
    terms = pl.pallas_call(
        functools.partial(term_kernel, pred_cols),
        out_shape=jax.ShapeDtypeStruct((plane, width // plane * lanes // 128 + 16, 128), BF16),
        in_specs=[smem] + [vmem] * 11,
        out_specs=vmem,
        scratch_shapes=[pltpu.VMEM((2, ring * frames, lanes), BF16)],
        compiler_params=limit,
        cost_estimate=pl.CostEstimate(flops=1600000000, bytes_accessed=6000000, transcendentals=0),
    )(core_word, loss_part, *same, *cross, rows_ring, rows_cross)

    owned = width // devices
    terms = lax.all_to_all(terms, PLANE, 0, 0, tiled=True)
    sums = pl.pallas_call(
        sum_kernel,
        out_shape=jax.ShapeDtypeStruct((parts, 2 * owned, lanes), F32),
        in_specs=[vmem],
        out_specs=vmem,
    )(terms)
    got = lax.all_to_all(sums, RING, 0, 0, tiled=True)
    loss = jnp.sum(got[:, owned, 0]) * (1.0 / jnp.maximum(count[0, 0], 1.0))
    got = got[:, :owned].transpose(1, 0, 2)
    grad_pred = got[:, :, :pred_cols].reshape(owned, horizons, width)
    grad_proj = got[:, :, pred_cols:].reshape(owned, width)
    return (loss, grad_pred, grad_proj)


def solution(mesh):
    fine = Mesh(mesh.devices.reshape(4, 2, 8, 2, 2), ALL)
    placed = (P(DP, TM, None), P(DP, TM, None), P(), P(), P(DP, TM), P(DP, TM))
    return jax.shard_map(
        per_device,
        mesh=fine,
        in_specs=placed,
        out_specs=(P(), P(ALL, None, None), P(ALL, None)),
        check_vma=False,
    )
```

```python
import functools

import jax
import jax.numpy as jnp
from jax import lax
from jax.experimental import pallas as pl
from jax.experimental.pallas import tpu as pltpu
from jax.sharding import Mesh, PartitionSpec as P

DP = ("y", "xh")
TM = ("z", "xl", "core")
ALL = DP + TM
PLANE = ("xh", "z", "xl")
RING = ("y", "core")
CHIPS = ("y", "xh", "z", "xl")
F32 = jnp.float32
BF16 = jnp.bfloat16
REACH = 2


def size_of(names):
    size = 1
    for name in names:
        size *= lax.axis_size(name)
    return size


def ring_shift(block, axes, offset):
    size = size_of(axes)
    return lax.ppermute(block, axes, [((i + offset) % size, i) for i in range(size)])


def window_at(block, offset):
    return ring_shift(block, TM, offset)


def other_core(block):
    return lax.ppermute(block, "core", [(0, 1), (1, 0)])


def to_bf16_grid(value):
    return lax.reduce_precision(value, 8, 7)


def rows_dot(a, b):
    return lax.dot_general(a, b, (((1,), (1,)), ((), ())), preferred_element_type=F32)


def cols_dot(a, b):
    return lax.dot_general(a, b, (((0,), (0,)), ((), ())), preferred_element_type=F32)


def flags_kernel(
    horizons, windows, spot_ref, flags_ref, start_ref, count_ref, near_ref, act_ref
):
    chips, span = flags_ref.shape
    frames = span // 2
    device, tm = spot_ref[0, 0], spot_ref[0, 1]
    flags = flags_ref[...]
    row = lax.broadcasted_iota(jnp.int32, flags.shape, 0)
    lane = lax.broadcasted_iota(jnp.int32, flags.shape, 1)
    last = row % (windows // 2) == windows // 2 - 1
    following = jnp.where(last, 0.0, pltpu.roll(flags, chips - 1, 0))
    slot = lax.broadcasted_iota(jnp.int32, (chips, 16), 1)
    source = lax.broadcasted_iota(jnp.int32, (chips, 16), 0)

    def picked(values, reach, transposed):
        window = slot - reach
        inside = (tm + window >= 0) & (tm + window < windows)
        out = 0.0
        for half in range(2):
            pick = (2 * source + half == device + window) & inside
            pick = jnp.where(pick, 1.0, 0.0).astype(BF16)
            part = values[:, half * frames : (half + 1) * frames].astype(BF16)
            out = out + (cols_dot(part, pick) if transposed else cols_dot(pick, part))
        return out

    total = jnp.zeros((1, span), F32)
    for h in range(1, horizons + 1):
        ahead = jnp.where(
            lane < span - h, pltpu.roll(flags, span - h, 1), pltpu.roll(following, span - h, 1)
        )
        pairs = flags * ahead
        total = total + jnp.sum(pairs, axis=0, keepdims=True)
        act_ref[(h - 1) * frames : h * frames] = picked(pairs, REACH, True)
    count_ref[...] = start_ref[...] + jnp.sum(total, axis=1, keepdims=True)
    near_ref[...] = picked(flags, 2 * REACH, False)


def stacked_dot(rows, weights, out_ref):
    windows, stacked, width = out_ref.shape
    tile = 512
    frames = stacked * width // weights.shape[1]
    for at in range(0, weights.shape[1], tile):
        part = jnp.dot(rows, weights[:, at : at + tile], preferred_element_type=F32).astype(BF16)
        step, lane = divmod(at, width)
        for w in range(windows):
            out_ref[w, step * frames : (step + 1) * frames, lane : lane + tile] = part[
                w * frames : (w + 1) * frames
            ]


def pred_kernel(low2, ctx, high2, weights, out_ref, done_ref, rows, sems):
    frames = ctx.shape[0]
    copies = [
        pltpu.make_async_copy(block, rows.at[pl.ds(slot * frames, frames)], sems.at[slot])
        for slot, block in enumerate(
            (low2.at[pl.ds(frames, frames)], ctx, high2.at[pl.ds(frames, frames)])
        )
    ]
    for copy in copies:
        copy.start()
    for copy in copies:
        copy.wait()
    stacked_dot(rows[...], weights, out_ref)
    done_ref[...] = jnp.zeros_like(done_ref)


def delta_kernel(
    horizons, core_ref, count_ref, flags_ref, act_ref, preds_ref, weights,
    both, low2, high2, low4, high4, both_x, low2_x, high2_x, low4_x, high4_x,
    out_0, out_1, out_2, out_3, loss_ref, codes, code_acc, odd_ctx, odd_pred, blocks, sems,
):
    frames, width = low4.shape
    scale = width ** (-0.5)
    ring, cores = blocks.shape[:2]
    parts = ring * cores
    pred_cols, code_cols = horizons * width // parts, width // parts
    core, place = core_ref[0, 0], core_ref[0, 1]

    def put(sem, block, start, held, slot):
        at = slot * frames
        if not isinstance(slot, int):
            at = pl.multiple_of(at, frames)
        return pltpu.make_async_copy(
            block.at[pl.ds(start, frames)], held.at[pl.ds(at, frames)], sems.at[sem]
        )

    ctx_copies = [
        put(0, low2_x, frames, odd_ctx, 1 - core),
        put(1, both_x, frames, odd_ctx, 2 - core),
        put(2, high2_x, frames, odd_ctx, 3 - core),
    ]
    code_copies = [
        put(3, low4, 0, codes, 1),
        put(4, low2, 0, codes, 3),
        put(5, both, 0, codes, 5),
        put(6, high2, 0, codes, 7),
        put(7, high4, 0, codes, 9),
        put(8, low4_x, 0, codes, 2 - 2 * core),
        put(9, low2_x, 0, codes, 4 - 2 * core),
        put(10, both_x, 0, codes, 6 - 2 * core),
        put(11, high2_x, 0, codes, 8 - 2 * core),
        put(12, high4_x, 0, codes, 10 - 2 * core),
    ]
    for copy in ctx_copies + code_copies:
        copy.start()
    for copy in ctx_copies:
        copy.wait()
    stacked_dot(odd_ctx[frames : 3 * frames], weights, odd_pred)
    for copy in code_copies:
        copy.wait()
    shape = (horizons * frames, frames)
    row = lax.broadcasted_iota(jnp.int32, shape, 0)
    ahead = row % frames + row // frames + 1
    col = lax.broadcasted_iota(jnp.int32, shape, 1)
    here, after = col == ahead, col == ahead - frames
    preds = {-2: preds_ref[0], -1: odd_pred[0], 0: preds_ref[1], 1: odd_pred[1], 2: preds_ref[2]}
    factor = (1.0 / jnp.maximum(count_ref[:, :1], 1.0)) * scale
    beside = (-2, -1, 1, 2)
    for window in (-2, -1, 1, 2, 0):
        base = (window + 3) * frames
        query = preds[window]
        scores = rows_dot(query, codes[base : base + 5 * frames]) * scale
        block = {
            d: scores[:, (d + 2) * frames : (d + 3) * frames] for d in range(-REACH, REACH + 1)
        }
        positive = jnp.sum(
            jnp.where(here, block[0], 0.0) + jnp.where(after, block[1], 0.0),
            axis=1,
            keepdims=True,
        )
        for d in beside:
            usable = flags_ref[window + d + 4 : window + d + 5, :]
            block[d] = jnp.where(usable > 0, block[d], -1e30)
        top = jnp.maximum(jnp.maximum(block[-2], block[-1]), jnp.maximum(block[1], block[2]))
        top = jnp.maximum(positive, jnp.max(top, axis=1, keepdims=True))
        total = sum(jnp.exp(block[d] - top) for d in beside)
        total = jnp.sum(total, axis=1, keepdims=True)
        log_total = top + jnp.log(jnp.exp(positive - top) + total)
        active = act_ref[:, window + 2 : window + 3]
        weight = factor * active
        pos_coef = weight * (jnp.exp(positive - log_total) - 1.0)
        pos_after = jnp.where(after, pos_coef, 0.0).astype(BF16)
        if window != 0:
            coef = (weight * jnp.exp(block[-window] - log_total)).astype(BF16)
            term = cols_dot(coef, query)
            if window == -1:
                term = term + cols_dot(pos_after, query)
            if window == -2:
                code_acc[...] = term
            else:
                code_acc[...] += term
        else:
            coefs = {d: (weight * jnp.exp(block[d] - log_total)).astype(BF16) for d in beside}
            coefs[0] = jnp.where(here, pos_coef, 0.0).astype(BF16)
            wide = jnp.concatenate([coefs[d] for d in range(-REACH, REACH + 1)], axis=1)
            delta = jnp.dot(
                wide, codes[base : base + 5 * frames], preferred_element_type=F32
            ) + jnp.dot(
                pos_after, codes[base + 3 * frames : base + 4 * frames], preferred_element_type=F32
            )
            delta = delta.astype(BF16)
            for part in range(parts):
                step, at = divmod(part * pred_cols, width)
                blocks[part // cores, part % cores, :, :pred_cols] = delta[
                    step * frames : (step + 1) * frames, at : at + pred_cols
                ]
            code_delta = (code_acc[...] + cols_dot(coefs[0], query)).astype(BF16)
            for part in range(parts):
                blocks[part // cores, part % cores, :, pred_cols:] = code_delta[
                    :, part * code_cols : (part + 1) * code_cols
                ]
            loss = jnp.sum(active * (log_total - positive), axis=0, keepdims=True)
            loss_ref[...] = jnp.broadcast_to(loss, loss_ref.shape)
    copies = [
        pltpu.make_async_copy(blocks.at[(place + ring - back) % ring], out, sems.at[back])
        for back, out in enumerate((out_0, out_1, out_2, out_3))
    ]
    for copy in copies:
        copy.start()
    for copy in copies:
        copy.wait()


def term_kernel(
    pred_cols, core_ref, same_0, same_1, same_2, same_3, cross_0, cross_1, cross_2, cross_3,
    rows_same, rows_cross, out_ref, held,
):
    _, frames, lanes_all = same_0.shape
    plane = out_ref.shape[0]
    core, place = core_ref[0, 0], core_ref[0, 1]
    both = ((same_0, same_1, same_2, same_3), (cross_0, cross_1, cross_2, cross_3))
    ring = len(both[0])
    for side, blocks in enumerate(both):
        for spot, block in enumerate(blocks):
            start = pl.multiple_of((place + spot) % ring * frames, frames)
            held[side, pl.ds(start, frames)] = block[core]
    width = rows_same.shape[1] // 2
    rows = 2 * width // ring
    span = rows // plane
    depth = ring * span // 2
    for first, lanes in ((width, slice(0, pred_cols)), (0, slice(pred_cols, lanes_all))):
        for half in range(ring // 2):
            blocks = slice(first + half * rows, first + (half + 1) * rows)
            term = cols_dot(rows_same[:, blocks], held[0, :, lanes])
            term = term + cols_dot(rows_cross[:, blocks], held[1, :, lanes])
            term = term.reshape(2, plane, span // 2, -1)
            term = jnp.concatenate([term[0], term[1]], axis=1).astype(BF16)
            for tile in range(term.shape[2] // 128):
                at = (lanes.start // 128 + tile) * depth + half * span
                out_ref[:, at : at + span] = term[:, :, tile * 128 : (tile + 1) * 128]


def sum_kernel(terms_ref, loss_ref, out_ref):
    total = terms_ref[0].astype(F32)
    for source in range(1, terms_ref.shape[0]):
        total = total + terms_ref[source].astype(F32)
    parts, owned = out_ref.shape[0], out_ref.shape[1] // 2
    depth = parts * owned
    loss = jnp.sum(loss_ref[:, :, :1].astype(F32), axis=(0, 1)).reshape(1, 1)
    for part in range(parts):
        for tile in range(out_ref.shape[2] // 128):
            at = tile * depth + part * owned
            out_ref[part, :owned, tile * 128 : (tile + 1) * 128] = total[at : at + owned]
        out_ref[part, owned:] = jnp.broadcast_to(loss, (owned, out_ref.shape[2]))


def per_device(features, context, predictor, projection, lengths, frame_mask):
    frames, width = features.shape[1], features.shape[2]
    horizons = predictor.shape[1]
    feat, ctx = features[0], context[0]
    windows, recordings = size_of(TM), size_of(DP)
    devices = windows * recordings
    parts, plane = size_of(RING), size_of(PLANE)
    tm = lax.axis_index(TM)
    core = lax.axis_index("core")

    encoded = jnp.dot(feat, projection, preferred_element_type=F32).astype(BF16)
    both = jnp.concatenate([encoded, ctx], axis=0)
    low2, high2 = window_at(both, -2), window_at(both, 2)
    both_x = other_core(both)
    positions = lax.broadcasted_iota(jnp.int32, (1, frames), 1)
    usable = ((frame_mask == 1) & (positions < lengths)).astype(F32)
    usable_x = other_core(usable)
    pair = jnp.concatenate(
        [jnp.where(core == 0, usable, usable_x), jnp.where(core == 0, usable_x, usable)], axis=1
    )
    pair, both_x = lax.optimization_barrier((pair, both_x))
    later, _ = lax.optimization_barrier((feat, usable_x))
    rows_ring = lax.all_gather(jnp.concatenate([later, ctx], axis=1), "y", tiled=True)
    chips = size_of(CHIPS)
    flags = lax.all_to_all(
        jnp.broadcast_to(pair, (chips, 2 * frames)), CHIPS, 0, 0, tiled=True
    )
    low4, high4 = window_at(encoded, -4), window_at(encoded, 4)
    weights = predictor.reshape(width, horizons * width)
    smem = pl.BlockSpec(memory_space=pltpu.SMEM)
    vmem = pl.BlockSpec(memory_space=pltpu.VMEM)
    anywhere = pl.BlockSpec(memory_space=pl.ANY)
    limit = pltpu.CompilerParams(vmem_limit_bytes=16 * 2**20)

    preds, done = pl.pallas_call(
        pred_kernel,
        out_shape=(
            jax.ShapeDtypeStruct((3, horizons * frames, width), BF16),
            jax.ShapeDtypeStruct((1, 128), F32),
        ),
        in_specs=[anywhere] * 3 + [vmem],
        out_specs=(vmem, vmem),
        scratch_shapes=[pltpu.VMEM((3 * frames, width), BF16), pltpu.SemaphoreType.DMA((3,))],
        compiler_params=limit,
        cost_estimate=pl.CostEstimate(flops=1600000000, bytes_accessed=6500000, transcendentals=0),
    )(low2, ctx, high2, weights)
    late_low2, late_high2, flags, done = lax.optimization_barrier((low2, high2, flags, done))
    low2_x, high2_x = other_core(late_low2), other_core(late_high2)
    low4_x, high4_x = other_core(low4), other_core(high4)
    spot = jnp.stack([lax.axis_index(ALL), tm]).reshape(1, 2).astype(jnp.int32)
    count, near, act = pl.pallas_call(
        functools.partial(flags_kernel, horizons, windows),
        out_shape=(
            jax.ShapeDtypeStruct((1, 128), F32),
            jax.ShapeDtypeStruct((16, frames), F32),
            jax.ShapeDtypeStruct((horizons * frames, 16), F32),
        ),
        in_specs=[smem, vmem, vmem],
        out_specs=(vmem, vmem, vmem),
    )(spot, flags, done)

    pred_cols, code_cols = horizons * width // parts, width // parts
    lanes = pred_cols + code_cols
    core_word = jnp.stack([core, lax.axis_index("y")]).reshape(1, 2).astype(jnp.int32)
    ring = lax.axis_size("y")
    *deltas, loss_part = pl.pallas_call(
        functools.partial(delta_kernel, horizons),
        out_shape=[jax.ShapeDtypeStruct((2, frames, lanes), BF16)] * ring
        + [jax.ShapeDtypeStruct((1, 128), F32)],
        in_specs=[smem] + [vmem] * 5 + [anywhere] * 10,
        out_specs=[anywhere] * ring + [vmem],
        scratch_shapes=[
            pltpu.VMEM((11 * frames, width), BF16),
            pltpu.VMEM((frames, width), F32),
            pltpu.VMEM((4 * frames, width), BF16),
            pltpu.VMEM((2, horizons * frames, width), BF16),
            pltpu.VMEM((ring, 2, frames, lanes), BF16),
            pltpu.SemaphoreType.DMA((13,)),
        ],
        compiler_params=pltpu.CompilerParams(vmem_limit_bytes=20 * 2**20),
        cost_estimate=pl.CostEstimate(
            flops=4000000000, bytes_accessed=12000000, transcendentals=900000
        ),
    )(
        core_word, count, near, act, preds, weights,
        both, low2, high2, low4, high4, both_x, low2_x, high2_x, low4_x, high4_x,
    )

    _, later = lax.optimization_barrier((loss_part, rows_ring))
    rows_cross = other_core(later)
    same = [deltas[0]] + [ring_shift(deltas[step], ("y",), step) for step in range(1, ring)]
    loss_part = lax.all_to_all(
        jnp.broadcast_to(loss_part, (lax.axis_size("z"), 128)), "z", 0, 0, tiled=True
    )
    *same[1:], loss_part = lax.optimization_barrier((*same[1:], loss_part))
    cross = [other_core(block) for block in same]
    terms = pl.pallas_call(
        functools.partial(term_kernel, pred_cols),
        out_shape=jax.ShapeDtypeStruct((plane, width // plane * lanes // 128, 128), BF16),
        in_specs=[smem] + [vmem] * 10,
        out_specs=vmem,
        scratch_shapes=[pltpu.VMEM((2, ring * frames, lanes), BF16)],
        compiler_params=limit,
        cost_estimate=pl.CostEstimate(flops=1600000000, bytes_accessed=6000000, transcendentals=0),
    )(core_word, *same, *cross, rows_ring, rows_cross)

    owned = width // devices
    loss_part = jnp.sum(loss_part, axis=0, keepdims=True)
    _, loss_part = lax.optimization_barrier((terms, loss_part))
    terms = lax.all_to_all(terms, PLANE, 0, 0, tiled=True)
    high = to_bf16_grid(loss_part)
    middle = to_bf16_grid(loss_part - high)
    loss_part = jnp.concatenate([high, middle, loss_part - high - middle], axis=0).astype(BF16)
    loss_plane = lax.all_gather(loss_part, ("xh", "xl"))
    sums = pl.pallas_call(
        sum_kernel,
        out_shape=jax.ShapeDtypeStruct((parts, 2 * owned, lanes), F32),
        in_specs=[vmem, vmem],
        out_specs=vmem,
    )(terms, loss_plane)
    got = lax.all_to_all(sums, RING, 0, 0, tiled=True)
    loss = jnp.sum(got[:, owned, 0]) * (1.0 / jnp.maximum(count[0, 0], 1.0))
    got = got[:, :owned].transpose(1, 0, 2)
    grad_pred = got[:, :, :pred_cols].reshape(owned, horizons, width)
    grad_proj = got[:, :, pred_cols:].reshape(owned, width)
    return (loss, grad_pred, grad_proj)


def solution(mesh):
    fine = Mesh(mesh.devices.reshape(4, 2, 8, 2, 2), ALL)
    placed = (P(DP, TM, None), P(DP, TM, None), P(), P(), P(DP, TM), P(DP, TM))
    return jax.shard_map(
        per_device,
        mesh=fine,
        in_specs=placed,
        out_specs=(P(), P(ALL, None, None), P(ALL, None)),
        check_vma=False,
    )
```

```python
import functools

import jax
import jax.numpy as jnp
from jax import lax
from jax.experimental import pallas as pl
from jax.experimental.pallas import tpu as pltpu
from jax.sharding import Mesh, PartitionSpec as P

DP = ("y", "xh")
TM = ("z", "xl", "core")
ALL = DP + TM
PLANE = ("xh", "z", "xl")
RING = ("y", "core")
CHIPS = ("y", "xh", "z", "xl")
F32 = jnp.float32
BF16 = jnp.bfloat16
REACH = 2


def size_of(names):
    size = 1
    for name in names:
        size *= lax.axis_size(name)
    return size


def ring_shift(block, axes, offset):
    size = size_of(axes)
    return lax.ppermute(block, axes, [((i + offset) % size, i) for i in range(size)])


def window_at(block, offset):
    return ring_shift(block, TM, offset)


def other_core(block):
    return lax.ppermute(block, "core", [(0, 1), (1, 0)])


def rows_dot(a, b):
    return lax.dot_general(a, b, (((1,), (1,)), ((), ())), preferred_element_type=F32)


def cols_dot(a, b):
    return lax.dot_general(a, b, (((0,), (0,)), ((), ())), preferred_element_type=F32)


def prepare_kernel(
    horizons, windows, spot_ref, flags_ref, weights, low2, ctx, high2, count_ref, near_ref, act_ref,
    preds_ref, rows, sems,
):
    chips, span = flags_ref.shape
    frames = span // 2
    copies = [
        pltpu.make_async_copy(block, rows.at[pl.ds(slot * frames, frames)], sems.at[slot])
        for slot, block in enumerate(
            (low2.at[pl.ds(frames, frames)], ctx, high2.at[pl.ds(frames, frames)])
        )
    ]
    for copy in copies:
        copy.start()
    device, tm = spot_ref[0, 0], spot_ref[0, 1]
    flags = flags_ref[...]
    row = lax.broadcasted_iota(jnp.int32, flags.shape, 0)
    lane = lax.broadcasted_iota(jnp.int32, flags.shape, 1)
    last = row % (windows // 2) == windows // 2 - 1
    following = jnp.where(last, 0.0, pltpu.roll(flags, chips - 1, 0))
    slot = lax.broadcasted_iota(jnp.int32, (chips, 16), 1)
    source = lax.broadcasted_iota(jnp.int32, (chips, 16), 0)

    def picked(values, reach, transposed):
        window = slot - reach
        inside = (tm + window >= 0) & (tm + window < windows)
        out = 0.0
        for half in range(2):
            pick = (2 * source + half == device + window) & inside
            pick = jnp.where(pick, 1.0, 0.0).astype(BF16)
            part = values[:, half * frames : (half + 1) * frames].astype(BF16)
            out = out + (cols_dot(part, pick) if transposed else cols_dot(pick, part))
        return out

    total = jnp.zeros((1, span), F32)
    for h in range(1, horizons + 1):
        ahead = jnp.where(
            lane < span - h, pltpu.roll(flags, span - h, 1), pltpu.roll(following, span - h, 1)
        )
        pairs = flags * ahead
        total = total + jnp.sum(pairs, axis=0, keepdims=True)
        act_ref[(h - 1) * frames : h * frames] = picked(pairs, REACH, True)
    count_ref[...] = jnp.broadcast_to(jnp.sum(total, axis=1, keepdims=True), count_ref.shape)
    near_ref[...] = picked(flags, 2 * REACH, False)
    for copy in copies:
        copy.wait()
    stacked_dot(rows[...], weights, preds_ref)


def stacked_dot(rows, weights, out_ref):
    windows, stacked, width = out_ref.shape
    tile = 512
    frames = stacked * width // weights.shape[1]
    for at in range(0, weights.shape[1], tile):
        part = jnp.dot(rows, weights[:, at : at + tile], preferred_element_type=F32).astype(BF16)
        step, lane = divmod(at, width)
        for w in range(windows):
            out_ref[w, step * frames : (step + 1) * frames, lane : lane + tile] = part[
                w * frames : (w + 1) * frames
            ]


def delta_kernel(
    horizons, core_ref, count_ref, flags_ref, act_ref, preds_ref, weights,
    both, low2, high2, low4, high4, both_x, low2_x, high2_x, low4_x, high4_x,
    out_0, out_1, out_2, out_3, loss_ref, codes, code_acc, odd_ctx, odd_pred, blocks, sems,
):
    frames, width = low4.shape
    scale = width ** (-0.5)
    ring, cores = blocks.shape[:2]
    parts = ring * cores
    pred_cols, code_cols = horizons * width // parts, width // parts
    core, place = core_ref[0, 0], core_ref[0, 1]

    def put(sem, block, start, held, slot):
        at = slot * frames
        if not isinstance(slot, int):
            at = pl.multiple_of(at, frames)
        return pltpu.make_async_copy(
            block.at[pl.ds(start, frames)], held.at[pl.ds(at, frames)], sems.at[sem]
        )

    ctx_copies = [
        put(0, low2_x, frames, odd_ctx, 1 - core),
        put(1, both_x, frames, odd_ctx, 2 - core),
        put(2, high2_x, frames, odd_ctx, 3 - core),
    ]
    code_copies = [
        put(3, low4, 0, codes, 1),
        put(4, low2, 0, codes, 3),
        put(5, both, 0, codes, 5),
        put(6, high2, 0, codes, 7),
        put(7, high4, 0, codes, 9),
        put(8, low4_x, 0, codes, 2 - 2 * core),
        put(9, low2_x, 0, codes, 4 - 2 * core),
        put(10, both_x, 0, codes, 6 - 2 * core),
        put(11, high2_x, 0, codes, 8 - 2 * core),
        put(12, high4_x, 0, codes, 10 - 2 * core),
    ]
    for copy in ctx_copies + code_copies:
        copy.start()
    for copy in ctx_copies:
        copy.wait()
    stacked_dot(odd_ctx[frames : 3 * frames], weights, odd_pred)
    for copy in code_copies:
        copy.wait()
    shape = (horizons * frames, frames)
    row = lax.broadcasted_iota(jnp.int32, shape, 0)
    ahead = row % frames + row // frames + 1
    col = lax.broadcasted_iota(jnp.int32, shape, 1)
    here, after = col == ahead, col == ahead - frames
    preds = {-2: preds_ref[0], -1: odd_pred[0], 0: preds_ref[1], 1: odd_pred[1], 2: preds_ref[2]}
    factor = (1.0 / jnp.maximum(count_ref[:, :1], 1.0)) * scale
    beside = (-2, -1, 1, 2)
    for window in (-2, -1, 1, 2, 0):
        base = (window + 3) * frames
        query = preds[window]
        scores = rows_dot(query, codes[base : base + 5 * frames]) * scale
        block = {
            d: scores[:, (d + 2) * frames : (d + 3) * frames] for d in range(-REACH, REACH + 1)
        }
        positive = jnp.sum(
            jnp.where(here, block[0], 0.0) + jnp.where(after, block[1], 0.0),
            axis=1,
            keepdims=True,
        )
        for d in beside:
            usable = flags_ref[window + d + 4 : window + d + 5, :]
            block[d] = jnp.where(usable > 0, block[d], -1e30)
        top = jnp.maximum(jnp.maximum(block[-2], block[-1]), jnp.maximum(block[1], block[2]))
        top = jnp.maximum(positive, jnp.max(top, axis=1, keepdims=True))
        total = sum(jnp.exp(block[d] - top) for d in beside)
        total = jnp.sum(total, axis=1, keepdims=True)
        log_total = top + jnp.log(jnp.exp(positive - top) + total)
        active = act_ref[:, window + 2 : window + 3]
        weight = factor * active
        pos_coef = weight * (jnp.exp(positive - log_total) - 1.0)
        pos_after = jnp.where(after, pos_coef, 0.0).astype(BF16)
        if window != 0:
            coef = (weight * jnp.exp(block[-window] - log_total)).astype(BF16)
            term = cols_dot(coef, query)
            if window == -1:
                term = term + cols_dot(pos_after, query)
            if window == -2:
                code_acc[...] = term
            else:
                code_acc[...] += term
        else:
            coefs = {d: (weight * jnp.exp(block[d] - log_total)).astype(BF16) for d in beside}
            coefs[0] = jnp.where(here, pos_coef, 0.0).astype(BF16)
            wide = jnp.concatenate([coefs[d] for d in range(-REACH, REACH + 1)], axis=1)
            delta = jnp.dot(
                wide, codes[base : base + 5 * frames], preferred_element_type=F32
            ) + jnp.dot(
                pos_after, codes[base + 3 * frames : base + 4 * frames], preferred_element_type=F32
            )
            delta = delta.astype(BF16)
            for part in range(parts):
                step, at = divmod(part * pred_cols, width)
                blocks[part // cores, part % cores, :, :pred_cols] = delta[
                    step * frames : (step + 1) * frames, at : at + pred_cols
                ]
            code_delta = (code_acc[...] + cols_dot(coefs[0], query)).astype(BF16)
            for part in range(parts):
                blocks[part // cores, part % cores, :, pred_cols:] = code_delta[
                    :, part * code_cols : (part + 1) * code_cols
                ]
            loss = jnp.sum(active * (log_total - positive), axis=0, keepdims=True)
            loss_ref[...] = jnp.broadcast_to(loss, loss_ref.shape)
    for back, out in enumerate((out_0, out_1, out_2, out_3)):
        out[...] = blocks[(place + ring - back) % ring]


def term_kernel(
    pred_cols, core_ref, loss_ref, same_0, same_1, same_2, same_3, cross_0, cross_1, cross_2, cross_3,
    rows_same, rows_cross, out_ref, held,
):
    _, frames, lanes_all = same_0.shape
    plane = out_ref.shape[0]
    core, place = core_ref[0, 0], core_ref[0, 1]
    both = ((same_0, same_1, same_2, same_3), (cross_0, cross_1, cross_2, cross_3))
    ring = len(both[0])
    for side, blocks in enumerate(both):
        for spot, block in enumerate(blocks):
            start = pl.multiple_of((place + spot) % ring * frames, frames)
            held[side, pl.ds(start, frames)] = block[core]
    width = rows_same.shape[1] // 2
    rows = 2 * width // ring
    span = rows // plane
    depth = ring * span // 2
    for first, lanes in ((width, slice(0, pred_cols)), (0, slice(pred_cols, lanes_all))):
        for half in range(ring // 2):
            blocks = slice(first + half * rows, first + (half + 1) * rows)
            term = cols_dot(rows_same[:, blocks], held[0, :, lanes])
            term = term + cols_dot(rows_cross[:, blocks], held[1, :, lanes])
            term = term.reshape(2, plane, span // 2, -1)
            term = jnp.concatenate([term[0], term[1]], axis=1).astype(BF16)
            for tile in range(term.shape[2] // 128):
                at = (lanes.start // 128 + tile) * depth + half * span
                out_ref[:, at : at + span] = term[:, :, tile * 128 : (tile + 1) * 128]
    loss = loss_ref[...]
    high = loss.astype(BF16).astype(F32)
    middle = (loss - high).astype(BF16).astype(F32)
    row = lax.broadcasted_iota(jnp.int32, (16, 128), 0)
    terms = jnp.where(row == 0, high, jnp.where(row == 1, middle, loss - high - middle))
    terms = jnp.where(row < 3, terms, 0.0).astype(BF16)
    out_ref[:, out_ref.shape[1] - 16 :] = jnp.broadcast_to(terms[None], (plane, 16, 128))


def sum_kernel(core_ref, terms_ref, out_0, out_1, out_2, out_3, blocks):
    total = terms_ref[0].astype(F32)
    for source in range(1, terms_ref.shape[0]):
        total = total + terms_ref[source].astype(F32)
    place = core_ref[0, 1]
    ring, cores, rows, lanes = blocks.shape
    owned = rows // 2
    depth = ring * cores * owned
    loss = jnp.sum(total[total.shape[0] - 16 :, :1], axis=0, keepdims=True)
    for part in range(ring * cores):
        for tile in range(lanes // 128):
            at = tile * depth + part * owned
            blocks[part // cores, part % cores, :owned, tile * 128 : (tile + 1) * 128] = total[
                at : at + owned
            ]
        blocks[part // cores, part % cores, owned:] = jnp.broadcast_to(loss, (owned, lanes))
    for back, out in enumerate((out_0, out_1, out_2, out_3)):
        out[...] = blocks[(place + ring - back) % ring]


def gather_kernel(
    core_ref, count_ref, same_0, same_1, same_2, same_3, cross_0, cross_1, cross_2, cross_3,
    loss_ref, pred_ref, proj_ref, held,
):
    core, place = core_ref[0, 0], core_ref[0, 1]
    both = ((same_0, same_1, same_2, same_3), (cross_0, cross_1, cross_2, cross_3))
    ring = len(both[0])
    for side, blocks in enumerate(both):
        for spot, block in enumerate(blocks):
            source = 2 * ((place + spot) % ring) + (core if side == 0 else 1 - core)
            held[source] = block[core]
    parts, rows, lanes = held.shape
    owned, horizons, width = pred_ref.shape
    code_cols = width // parts
    pred_cols = lanes - code_cols
    loss = jnp.zeros((1, 1), F32)
    for part in range(parts):
        block = held[part]
        step, at = divmod(part * pred_cols, width)
        pred_ref[:, step, at : at + pred_cols] = block[:owned, :pred_cols]
        proj_ref[:, part * code_cols : (part + 1) * code_cols] = block[:owned, pred_cols:]
        loss = loss + block[owned : owned + 1, :1]
    loss_ref[...] = loss * (1.0 / jnp.maximum(count_ref[:, :1], 1.0))


def per_device(features, context, predictor, projection, lengths, frame_mask):
    frames, width = features.shape[1], features.shape[2]
    horizons = predictor.shape[1]
    feat, ctx = features[0], context[0]
    windows, recordings = size_of(TM), size_of(DP)
    devices = windows * recordings
    parts, plane = size_of(RING), size_of(PLANE)
    tm = lax.axis_index(TM)
    core = lax.axis_index("core")

    encoded = jnp.dot(feat, projection, preferred_element_type=F32).astype(BF16)
    both = jnp.concatenate([encoded, ctx], axis=0)
    low2, high2 = window_at(both, -2), window_at(both, 2)
    both_x = other_core(both)
    positions = lax.broadcasted_iota(jnp.int32, (1, frames), 1)
    usable = ((frame_mask == 1) & (positions < lengths)).astype(F32)
    usable_x = other_core(usable)
    pair = jnp.concatenate(
        [jnp.where(core == 0, usable, usable_x), jnp.where(core == 0, usable_x, usable)], axis=1
    )
    pair, both_x = lax.optimization_barrier((pair, both_x))
    chips = size_of(CHIPS)
    flags = lax.all_to_all(
        jnp.broadcast_to(pair, (chips, 2 * frames)), CHIPS, 0, 0, tiled=True
    )
    low4, high4 = window_at(encoded, -4), window_at(encoded, 4)
    weights = predictor.reshape(width, horizons * width)
    low2, high2, weights, flags = lax.optimization_barrier((low2, high2, weights, flags))
    low2_x, high2_x = other_core(low2), other_core(high2)
    low4_x, high4_x = other_core(low4), other_core(high4)
    rows_ring = lax.all_gather(jnp.concatenate([feat, ctx], axis=1), "y", tiled=True)

    smem = pl.BlockSpec(memory_space=pltpu.SMEM)
    vmem = pl.BlockSpec(memory_space=pltpu.VMEM)
    anywhere = pl.BlockSpec(memory_space=pl.ANY)
    limit = pltpu.CompilerParams(vmem_limit_bytes=16 * 2**20)

    spot = jnp.stack([lax.axis_index(ALL), tm]).reshape(1, 2).astype(jnp.int32)
    count, near, act, preds = pl.pallas_call(
        functools.partial(prepare_kernel, horizons, windows),
        out_shape=(
            jax.ShapeDtypeStruct((1, 128), F32),
            jax.ShapeDtypeStruct((16, frames), F32),
            jax.ShapeDtypeStruct((horizons * frames, 16), F32),
            jax.ShapeDtypeStruct((3, horizons * frames, width), BF16),
        ),
        in_specs=[smem, vmem, vmem] + [anywhere] * 3,
        out_specs=(vmem, vmem, vmem, vmem),
        scratch_shapes=[pltpu.VMEM((3 * frames, width), BF16), pltpu.SemaphoreType.DMA((3,))],
        compiler_params=limit,
        cost_estimate=pl.CostEstimate(flops=1700000000, bytes_accessed=6500000, transcendentals=0),
    )(spot, flags, weights, low2, ctx, high2)

    pred_cols, code_cols = horizons * width // parts, width // parts
    lanes = pred_cols + code_cols
    core_word = jnp.stack([core, lax.axis_index("y")]).reshape(1, 2).astype(jnp.int32)
    ring = lax.axis_size("y")
    *deltas, loss_part = pl.pallas_call(
        functools.partial(delta_kernel, horizons),
        out_shape=[jax.ShapeDtypeStruct((2, frames, lanes), BF16)] * ring
        + [jax.ShapeDtypeStruct((1, 128), F32)],
        in_specs=[smem] + [vmem] * 5 + [anywhere] * 10,
        out_specs=[vmem] * (ring + 1),
        scratch_shapes=[
            pltpu.VMEM((11 * frames, width), BF16),
            pltpu.VMEM((frames, width), F32),
            pltpu.VMEM((4 * frames, width), BF16),
            pltpu.VMEM((2, horizons * frames, width), BF16),
            pltpu.VMEM((ring, 2, frames, lanes), BF16),
            pltpu.SemaphoreType.DMA((13,)),
        ],
        compiler_params=pltpu.CompilerParams(vmem_limit_bytes=20 * 2**20),
        cost_estimate=pl.CostEstimate(
            flops=4000000000, bytes_accessed=12000000, transcendentals=900000
        ),
    )(
        core_word, count, near, act, preds, weights,
        both, low2, high2, low4, high4, both_x, low2_x, high2_x, low4_x, high4_x,
    )

    _, rows_ring = lax.optimization_barrier((loss_part, rows_ring))
    rows_cross = other_core(rows_ring)
    same = [deltas[0]] + [ring_shift(deltas[step], ("y",), step) for step in range(1, ring)]
    cross = [other_core(block) for block in same]
    terms = pl.pallas_call(
        functools.partial(term_kernel, pred_cols),
        out_shape=jax.ShapeDtypeStruct((plane, width // plane * lanes // 128 + 16, 128), BF16),
        in_specs=[smem] + [vmem] * 11,
        out_specs=vmem,
        scratch_shapes=[pltpu.VMEM((2, ring * frames, lanes), BF16)],
        compiler_params=limit,
        cost_estimate=pl.CostEstimate(flops=1600000000, bytes_accessed=6000000, transcendentals=0),
    )(core_word, loss_part, *same, *cross, rows_ring, rows_cross)

    owned = width // devices
    terms = lax.all_to_all(terms, PLANE, 0, 0, tiled=True)
    block = jax.ShapeDtypeStruct((2, 2 * owned, lanes), F32)
    sums = pl.pallas_call(
        sum_kernel,
        out_shape=[block] * ring,
        in_specs=[smem, vmem],
        out_specs=[vmem] * ring,
        scratch_shapes=[pltpu.VMEM((ring, 2, 2 * owned, lanes), F32)],
    )(core_word, terms)
    same = [sums[0]] + [ring_shift(sums[step], ("y",), step) for step in range(1, ring)]
    cross = [other_core(block) for block in same]
    loss, grad_pred, grad_proj = pl.pallas_call(
        gather_kernel,
        out_shape=(
            jax.ShapeDtypeStruct((1, 1), F32),
            jax.ShapeDtypeStruct((owned, horizons, width), F32),
            jax.ShapeDtypeStruct((owned, width), F32),
        ),
        in_specs=[smem] + [vmem] * 9,
        out_specs=(vmem, vmem, vmem),
        scratch_shapes=[pltpu.VMEM((parts, 2 * owned, lanes), F32)],
    )(core_word, count, *same, *cross)
    return (loss.reshape(()), grad_pred, grad_proj)


def solution(mesh):
    fine = Mesh(mesh.devices.reshape(4, 2, 8, 2, 2), ALL)
    placed = (P(DP, TM, None), P(DP, TM, None), P(), P(), P(DP, TM), P(DP, TM))
    return jax.shard_map(
        per_device,
        mesh=fine,
        in_specs=placed,
        out_specs=(P(), P(ALL, None, None), P(ALL, None)),
        check_vma=False,
    )
```

```python
import functools

import jax
import jax.numpy as jnp
from jax import lax
from jax.experimental import pallas as pl
from jax.experimental.pallas import tpu as pltpu
from jax.sharding import Mesh, PartitionSpec as P

DP = ("y", "xh")
TM = ("z", "xl", "core")
ALL = DP + TM
PLANE = ("xh", "z", "xl")
RING = ("y", "core")
CHIPS = ("y", "xh", "z", "xl")
F32 = jnp.float32
BF16 = jnp.bfloat16
REACH = 2


def size_of(names):
    size = 1
    for name in names:
        size *= lax.axis_size(name)
    return size


def ring_shift(block, axes, offset):
    size = size_of(axes)
    return lax.ppermute(block, axes, [((i + offset) % size, i) for i in range(size)])


def window_at(block, offset):
    return ring_shift(block, TM, offset)


def other_core(block):
    return lax.ppermute(block, "core", [(0, 1), (1, 0)])


def rows_dot(a, b):
    return lax.dot_general(a, b, (((1,), (1,)), ((), ())), preferred_element_type=F32)


def cols_dot(a, b):
    return lax.dot_general(a, b, (((0,), (0,)), ((), ())), preferred_element_type=F32)


def token_kernel(_, out_ref):
    out_ref[...] = jnp.zeros_like(out_ref)


def prepare_kernel(
    horizons, windows, spot_ref, flags_ref, start_ref, weights, low2, ctx, high2, count_ref, near_ref, act_ref,
    preds_ref, rows, sems,
):
    chips, span = flags_ref.shape
    frames = span // 2
    copies = [
        pltpu.make_async_copy(block, rows.at[pl.ds(slot * frames, frames)], sems.at[slot])
        for slot, block in enumerate(
            (low2.at[pl.ds(frames, frames)], ctx, high2.at[pl.ds(frames, frames)])
        )
    ]
    for copy in copies:
        copy.start()
    device, tm = spot_ref[0, 0], spot_ref[0, 1]
    flags = flags_ref[...]
    row = lax.broadcasted_iota(jnp.int32, flags.shape, 0)
    lane = lax.broadcasted_iota(jnp.int32, flags.shape, 1)
    last = row % (windows // 2) == windows // 2 - 1
    following = jnp.where(last, 0.0, pltpu.roll(flags, chips - 1, 0))
    slot = lax.broadcasted_iota(jnp.int32, (chips, 16), 1)
    source = lax.broadcasted_iota(jnp.int32, (chips, 16), 0)

    def picked(values, reach, transposed):
        window = slot - reach
        inside = (tm + window >= 0) & (tm + window < windows)
        out = 0.0
        for half in range(2):
            pick = (2 * source + half == device + window) & inside
            pick = jnp.where(pick, 1.0, 0.0).astype(BF16)
            part = values[:, half * frames : (half + 1) * frames].astype(BF16)
            out = out + (cols_dot(part, pick) if transposed else cols_dot(pick, part))
        return out

    total = jnp.zeros((1, span), F32)
    for h in range(1, horizons + 1):
        ahead = jnp.where(
            lane < span - h, pltpu.roll(flags, span - h, 1), pltpu.roll(following, span - h, 1)
        )
        pairs = flags * ahead
        total = total + jnp.sum(pairs, axis=0, keepdims=True)
        act_ref[(h - 1) * frames : h * frames] = picked(pairs, REACH, True)
    count_ref[...] = start_ref[...] + jnp.sum(total, axis=1, keepdims=True)
    near_ref[...] = picked(flags, 2 * REACH, False)
    for copy in copies:
        copy.wait()
    stacked_dot(rows[...], weights, preds_ref)


def stacked_dot(rows, weights, out_ref):
    windows, stacked, width = out_ref.shape
    tile = 512
    frames = stacked * width // weights.shape[1]
    for at in range(0, weights.shape[1], tile):
        part = jnp.dot(rows, weights[:, at : at + tile], preferred_element_type=F32).astype(BF16)
        step, lane = divmod(at, width)
        for w in range(windows):
            out_ref[w, step * frames : (step + 1) * frames, lane : lane + tile] = part[
                w * frames : (w + 1) * frames
            ]


def delta_kernel(
    horizons, core_ref, count_ref, flags_ref, act_ref, preds_ref, weights,
    both, low2, high2, low4, high4, both_x, low2_x, high2_x, low4_x, high4_x,
    out_0, out_1, out_2, out_3, loss_ref, codes, code_acc, odd_ctx, odd_pred, blocks, sems,
):
    frames, width = low4.shape
    scale = width ** (-0.5)
    ring, cores = blocks.shape[:2]
    parts = ring * cores
    pred_cols, code_cols = horizons * width // parts, width // parts
    core, place = core_ref[0, 0], core_ref[0, 1]

    def put(sem, block, start, held, slot):
        at = slot * frames
        if not isinstance(slot, int):
            at = pl.multiple_of(at, frames)
        return pltpu.make_async_copy(
            block.at[pl.ds(start, frames)], held.at[pl.ds(at, frames)], sems.at[sem]
        )

    ctx_copies = [
        put(0, low2_x, frames, odd_ctx, 1 - core),
        put(1, both_x, frames, odd_ctx, 2 - core),
        put(2, high2_x, frames, odd_ctx, 3 - core),
    ]
    code_copies = [
        put(3, low4, 0, codes, 1),
        put(4, low2, 0, codes, 3),
        put(5, both, 0, codes, 5),
        put(6, high2, 0, codes, 7),
        put(7, high4, 0, codes, 9),
        put(8, low4_x, 0, codes, 2 - 2 * core),
        put(9, low2_x, 0, codes, 4 - 2 * core),
        put(10, both_x, 0, codes, 6 - 2 * core),
        put(11, high2_x, 0, codes, 8 - 2 * core),
        put(12, high4_x, 0, codes, 10 - 2 * core),
    ]
    for copy in ctx_copies + code_copies:
        copy.start()
    for copy in ctx_copies:
        copy.wait()
    stacked_dot(odd_ctx[frames : 3 * frames], weights, odd_pred)
    for copy in code_copies:
        copy.wait()
    shape = (horizons * frames, frames)
    row = lax.broadcasted_iota(jnp.int32, shape, 0)
    ahead = row % frames + row // frames + 1
    col = lax.broadcasted_iota(jnp.int32, shape, 1)
    here, after = col == ahead, col == ahead - frames
    preds = {-2: preds_ref[0], -1: odd_pred[0], 0: preds_ref[1], 1: odd_pred[1], 2: preds_ref[2]}
    factor = (1.0 / jnp.maximum(count_ref[:, :1], 1.0)) * scale
    beside = (-2, -1, 1, 2)
    for window in (-2, -1, 1, 2, 0):
        base = (window + 3) * frames
        query = preds[window]
        scores = rows_dot(query, codes[base : base + 5 * frames]) * scale
        block = {
            d: scores[:, (d + 2) * frames : (d + 3) * frames] for d in range(-REACH, REACH + 1)
        }
        positive = jnp.sum(
            jnp.where(here, block[0], 0.0) + jnp.where(after, block[1], 0.0),
            axis=1,
            keepdims=True,
        )
        for d in beside:
            usable = flags_ref[window + d + 4 : window + d + 5, :]
            block[d] = jnp.where(usable > 0, block[d], -1e30)
        top = jnp.maximum(jnp.maximum(block[-2], block[-1]), jnp.maximum(block[1], block[2]))
        top = jnp.maximum(positive, jnp.max(top, axis=1, keepdims=True))
        total = sum(jnp.exp(block[d] - top) for d in beside)
        total = jnp.sum(total, axis=1, keepdims=True)
        log_total = top + jnp.log(jnp.exp(positive - top) + total)
        active = act_ref[:, window + 2 : window + 3]
        weight = factor * active
        pos_coef = weight * (jnp.exp(positive - log_total) - 1.0)
        pos_after = jnp.where(after, pos_coef, 0.0).astype(BF16)
        if window != 0:
            coef = (weight * jnp.exp(block[-window] - log_total)).astype(BF16)
            term = cols_dot(coef, query)
            if window == -1:
                term = term + cols_dot(pos_after, query)
            if window == -2:
                code_acc[...] = term
            else:
                code_acc[...] += term
        else:
            coefs = {d: (weight * jnp.exp(block[d] - log_total)).astype(BF16) for d in beside}
            coefs[0] = jnp.where(here, pos_coef, 0.0).astype(BF16)
            wide = jnp.concatenate([coefs[d] for d in range(-REACH, REACH + 1)], axis=1)
            delta = jnp.dot(
                wide, codes[base : base + 5 * frames], preferred_element_type=F32
            ) + jnp.dot(
                pos_after, codes[base + 3 * frames : base + 4 * frames], preferred_element_type=F32
            )
            delta = delta.astype(BF16)
            for part in range(parts):
                step, at = divmod(part * pred_cols, width)
                blocks[part // cores, part % cores, :, :pred_cols] = delta[
                    step * frames : (step + 1) * frames, at : at + pred_cols
                ]
            code_delta = (code_acc[...] + cols_dot(coefs[0], query)).astype(BF16)
            for part in range(parts):
                blocks[part // cores, part % cores, :, pred_cols:] = code_delta[
                    :, part * code_cols : (part + 1) * code_cols
                ]
            loss = jnp.sum(active * (log_total - positive), axis=0, keepdims=True)
            loss_ref[...] = jnp.broadcast_to(loss, loss_ref.shape)
    for back, out in enumerate((out_0, out_1, out_2, out_3)):
        out[...] = blocks[(place + ring - back) % ring]


def term_kernel(
    pred_cols, core_ref, loss_ref, same_0, same_1, same_2, same_3, cross_0, cross_1, cross_2, cross_3,
    rows_same, rows_cross, out_ref, held,
):
    _, frames, lanes_all = same_0.shape
    plane = out_ref.shape[0]
    core, place = core_ref[0, 0], core_ref[0, 1]
    both = ((same_0, same_1, same_2, same_3), (cross_0, cross_1, cross_2, cross_3))
    ring = len(both[0])
    for side, blocks in enumerate(both):
        for spot, block in enumerate(blocks):
            start = pl.multiple_of((place + spot) % ring * frames, frames)
            held[side, pl.ds(start, frames)] = block[core]
    width = rows_same.shape[1] // 2
    rows = 2 * width // ring
    span = rows // plane
    depth = ring * span // 2
    for first, lanes in ((width, slice(0, pred_cols)), (0, slice(pred_cols, lanes_all))):
        for half in range(ring // 2):
            blocks = slice(first + half * rows, first + (half + 1) * rows)
            term = cols_dot(rows_same[:, blocks], held[0, :, lanes])
            term = term + cols_dot(rows_cross[:, blocks], held[1, :, lanes])
            term = term.reshape(2, plane, span // 2, -1)
            term = jnp.concatenate([term[0], term[1]], axis=1).astype(BF16)
            for tile in range(term.shape[2] // 128):
                at = (lanes.start // 128 + tile) * depth + half * span
                out_ref[:, at : at + span] = term[:, :, tile * 128 : (tile + 1) * 128]
    loss = loss_ref[...]
    high = loss.astype(BF16).astype(F32)
    middle = (loss - high).astype(BF16).astype(F32)
    row = lax.broadcasted_iota(jnp.int32, (16, 128), 0)
    terms = jnp.where(row == 0, high, jnp.where(row == 1, middle, loss - high - middle))
    terms = jnp.where(row < 3, terms, 0.0).astype(BF16)
    out_ref[:, out_ref.shape[1] - 16 :] = jnp.broadcast_to(terms[None], (plane, 16, 128))


def sum_kernel(core_ref, terms_ref, out_0, out_1, out_2, out_3, blocks):
    total = terms_ref[0].astype(F32)
    for source in range(1, terms_ref.shape[0]):
        total = total + terms_ref[source].astype(F32)
    place = core_ref[0, 1]
    ring, cores, rows, lanes = blocks.shape
    owned = rows // 2
    depth = ring * cores * owned
    loss = jnp.sum(total[total.shape[0] - 16 :, :1], axis=0, keepdims=True)
    for part in range(ring * cores):
        for tile in range(lanes // 128):
            at = tile * depth + part * owned
            blocks[part // cores, part % cores, :owned, tile * 128 : (tile + 1) * 128] = total[
                at : at + owned
            ]
        blocks[part // cores, part % cores, owned:] = jnp.broadcast_to(loss, (owned, lanes))
    for back, out in enumerate((out_0, out_1, out_2, out_3)):
        out[...] = blocks[(place + ring - back) % ring]


def gather_kernel(
    core_ref, count_ref, same_0, same_1, same_2, same_3, cross_0, cross_1, cross_2, cross_3,
    loss_ref, pred_ref, proj_ref, held,
):
    core, place = core_ref[0, 0], core_ref[0, 1]
    both = ((same_0, same_1, same_2, same_3), (cross_0, cross_1, cross_2, cross_3))
    ring = len(both[0])
    for side, blocks in enumerate(both):
        for spot, block in enumerate(blocks):
            source = 2 * ((place + spot) % ring) + (core if side == 0 else 1 - core)
            held[source] = block[core]
    parts, rows, lanes = held.shape
    owned, horizons, width = pred_ref.shape
    code_cols = width // parts
    pred_cols = lanes - code_cols
    loss = jnp.zeros((1, 1), F32)
    for part in range(parts):
        block = held[part]
        step, at = divmod(part * pred_cols, width)
        pred_ref[:, step, at : at + pred_cols] = block[:owned, :pred_cols]
        proj_ref[:, part * code_cols : (part + 1) * code_cols] = block[:owned, pred_cols:]
        loss = loss + block[owned : owned + 1, :1]
    loss_ref[...] = loss * (1.0 / jnp.maximum(count_ref[:, :1], 1.0))


def per_device(features, context, predictor, projection, lengths, frame_mask):
    frames, width = features.shape[1], features.shape[2]
    horizons = predictor.shape[1]
    feat, ctx = features[0], context[0]
    windows, recordings = size_of(TM), size_of(DP)
    devices = windows * recordings
    parts, plane = size_of(RING), size_of(PLANE)
    tm = lax.axis_index(TM)
    core = lax.axis_index("core")

    encoded = jnp.dot(feat, projection, preferred_element_type=F32).astype(BF16)
    both = jnp.concatenate([encoded, ctx], axis=0)
    low2, high2 = window_at(both, -2), window_at(both, 2)
    both_x = other_core(both)
    positions = lax.broadcasted_iota(jnp.int32, (1, frames), 1)
    usable = ((frame_mask == 1) & (positions < lengths)).astype(F32)
    usable_x = other_core(usable)
    pair = jnp.concatenate(
        [jnp.where(core == 0, usable, usable_x), jnp.where(core == 0, usable_x, usable)], axis=1
    )
    pair, both_x = lax.optimization_barrier((pair, both_x))
    chips = size_of(CHIPS)
    flags = lax.all_to_all(
        jnp.broadcast_to(pair, (chips, 2 * frames)), CHIPS, 0, 0, tiled=True
    )
    low4, high4 = window_at(encoded, -4), window_at(encoded, 4)
    weights = predictor.reshape(width, horizons * width)
    token = pl.pallas_call(
        token_kernel,
        out_shape=jax.ShapeDtypeStruct((1, 128), F32),
        in_specs=[pl.BlockSpec(memory_space=pl.ANY)],
        out_specs=pl.BlockSpec(memory_space=pltpu.VMEM),
    )(weights)
    low2, high2, flags, token = lax.optimization_barrier((low2, high2, flags, token))
    low2_x, high2_x = other_core(low2), other_core(high2)
    low4_x, high4_x = other_core(low4), other_core(high4)
    rows_ring = lax.all_gather(jnp.concatenate([feat, ctx], axis=1), "y", tiled=True)

    smem = pl.BlockSpec(memory_space=pltpu.SMEM)
    vmem = pl.BlockSpec(memory_space=pltpu.VMEM)
    anywhere = pl.BlockSpec(memory_space=pl.ANY)
    limit = pltpu.CompilerParams(vmem_limit_bytes=16 * 2**20)

    spot = jnp.stack([lax.axis_index(ALL), tm]).reshape(1, 2).astype(jnp.int32)
    count, near, act, preds = pl.pallas_call(
        functools.partial(prepare_kernel, horizons, windows),
        out_shape=(
            jax.ShapeDtypeStruct((1, 128), F32),
            jax.ShapeDtypeStruct((16, frames), F32),
            jax.ShapeDtypeStruct((horizons * frames, 16), F32),
            jax.ShapeDtypeStruct((3, horizons * frames, width), BF16),
        ),
        in_specs=[smem, vmem, vmem, vmem] + [anywhere] * 3,
        out_specs=(vmem, vmem, vmem, vmem),
        scratch_shapes=[pltpu.VMEM((3 * frames, width), BF16), pltpu.SemaphoreType.DMA((3,))],
        compiler_params=limit,
        cost_estimate=pl.CostEstimate(flops=1700000000, bytes_accessed=6500000, transcendentals=0),
    )(spot, flags, token, weights, low2, ctx, high2)

    pred_cols, code_cols = horizons * width // parts, width // parts
    lanes = pred_cols + code_cols
    core_word = jnp.stack([core, lax.axis_index("y")]).reshape(1, 2).astype(jnp.int32)
    ring = lax.axis_size("y")
    *deltas, loss_part = pl.pallas_call(
        functools.partial(delta_kernel, horizons),
        out_shape=[jax.ShapeDtypeStruct((2, frames, lanes), BF16)] * ring
        + [jax.ShapeDtypeStruct((1, 128), F32)],
        in_specs=[smem] + [vmem] * 5 + [anywhere] * 10,
        out_specs=[vmem] * (ring + 1),
        scratch_shapes=[
            pltpu.VMEM((11 * frames, width), BF16),
            pltpu.VMEM((frames, width), F32),
            pltpu.VMEM((4 * frames, width), BF16),
            pltpu.VMEM((2, horizons * frames, width), BF16),
            pltpu.VMEM((ring, 2, frames, lanes), BF16),
            pltpu.SemaphoreType.DMA((13,)),
        ],
        compiler_params=pltpu.CompilerParams(vmem_limit_bytes=20 * 2**20),
        cost_estimate=pl.CostEstimate(
            flops=4000000000, bytes_accessed=12000000, transcendentals=900000
        ),
    )(
        core_word, count, near, act, preds, weights,
        both, low2, high2, low4, high4, both_x, low2_x, high2_x, low4_x, high4_x,
    )

    _, rows_ring = lax.optimization_barrier((loss_part, rows_ring))
    rows_cross = other_core(rows_ring)
    same = [deltas[0]] + [ring_shift(deltas[step], ("y",), step) for step in range(1, ring)]
    cross = [other_core(block) for block in same]
    terms = pl.pallas_call(
        functools.partial(term_kernel, pred_cols),
        out_shape=jax.ShapeDtypeStruct((plane, width // plane * lanes // 128 + 16, 128), BF16),
        in_specs=[smem] + [vmem] * 11,
        out_specs=vmem,
        scratch_shapes=[pltpu.VMEM((2, ring * frames, lanes), BF16)],
        compiler_params=limit,
        cost_estimate=pl.CostEstimate(flops=1600000000, bytes_accessed=6000000, transcendentals=0),
    )(core_word, loss_part, *same, *cross, rows_ring, rows_cross)

    owned = width // devices
    terms = lax.all_to_all(terms, PLANE, 0, 0, tiled=True)
    block = jax.ShapeDtypeStruct((2, 2 * owned, lanes), F32)
    sums = pl.pallas_call(
        sum_kernel,
        out_shape=[block] * ring,
        in_specs=[smem, vmem],
        out_specs=[vmem] * ring,
        scratch_shapes=[pltpu.VMEM((ring, 2, 2 * owned, lanes), F32)],
    )(core_word, terms)
    same = [sums[0]] + [ring_shift(sums[step], ("y",), step) for step in range(1, ring)]
    cross = [other_core(block) for block in same]
    loss, grad_pred, grad_proj = pl.pallas_call(
        gather_kernel,
        out_shape=(
            jax.ShapeDtypeStruct((1, 1), F32),
            jax.ShapeDtypeStruct((owned, horizons, width), F32),
            jax.ShapeDtypeStruct((owned, width), F32),
        ),
        in_specs=[smem] + [vmem] * 9,
        out_specs=(vmem, vmem, vmem),
        scratch_shapes=[pltpu.VMEM((parts, 2 * owned, lanes), F32)],
    )(core_word, count, *same, *cross)
    return (loss.reshape(()), grad_pred, grad_proj)


def solution(mesh):
    fine = Mesh(mesh.devices.reshape(4, 2, 8, 2, 2), ALL)
    placed = (P(DP, TM, None), P(DP, TM, None), P(), P(), P(DP, TM), P(DP, TM))
    return jax.shard_map(
        per_device,
        mesh=fine,
        in_specs=placed,
        out_specs=(P(), P(ALL, None, None), P(ALL, None)),
        check_vma=False,
    )
```

```python
import functools

import jax
import jax.numpy as jnp
from jax import lax
from jax.experimental import pallas as pl
from jax.experimental.pallas import tpu as pltpu
from jax.sharding import Mesh, PartitionSpec as P

DP = ("y", "xh")
TM = ("z", "xl", "core")
ALL = DP + TM
PLANE = ("xh", "z", "xl")
RING = ("y", "core")
CHIPS = ("y", "xh", "z", "xl")
F32 = jnp.float32
BF16 = jnp.bfloat16
REACH = 2


def size_of(names):
    size = 1
    for name in names:
        size *= lax.axis_size(name)
    return size


def ring_shift(block, axes, offset):
    size = size_of(axes)
    return lax.ppermute(block, axes, [((i + offset) % size, i) for i in range(size)])


def window_at(block, offset):
    return ring_shift(block, TM, offset)


def other_core(block):
    return lax.ppermute(block, "core", [(0, 1), (1, 0)])


def rows_dot(a, b):
    return lax.dot_general(a, b, (((1,), (1,)), ((), ())), preferred_element_type=F32)


def cols_dot(a, b):
    return lax.dot_general(a, b, (((0,), (0,)), ((), ())), preferred_element_type=F32)


def flag_terms(horizons, windows, device, tm, flags):
    chips, span = flags.shape
    frames = span // 2
    row = lax.broadcasted_iota(jnp.int32, flags.shape, 0)
    lane = lax.broadcasted_iota(jnp.int32, flags.shape, 1)
    last = row % (windows // 2) == windows // 2 - 1
    following = jnp.where(last, 0.0, pltpu.roll(flags, chips - 1, 0))
    slot = lax.broadcasted_iota(jnp.int32, (chips, 16), 1)
    source = lax.broadcasted_iota(jnp.int32, (chips, 16), 0)

    def picked(values, reach, transposed):
        window = slot - reach
        inside = (tm + window >= 0) & (tm + window < windows)
        out = 0.0
        for half in range(2):
            pick = (2 * source + half == device + window) & inside
            pick = jnp.where(pick, 1.0, 0.0).astype(BF16)
            part = values[:, half * frames : (half + 1) * frames].astype(BF16)
            out = out + (cols_dot(part, pick) if transposed else cols_dot(pick, part))
        return out

    total = jnp.zeros((1, span), F32)
    act = []
    for h in range(1, horizons + 1):
        ahead = jnp.where(
            lane < span - h, pltpu.roll(flags, span - h, 1), pltpu.roll(following, span - h, 1)
        )
        pairs = flags * ahead
        total = total + jnp.sum(pairs, axis=0, keepdims=True)
        act.append(picked(pairs, REACH, True))
    count = jnp.sum(total, axis=1, keepdims=True)
    return count, picked(flags, 2 * REACH, False), jnp.concatenate(act, axis=0)


def stacked_dot(rows, weights, out_ref):
    windows, stacked, width = out_ref.shape
    tile = 512
    frames = stacked * width // weights.shape[1]
    for at in range(0, weights.shape[1], tile):
        part = jnp.dot(rows, weights[:, at : at + tile], preferred_element_type=F32).astype(BF16)
        step, lane = divmod(at, width)
        for w in range(windows):
            out_ref[w, step * frames : (step + 1) * frames, lane : lane + tile] = part[
                w * frames : (w + 1) * frames
            ]


def pred_kernel(low2, ctx, high2, weights, out_ref, rows, sems):
    frames = ctx.shape[0]
    copies = [
        pltpu.make_async_copy(block, rows.at[pl.ds(slot * frames, frames)], sems.at[slot])
        for slot, block in enumerate(
            (low2.at[pl.ds(frames, frames)], ctx, high2.at[pl.ds(frames, frames)])
        )
    ]
    for copy in copies:
        copy.start()
    for copy in copies:
        copy.wait()
    stacked_dot(rows[...], weights, out_ref)


def delta_kernel(
    horizons, windows, core_ref, flags_ref, preds_ref, weights,
    both, low2, high2, low4, high4, both_x, low2_x, high2_x, low4_x, high4_x,
    out_0, out_1, out_2, out_3, loss_ref, count_ref, codes, code_acc, odd_ctx, odd_pred, blocks, sems,
):
    frames, width = low4.shape
    scale = width ** (-0.5)
    ring, cores = blocks.shape[:2]
    parts = ring * cores
    pred_cols, code_cols = horizons * width // parts, width // parts
    core, place = core_ref[0, 0], core_ref[0, 1]

    def put(sem, block, start, held, slot):
        at = slot * frames
        if not isinstance(slot, int):
            at = pl.multiple_of(at, frames)
        return pltpu.make_async_copy(
            block.at[pl.ds(start, frames)], held.at[pl.ds(at, frames)], sems.at[sem]
        )

    ctx_copies = [
        put(0, low2_x, frames, odd_ctx, 1 - core),
        put(1, both_x, frames, odd_ctx, 2 - core),
        put(2, high2_x, frames, odd_ctx, 3 - core),
    ]
    code_copies = [
        put(3, low4, 0, codes, 1),
        put(4, low2, 0, codes, 3),
        put(5, both, 0, codes, 5),
        put(6, high2, 0, codes, 7),
        put(7, high4, 0, codes, 9),
        put(8, low4_x, 0, codes, 2 - 2 * core),
        put(9, low2_x, 0, codes, 4 - 2 * core),
        put(10, both_x, 0, codes, 6 - 2 * core),
        put(11, high2_x, 0, codes, 8 - 2 * core),
        put(12, high4_x, 0, codes, 10 - 2 * core),
    ]
    for copy in ctx_copies + code_copies:
        copy.start()
    for copy in ctx_copies:
        copy.wait()
    count, near, act = flag_terms(
        horizons, windows, core_ref[0, 2], core_ref[0, 3], flags_ref[...]
    )
    count_ref[...] = jnp.broadcast_to(count, count_ref.shape)
    stacked_dot(odd_ctx[frames : 3 * frames], weights, odd_pred)
    for copy in code_copies:
        copy.wait()
    shape = (horizons * frames, frames)
    row = lax.broadcasted_iota(jnp.int32, shape, 0)
    ahead = row % frames + row // frames + 1
    col = lax.broadcasted_iota(jnp.int32, shape, 1)
    here, after = col == ahead, col == ahead - frames
    preds = {-2: preds_ref[0], -1: odd_pred[0], 0: preds_ref[1], 1: odd_pred[1], 2: preds_ref[2]}
    factor = (1.0 / jnp.maximum(count, 1.0)) * scale
    beside = (-2, -1, 1, 2)
    for window in (-2, -1, 1, 2, 0):
        base = (window + 3) * frames
        query = preds[window]
        scores = rows_dot(query, codes[base : base + 5 * frames]) * scale
        block = {
            d: scores[:, (d + 2) * frames : (d + 3) * frames] for d in range(-REACH, REACH + 1)
        }
        positive = jnp.sum(
            jnp.where(here, block[0], 0.0) + jnp.where(after, block[1], 0.0),
            axis=1,
            keepdims=True,
        )
        for d in beside:
            usable = near[window + d + 4 : window + d + 5]
            block[d] = jnp.where(usable > 0, block[d], -1e30)
        top = jnp.maximum(jnp.maximum(block[-2], block[-1]), jnp.maximum(block[1], block[2]))
        top = jnp.maximum(positive, jnp.max(top, axis=1, keepdims=True))
        total = sum(jnp.exp(block[d] - top) for d in beside)
        total = jnp.sum(total, axis=1, keepdims=True)
        log_total = top + jnp.log(jnp.exp(positive - top) + total)
        active = act[:, window + 2 : window + 3]
        weight = factor * active
        pos_coef = weight * (jnp.exp(positive - log_total) - 1.0)
        pos_after = jnp.where(after, pos_coef, 0.0).astype(BF16)
        if window != 0:
            coef = (weight * jnp.exp(block[-window] - log_total)).astype(BF16)
            term = cols_dot(coef, query)
            if window == -1:
                term = term + cols_dot(pos_after, query)
            if window == -2:
                code_acc[...] = term
            else:
                code_acc[...] += term
        else:
            coefs = {d: (weight * jnp.exp(block[d] - log_total)).astype(BF16) for d in beside}
            coefs[0] = jnp.where(here, pos_coef, 0.0).astype(BF16)
            wide = jnp.concatenate([coefs[d] for d in range(-REACH, REACH + 1)], axis=1)
            delta = jnp.dot(
                wide, codes[base : base + 5 * frames], preferred_element_type=F32
            ) + jnp.dot(
                pos_after, codes[base + 3 * frames : base + 4 * frames], preferred_element_type=F32
            )
            delta = delta.astype(BF16)
            for part in range(parts):
                step, at = divmod(part * pred_cols, width)
                blocks[part // cores, part % cores, :, :pred_cols] = delta[
                    step * frames : (step + 1) * frames, at : at + pred_cols
                ]
            code_delta = (code_acc[...] + cols_dot(coefs[0], query)).astype(BF16)
            for part in range(parts):
                blocks[part // cores, part % cores, :, pred_cols:] = code_delta[
                    :, part * code_cols : (part + 1) * code_cols
                ]
            loss = jnp.sum(active * (log_total - positive), axis=0, keepdims=True)
            loss_ref[...] = jnp.broadcast_to(loss, loss_ref.shape)
    for back, out in enumerate((out_0, out_1, out_2, out_3)):
        out[...] = blocks[(place + ring - back) % ring]


def term_kernel(
    pred_cols, core_ref, loss_ref, same_0, same_1, same_2, same_3, cross_0, cross_1, cross_2, cross_3,
    rows_same, rows_cross, out_ref, held,
):
    _, frames, lanes_all = same_0.shape
    plane = out_ref.shape[0]
    core, place = core_ref[0, 0], core_ref[0, 1]
    both = ((same_0, same_1, same_2, same_3), (cross_0, cross_1, cross_2, cross_3))
    ring = len(both[0])
    for side, blocks in enumerate(both):
        for spot, block in enumerate(blocks):
            start = pl.multiple_of((place + spot) % ring * frames, frames)
            held[side, pl.ds(start, frames)] = block[core]
    width = rows_same.shape[1] // 2
    rows = 2 * width // ring
    span = rows // plane
    depth = ring * span // 2
    for first, lanes in ((width, slice(0, pred_cols)), (0, slice(pred_cols, lanes_all))):
        for half in range(ring // 2):
            blocks = slice(first + half * rows, first + (half + 1) * rows)
            term = cols_dot(rows_same[:, blocks], held[0, :, lanes])
            term = term + cols_dot(rows_cross[:, blocks], held[1, :, lanes])
            term = term.reshape(2, plane, span // 2, -1)
            term = jnp.concatenate([term[0], term[1]], axis=1).astype(BF16)
            for tile in range(term.shape[2] // 128):
                at = (lanes.start // 128 + tile) * depth + half * span
                out_ref[:, at : at + span] = term[:, :, tile * 128 : (tile + 1) * 128]
    loss = loss_ref[...]
    high = loss.astype(BF16).astype(F32)
    middle = (loss - high).astype(BF16).astype(F32)
    row = lax.broadcasted_iota(jnp.int32, (16, 128), 0)
    terms = jnp.where(row == 0, high, jnp.where(row == 1, middle, loss - high - middle))
    terms = jnp.where(row < 3, terms, 0.0).astype(BF16)
    out_ref[:, out_ref.shape[1] - 16 :] = jnp.broadcast_to(terms[None], (plane, 16, 128))


def sum_kernel(core_ref, terms_ref, out_0, out_1, out_2, out_3, blocks):
    total = terms_ref[0].astype(F32)
    for source in range(1, terms_ref.shape[0]):
        total = total + terms_ref[source].astype(F32)
    place = core_ref[0, 1]
    ring, cores, rows, lanes = blocks.shape
    owned = rows // 2
    depth = ring * cores * owned
    loss = jnp.sum(total[total.shape[0] - 16 :, :1], axis=0, keepdims=True)
    for part in range(ring * cores):
        for tile in range(lanes // 128):
            at = tile * depth + part * owned
            blocks[part // cores, part % cores, :owned, tile * 128 : (tile + 1) * 128] = total[
                at : at + owned
            ]
        blocks[part // cores, part % cores, owned:] = jnp.broadcast_to(loss, (owned, lanes))
    for back, out in enumerate((out_0, out_1, out_2, out_3)):
        out[...] = blocks[(place + ring - back) % ring]


def gather_kernel(
    core_ref, count_ref, same_0, same_1, same_2, same_3, cross_0, cross_1, cross_2, cross_3,
    loss_ref, pred_ref, proj_ref, held,
):
    core, place = core_ref[0, 0], core_ref[0, 1]
    both = ((same_0, same_1, same_2, same_3), (cross_0, cross_1, cross_2, cross_3))
    ring = len(both[0])
    for side, blocks in enumerate(both):
        for spot, block in enumerate(blocks):
            source = 2 * ((place + spot) % ring) + (core if side == 0 else 1 - core)
            held[source] = block[core]
    parts, rows, lanes = held.shape
    owned, horizons, width = pred_ref.shape
    code_cols = width // parts
    pred_cols = lanes - code_cols
    loss = jnp.zeros((1, 1), F32)
    for part in range(parts):
        block = held[part]
        step, at = divmod(part * pred_cols, width)
        pred_ref[:, step, at : at + pred_cols] = block[:owned, :pred_cols]
        proj_ref[:, part * code_cols : (part + 1) * code_cols] = block[:owned, pred_cols:]
        loss = loss + block[owned : owned + 1, :1]
    loss_ref[...] = loss * (1.0 / jnp.maximum(count_ref[:, :1], 1.0))


def per_device(features, context, predictor, projection, lengths, frame_mask):
    frames, width = features.shape[1], features.shape[2]
    horizons = predictor.shape[1]
    feat, ctx = features[0], context[0]
    windows, recordings = size_of(TM), size_of(DP)
    devices = windows * recordings
    parts, plane = size_of(RING), size_of(PLANE)
    tm = lax.axis_index(TM)
    core = lax.axis_index("core")

    encoded = jnp.dot(feat, projection, preferred_element_type=F32).astype(BF16)
    both = jnp.concatenate([encoded, ctx], axis=0)
    low2, high2 = window_at(both, -2), window_at(both, 2)
    both_x = other_core(both)
    positions = lax.broadcasted_iota(jnp.int32, (1, frames), 1)
    usable = ((frame_mask == 1) & (positions < lengths)).astype(F32)
    usable_x = other_core(usable)
    pair = jnp.concatenate(
        [jnp.where(core == 0, usable, usable_x), jnp.where(core == 0, usable_x, usable)], axis=1
    )
    pair, both_x = lax.optimization_barrier((pair, both_x))
    chips = size_of(CHIPS)
    flags = lax.all_to_all(
        jnp.broadcast_to(pair, (chips, 2 * frames)), CHIPS, 0, 0, tiled=True
    )
    low4, high4 = window_at(encoded, -4), window_at(encoded, 4)
    weights = predictor.reshape(width, horizons * width)
    low2, high2, weights, flags = lax.optimization_barrier((low2, high2, weights, flags))
    low2_x, high2_x = other_core(low2), other_core(high2)
    low4_x, high4_x = other_core(low4), other_core(high4)
    rows_ring = lax.all_gather(jnp.concatenate([feat, ctx], axis=1), "y", tiled=True)

    smem = pl.BlockSpec(memory_space=pltpu.SMEM)
    vmem = pl.BlockSpec(memory_space=pltpu.VMEM)
    anywhere = pl.BlockSpec(memory_space=pl.ANY)
    limit = pltpu.CompilerParams(vmem_limit_bytes=16 * 2**20)

    preds = pl.pallas_call(
        pred_kernel,
        out_shape=jax.ShapeDtypeStruct((3, horizons * frames, width), BF16),
        in_specs=[anywhere] * 3 + [vmem],
        out_specs=vmem,
        scratch_shapes=[pltpu.VMEM((3 * frames, width), BF16), pltpu.SemaphoreType.DMA((3,))],
        compiler_params=limit,
        cost_estimate=pl.CostEstimate(flops=1600000000, bytes_accessed=6500000, transcendentals=0),
    )(low2, ctx, high2, weights)

    pred_cols, code_cols = horizons * width // parts, width // parts
    lanes = pred_cols + code_cols
    core_word = jnp.stack([core, lax.axis_index("y"), lax.axis_index(ALL), tm])
    core_word = core_word.reshape(1, 4).astype(jnp.int32)
    ring = lax.axis_size("y")
    *deltas, loss_part, count = pl.pallas_call(
        functools.partial(delta_kernel, horizons, windows),
        out_shape=[jax.ShapeDtypeStruct((2, frames, lanes), BF16)] * ring
        + [jax.ShapeDtypeStruct((1, 128), F32)] * 2,
        in_specs=[smem] + [vmem] * 3 + [anywhere] * 10,
        out_specs=[vmem] * (ring + 2),
        scratch_shapes=[
            pltpu.VMEM((11 * frames, width), BF16),
            pltpu.VMEM((frames, width), F32),
            pltpu.VMEM((4 * frames, width), BF16),
            pltpu.VMEM((2, horizons * frames, width), BF16),
            pltpu.VMEM((ring, 2, frames, lanes), BF16),
            pltpu.SemaphoreType.DMA((13,)),
        ],
        compiler_params=pltpu.CompilerParams(vmem_limit_bytes=20 * 2**20),
        cost_estimate=pl.CostEstimate(
            flops=4000000000, bytes_accessed=12000000, transcendentals=900000
        ),
    )(
        core_word, flags, preds, weights,
        both, low2, high2, low4, high4, both_x, low2_x, high2_x, low4_x, high4_x,
    )

    _, rows_ring = lax.optimization_barrier((loss_part, rows_ring))
    rows_cross = other_core(rows_ring)
    same = [deltas[0]] + [ring_shift(deltas[step], ("y",), step) for step in range(1, ring)]
    cross = [other_core(block) for block in same]
    terms = pl.pallas_call(
        functools.partial(term_kernel, pred_cols),
        out_shape=jax.ShapeDtypeStruct((plane, width // plane * lanes // 128 + 16, 128), BF16),
        in_specs=[smem] + [vmem] * 11,
        out_specs=vmem,
        scratch_shapes=[pltpu.VMEM((2, ring * frames, lanes), BF16)],
        compiler_params=limit,
        cost_estimate=pl.CostEstimate(flops=1600000000, bytes_accessed=6000000, transcendentals=0),
    )(core_word, loss_part, *same, *cross, rows_ring, rows_cross)

    owned = width // devices
    terms = lax.all_to_all(terms, PLANE, 0, 0, tiled=True)
    block = jax.ShapeDtypeStruct((2, 2 * owned, lanes), F32)
    sums = pl.pallas_call(
        sum_kernel,
        out_shape=[block] * ring,
        in_specs=[smem, vmem],
        out_specs=[vmem] * ring,
        scratch_shapes=[pltpu.VMEM((ring, 2, 2 * owned, lanes), F32)],
    )(core_word, terms)
    same = [sums[0]] + [ring_shift(sums[step], ("y",), step) for step in range(1, ring)]
    cross = [other_core(block) for block in same]
    loss, grad_pred, grad_proj = pl.pallas_call(
        gather_kernel,
        out_shape=(
            jax.ShapeDtypeStruct((1, 1), F32),
            jax.ShapeDtypeStruct((owned, horizons, width), F32),
            jax.ShapeDtypeStruct((owned, width), F32),
        ),
        in_specs=[smem] + [vmem] * 9,
        out_specs=(vmem, vmem, vmem),
        scratch_shapes=[pltpu.VMEM((parts, 2 * owned, lanes), F32)],
    )(core_word, count, *same, *cross)
    return (loss.reshape(()), grad_pred, grad_proj)


def solution(mesh):
    fine = Mesh(mesh.devices.reshape(4, 2, 8, 2, 2), ALL)
    placed = (P(DP, TM, None), P(DP, TM, None), P(), P(), P(DP, TM), P(DP, TM))
    return jax.shard_map(
        per_device,
        mesh=fine,
        in_specs=placed,
        out_specs=(P(), P(ALL, None, None), P(ALL, None)),
        check_vma=False,
    )
```

```python
import functools

import jax
import jax.numpy as jnp
from jax import lax
from jax.experimental import pallas as pl
from jax.experimental.pallas import tpu as pltpu
from jax.sharding import Mesh, PartitionSpec as P

DP = ("y", "xh")
TM = ("z", "xl", "core")
ALL = DP + TM
PLANE = ("xh", "z", "xl")
RING = ("y", "core")
CHIPS = ("y", "xh", "z", "xl")
F32 = jnp.float32
BF16 = jnp.bfloat16
REACH = 2


def size_of(names):
    size = 1
    for name in names:
        size *= lax.axis_size(name)
    return size


def ring_shift(block, axes, offset):
    size = size_of(axes)
    return lax.ppermute(block, axes, [((i + offset) % size, i) for i in range(size)])


def window_at(block, offset):
    return ring_shift(block, TM, offset)


def other_core(block):
    return lax.ppermute(block, "core", [(0, 1), (1, 0)])


def rows_dot(a, b):
    return lax.dot_general(a, b, (((1,), (1,)), ((), ())), preferred_element_type=F32)


def cols_dot(a, b):
    return lax.dot_general(a, b, (((0,), (0,)), ((), ())), preferred_element_type=F32)


def flag_terms(horizons, windows, device, tm, flags):
    chips, span = flags.shape
    frames = span // 2
    row = lax.broadcasted_iota(jnp.int32, flags.shape, 0)
    lane = lax.broadcasted_iota(jnp.int32, flags.shape, 1)
    last = row % (windows // 2) == windows // 2 - 1
    following = jnp.where(last, 0.0, pltpu.roll(flags, chips - 1, 0))
    slot = lax.broadcasted_iota(jnp.int32, (chips, 16), 1)
    source = lax.broadcasted_iota(jnp.int32, (chips, 16), 0)

    def picked(values, reach, transposed):
        window = slot - reach
        inside = (tm + window >= 0) & (tm + window < windows)
        out = 0.0
        for half in range(2):
            pick = (2 * source + half == device + window) & inside
            pick = jnp.where(pick, 1.0, 0.0).astype(BF16)
            part = values[:, half * frames : (half + 1) * frames].astype(BF16)
            out = out + (cols_dot(part, pick) if transposed else cols_dot(pick, part))
        return out

    total = jnp.zeros((1, span), F32)
    act = []
    for h in range(1, horizons + 1):
        ahead = jnp.where(
            lane < span - h, pltpu.roll(flags, span - h, 1), pltpu.roll(following, span - h, 1)
        )
        pairs = flags * ahead
        total = total + jnp.sum(pairs, axis=0, keepdims=True)
        act.append(picked(pairs, REACH, True))
    count = jnp.sum(total, axis=1, keepdims=True)
    return count, picked(flags, 2 * REACH, False), jnp.concatenate(act, axis=0)


def stacked_dot(rows, weights, out_ref):
    windows, stacked, width = out_ref.shape
    tile = 512
    frames = stacked * width // weights.shape[1]
    for at in range(0, weights.shape[1], tile):
        part = jnp.dot(rows, weights[:, at : at + tile], preferred_element_type=F32).astype(BF16)
        step, lane = divmod(at, width)
        for w in range(windows):
            out_ref[w, step * frames : (step + 1) * frames, lane : lane + tile] = part[
                w * frames : (w + 1) * frames
            ]


def pred_kernel(low2, ctx, high2, weights, out_ref, done_ref, rows, sems):
    frames = ctx.shape[0]
    copies = [
        pltpu.make_async_copy(block, rows.at[pl.ds(slot * frames, frames)], sems.at[slot])
        for slot, block in enumerate(
            (low2.at[pl.ds(frames, frames)], ctx, high2.at[pl.ds(frames, frames)])
        )
    ]
    for copy in copies:
        copy.start()
    for copy in copies:
        copy.wait()
    stacked_dot(rows[...], weights, out_ref)
    done_ref[...] = jnp.zeros_like(done_ref)


def delta_kernel(
    horizons, windows, core_ref, flags_ref, preds_ref, weights,
    both, low2, high2, low4, high4, both_x, low2_x, high2_x, low4_x, high4_x,
    out_0, out_1, out_2, out_3, loss_ref, codes, code_acc, odd_ctx, odd_pred, blocks, sems,
):
    frames, width = low4.shape
    scale = width ** (-0.5)
    ring, cores = blocks.shape[:2]
    parts = ring * cores
    pred_cols, code_cols = horizons * width // parts, width // parts
    core, place = core_ref[0, 0], core_ref[0, 1]

    def put(sem, block, start, held, slot):
        at = slot * frames
        if not isinstance(slot, int):
            at = pl.multiple_of(at, frames)
        return pltpu.make_async_copy(
            block.at[pl.ds(start, frames)], held.at[pl.ds(at, frames)], sems.at[sem]
        )

    ctx_copies = [
        put(0, low2_x, frames, odd_ctx, 1 - core),
        put(1, both_x, frames, odd_ctx, 2 - core),
        put(2, high2_x, frames, odd_ctx, 3 - core),
    ]
    code_copies = [
        put(3, low4, 0, codes, 1),
        put(4, low2, 0, codes, 3),
        put(5, both, 0, codes, 5),
        put(6, high2, 0, codes, 7),
        put(7, high4, 0, codes, 9),
        put(8, low4_x, 0, codes, 2 - 2 * core),
        put(9, low2_x, 0, codes, 4 - 2 * core),
        put(10, both_x, 0, codes, 6 - 2 * core),
        put(11, high2_x, 0, codes, 8 - 2 * core),
        put(12, high4_x, 0, codes, 10 - 2 * core),
    ]
    for copy in ctx_copies + code_copies:
        copy.start()
    for copy in ctx_copies:
        copy.wait()
    count, near, act = flag_terms(
        horizons, windows, core_ref[0, 2], core_ref[0, 3], flags_ref[...]
    )
    stacked_dot(odd_ctx[frames : 3 * frames], weights, odd_pred)
    for copy in code_copies:
        copy.wait()
    shape = (horizons * frames, frames)
    row = lax.broadcasted_iota(jnp.int32, shape, 0)
    ahead = row % frames + row // frames + 1
    col = lax.broadcasted_iota(jnp.int32, shape, 1)
    here, after = col == ahead, col == ahead - frames
    preds = {-2: preds_ref[0], -1: odd_pred[0], 0: preds_ref[1], 1: odd_pred[1], 2: preds_ref[2]}
    factor = (1.0 / jnp.maximum(count, 1.0)) * scale
    beside = (-2, -1, 1, 2)
    for window in (-2, -1, 1, 2, 0):
        base = (window + 3) * frames
        query = preds[window]
        scores = rows_dot(query, codes[base : base + 5 * frames]) * scale
        block = {
            d: scores[:, (d + 2) * frames : (d + 3) * frames] for d in range(-REACH, REACH + 1)
        }
        positive = jnp.sum(
            jnp.where(here, block[0], 0.0) + jnp.where(after, block[1], 0.0),
            axis=1,
            keepdims=True,
        )
        for d in beside:
            usable = near[window + d + 4 : window + d + 5]
            block[d] = jnp.where(usable > 0, block[d], -1e30)
        top = jnp.maximum(jnp.maximum(block[-2], block[-1]), jnp.maximum(block[1], block[2]))
        top = jnp.maximum(positive, jnp.max(top, axis=1, keepdims=True))
        total = sum(jnp.exp(block[d] - top) for d in beside)
        total = jnp.sum(total, axis=1, keepdims=True)
        log_total = top + jnp.log(jnp.exp(positive - top) + total)
        active = act[:, window + 2 : window + 3]
        weight = factor * active
        pos_coef = weight * (jnp.exp(positive - log_total) - 1.0)
        pos_after = jnp.where(after, pos_coef, 0.0).astype(BF16)
        if window != 0:
            coef = (weight * jnp.exp(block[-window] - log_total)).astype(BF16)
            term = cols_dot(coef, query)
            if window == -1:
                term = term + cols_dot(pos_after, query)
            if window == -2:
                code_acc[...] = term
            else:
                code_acc[...] += term
        else:
            coefs = {d: (weight * jnp.exp(block[d] - log_total)).astype(BF16) for d in beside}
            coefs[0] = jnp.where(here, pos_coef, 0.0).astype(BF16)
            wide = jnp.concatenate([coefs[d] for d in range(-REACH, REACH + 1)], axis=1)
            delta = jnp.dot(
                wide, codes[base : base + 5 * frames], preferred_element_type=F32
            ) + jnp.dot(
                pos_after, codes[base + 3 * frames : base + 4 * frames], preferred_element_type=F32
            )
            delta = delta.astype(BF16)
            for part in range(parts):
                step, at = divmod(part * pred_cols, width)
                blocks[part // cores, part % cores, :, :pred_cols] = delta[
                    step * frames : (step + 1) * frames, at : at + pred_cols
                ]
            code_delta = (code_acc[...] + cols_dot(coefs[0], query)).astype(BF16)
            for part in range(parts):
                blocks[part // cores, part % cores, :, pred_cols:] = code_delta[
                    :, part * code_cols : (part + 1) * code_cols
                ]
            loss = jnp.sum(active * (log_total - positive), axis=0, keepdims=True)
            loss = loss * (1.0 / jnp.maximum(count, 1.0))
            loss_ref[...] = jnp.broadcast_to(loss, loss_ref.shape)
    for back, out in enumerate((out_0, out_1, out_2, out_3)):
        out[...] = blocks[(place + ring - back) % ring]


def term_kernel(
    pred_cols, core_ref, loss_ref, same_0, same_1, same_2, same_3, cross_0, cross_1, cross_2, cross_3,
    rows_same, rows_cross, out_ref, held,
):
    _, frames, lanes_all = same_0.shape
    plane = out_ref.shape[0]
    core, place = core_ref[0, 0], core_ref[0, 1]
    both = ((same_0, same_1, same_2, same_3), (cross_0, cross_1, cross_2, cross_3))
    ring = len(both[0])
    for side, blocks in enumerate(both):
        for spot, block in enumerate(blocks):
            start = pl.multiple_of((place + spot) % ring * frames, frames)
            held[side, pl.ds(start, frames)] = block[core]
    width = rows_same.shape[1] // 2
    rows = 2 * width // ring
    span = rows // plane
    depth = ring * span // 2
    for first, lanes in ((width, slice(0, pred_cols)), (0, slice(pred_cols, lanes_all))):
        for half in range(ring // 2):
            blocks = slice(first + half * rows, first + (half + 1) * rows)
            term = cols_dot(rows_same[:, blocks], held[0, :, lanes])
            term = term + cols_dot(rows_cross[:, blocks], held[1, :, lanes])
            term = term.reshape(2, plane, span // 2, -1)
            term = jnp.concatenate([term[0], term[1]], axis=1).astype(BF16)
            for tile in range(term.shape[2] // 128):
                at = (lanes.start // 128 + tile) * depth + half * span
                out_ref[:, at : at + span] = term[:, :, tile * 128 : (tile + 1) * 128]
    loss = loss_ref[...]
    high = loss.astype(BF16).astype(F32)
    middle = (loss - high).astype(BF16).astype(F32)
    row = lax.broadcasted_iota(jnp.int32, (16, 128), 0)
    terms = jnp.where(row == 0, high, jnp.where(row == 1, middle, loss - high - middle))
    terms = jnp.where(row < 3, terms, 0.0).astype(BF16)
    out_ref[:, out_ref.shape[1] - 16 :] = jnp.broadcast_to(terms[None], (plane, 16, 128))


def sum_kernel(core_ref, terms_ref, out_0, out_1, out_2, out_3, blocks):
    total = terms_ref[0].astype(F32)
    for source in range(1, terms_ref.shape[0]):
        total = total + terms_ref[source].astype(F32)
    place = core_ref[0, 1]
    ring, cores, rows, lanes = blocks.shape
    owned = rows // 2
    depth = ring * cores * owned
    loss = jnp.sum(total[total.shape[0] - 16 :, :1], axis=0, keepdims=True)
    for part in range(ring * cores):
        for tile in range(lanes // 128):
            at = tile * depth + part * owned
            blocks[part // cores, part % cores, :owned, tile * 128 : (tile + 1) * 128] = total[
                at : at + owned
            ]
        blocks[part // cores, part % cores, owned:] = jnp.broadcast_to(loss, (owned, lanes))
    for back, out in enumerate((out_0, out_1, out_2, out_3)):
        out[...] = blocks[(place + ring - back) % ring]


def gather_kernel(
    core_ref, same_0, same_1, same_2, same_3, cross_0, cross_1, cross_2, cross_3,
    loss_ref, pred_ref, proj_ref, held,
):
    core, place = core_ref[0, 0], core_ref[0, 1]
    both = ((same_0, same_1, same_2, same_3), (cross_0, cross_1, cross_2, cross_3))
    ring = len(both[0])
    for side, blocks in enumerate(both):
        for spot, block in enumerate(blocks):
            source = 2 * ((place + spot) % ring) + (core if side == 0 else 1 - core)
            held[source] = block[core]
    parts, rows, lanes = held.shape
    owned, horizons, width = pred_ref.shape
    code_cols = width // parts
    pred_cols = lanes - code_cols
    loss = jnp.zeros((1, 1), F32)
    for part in range(parts):
        block = held[part]
        step, at = divmod(part * pred_cols, width)
        pred_ref[:, step, at : at + pred_cols] = block[:owned, :pred_cols]
        proj_ref[:, part * code_cols : (part + 1) * code_cols] = block[:owned, pred_cols:]
        loss = loss + block[owned : owned + 1, :1]
    loss_ref[...] = loss


def per_device(features, context, predictor, projection, lengths, frame_mask):
    frames, width = features.shape[1], features.shape[2]
    horizons = predictor.shape[1]
    feat, ctx = features[0], context[0]
    windows, recordings = size_of(TM), size_of(DP)
    devices = windows * recordings
    parts, plane = size_of(RING), size_of(PLANE)
    tm = lax.axis_index(TM)
    core = lax.axis_index("core")

    encoded = jnp.dot(feat, projection, preferred_element_type=F32).astype(BF16)
    both = jnp.concatenate([encoded, ctx], axis=0)
    low2, high2 = window_at(both, -2), window_at(both, 2)
    both_x = other_core(both)
    positions = lax.broadcasted_iota(jnp.int32, (1, frames), 1)
    usable = ((frame_mask == 1) & (positions < lengths)).astype(F32)
    usable_x = other_core(usable)
    pair = jnp.concatenate(
        [jnp.where(core == 0, usable, usable_x), jnp.where(core == 0, usable_x, usable)], axis=1
    )
    pair, both_x = lax.optimization_barrier((pair, both_x))
    chips = size_of(CHIPS)
    flags = lax.all_to_all(
        jnp.broadcast_to(pair, (chips, 2 * frames)), CHIPS, 0, 0, tiled=True
    )
    low4, high4 = window_at(encoded, -4), window_at(encoded, 4)
    weights = predictor.reshape(width, horizons * width)
    low2, high2, weights, flags = lax.optimization_barrier((low2, high2, weights, flags))
    low2_x, high2_x = other_core(low2), other_core(high2)
    low4_x, high4_x = other_core(low4), other_core(high4)
    rows_ring = lax.all_gather(jnp.concatenate([feat, ctx], axis=1), "y", tiled=True)

    smem = pl.BlockSpec(memory_space=pltpu.SMEM)
    vmem = pl.BlockSpec(memory_space=pltpu.VMEM)
    anywhere = pl.BlockSpec(memory_space=pl.ANY)
    limit = pltpu.CompilerParams(vmem_limit_bytes=16 * 2**20)

    preds, done = pl.pallas_call(
        pred_kernel,
        out_shape=(
            jax.ShapeDtypeStruct((3, horizons * frames, width), BF16),
            jax.ShapeDtypeStruct((1, 128), F32),
        ),
        in_specs=[anywhere] * 3 + [vmem],
        out_specs=(vmem, vmem),
        scratch_shapes=[pltpu.VMEM((3 * frames, width), BF16), pltpu.SemaphoreType.DMA((3,))],
        compiler_params=limit,
        cost_estimate=pl.CostEstimate(flops=1600000000, bytes_accessed=6500000, transcendentals=0),
    )(low2, ctx, high2, weights)

    _, later = lax.optimization_barrier((done, rows_ring))
    rows_cross = other_core(later)

    pred_cols, code_cols = horizons * width // parts, width // parts
    lanes = pred_cols + code_cols
    core_word = jnp.stack([core, lax.axis_index("y"), lax.axis_index(ALL), tm])
    core_word = core_word.reshape(1, 4).astype(jnp.int32)
    ring = lax.axis_size("y")
    *deltas, loss_part = pl.pallas_call(
        functools.partial(delta_kernel, horizons, windows),
        out_shape=[jax.ShapeDtypeStruct((2, frames, lanes), BF16)] * ring
        + [jax.ShapeDtypeStruct((1, 128), F32)],
        in_specs=[smem] + [vmem] * 3 + [anywhere] * 10,
        out_specs=[vmem] * (ring + 1),
        scratch_shapes=[
            pltpu.VMEM((11 * frames, width), BF16),
            pltpu.VMEM((frames, width), F32),
            pltpu.VMEM((4 * frames, width), BF16),
            pltpu.VMEM((2, horizons * frames, width), BF16),
            pltpu.VMEM((ring, 2, frames, lanes), BF16),
            pltpu.SemaphoreType.DMA((13,)),
        ],
        compiler_params=pltpu.CompilerParams(vmem_limit_bytes=20 * 2**20),
        cost_estimate=pl.CostEstimate(
            flops=4000000000, bytes_accessed=12000000, transcendentals=900000
        ),
    )(
        core_word, flags, preds, weights,
        both, low2, high2, low4, high4, both_x, low2_x, high2_x, low4_x, high4_x,
    )

    _, rows_ring = lax.optimization_barrier((loss_part, rows_ring))
    rows_cross = other_core(rows_ring)
    same = [deltas[0]] + [ring_shift(deltas[step], ("y",), step) for step in range(1, ring)]
    cross = [other_core(block) for block in same]
    terms = pl.pallas_call(
        functools.partial(term_kernel, pred_cols),
        out_shape=jax.ShapeDtypeStruct((plane, width // plane * lanes // 128 + 16, 128), BF16),
        in_specs=[smem] + [vmem] * 11,
        out_specs=vmem,
        scratch_shapes=[pltpu.VMEM((2, ring * frames, lanes), BF16)],
        compiler_params=limit,
        cost_estimate=pl.CostEstimate(flops=1600000000, bytes_accessed=6000000, transcendentals=0),
    )(core_word, loss_part, *same, *cross, rows_ring, rows_cross)

    owned = width // devices
    terms = lax.all_to_all(terms, PLANE, 0, 0, tiled=True)
    block = jax.ShapeDtypeStruct((2, 2 * owned, lanes), F32)
    sums = pl.pallas_call(
        sum_kernel,
        out_shape=[block] * ring,
        in_specs=[smem, vmem],
        out_specs=[vmem] * ring,
        scratch_shapes=[pltpu.VMEM((ring, 2, 2 * owned, lanes), F32)],
    )(core_word, terms)
    same = [sums[0]] + [ring_shift(sums[step], ("y",), step) for step in range(1, ring)]
    cross = [other_core(block) for block in same]
    loss, grad_pred, grad_proj = pl.pallas_call(
        gather_kernel,
        out_shape=(
            jax.ShapeDtypeStruct((1, 1), F32),
            jax.ShapeDtypeStruct((owned, horizons, width), F32),
            jax.ShapeDtypeStruct((owned, width), F32),
        ),
        in_specs=[smem] + [vmem] * 8,
        out_specs=(vmem, vmem, vmem),
        scratch_shapes=[pltpu.VMEM((parts, 2 * owned, lanes), F32)],
    )(core_word, *same, *cross)
    return (loss.reshape(()), grad_pred, grad_proj)


def solution(mesh):
    fine = Mesh(mesh.devices.reshape(4, 2, 8, 2, 2), ALL)
    placed = (P(DP, TM, None), P(DP, TM, None), P(), P(), P(DP, TM), P(DP, TM))
    return jax.shard_map(
        per_device,
        mesh=fine,
        in_specs=placed,
        out_specs=(P(), P(ALL, None, None), P(ALL, None)),
        check_vma=False,
    )
```

```python
import functools

import jax
import jax.numpy as jnp
from jax import lax
from jax.experimental import pallas as pl
from jax.experimental.pallas import tpu as pltpu
from jax.sharding import Mesh, PartitionSpec as P

DP = ("y", "xh")
TM = ("z", "xl", "core")
ALL = DP + TM
PLANE = ("xh", "z", "xl")
RING = ("y", "core")
CHIPS = ("y", "xh", "z", "xl")
F32 = jnp.float32
BF16 = jnp.bfloat16
REACH = 2


def size_of(names):
    size = 1
    for name in names:
        size *= lax.axis_size(name)
    return size


def ring_shift(block, axes, offset):
    size = size_of(axes)
    return lax.ppermute(block, axes, [((i + offset) % size, i) for i in range(size)])


def window_at(block, offset):
    return ring_shift(block, TM, offset)


def other_core(block):
    return lax.ppermute(block, "core", [(0, 1), (1, 0)])


def rows_dot(a, b):
    return lax.dot_general(a, b, (((1,), (1,)), ((), ())), preferred_element_type=F32)


def cols_dot(a, b):
    return lax.dot_general(a, b, (((0,), (0,)), ((), ())), preferred_element_type=F32)


def flag_terms(horizons, windows, device, tm, flags):
    chips, span = flags.shape
    frames = span // 2
    row = lax.broadcasted_iota(jnp.int32, flags.shape, 0)
    lane = lax.broadcasted_iota(jnp.int32, flags.shape, 1)
    last = row % (windows // 2) == windows // 2 - 1
    following = jnp.where(last, 0.0, pltpu.roll(flags, chips - 1, 0))
    slot = lax.broadcasted_iota(jnp.int32, (chips, 16), 1)
    source = lax.broadcasted_iota(jnp.int32, (chips, 16), 0)

    def picked(values, reach, transposed):
        window = slot - reach
        inside = (tm + window >= 0) & (tm + window < windows)
        out = 0.0
        for half in range(2):
            pick = (2 * source + half == device + window) & inside
            pick = jnp.where(pick, 1.0, 0.0).astype(BF16)
            part = values[:, half * frames : (half + 1) * frames].astype(BF16)
            out = out + (cols_dot(part, pick) if transposed else cols_dot(pick, part))
        return out

    total = jnp.zeros((1, span), F32)
    act = []
    for h in range(1, horizons + 1):
        ahead = jnp.where(
            lane < span - h, pltpu.roll(flags, span - h, 1), pltpu.roll(following, span - h, 1)
        )
        pairs = flags * ahead
        total = total + jnp.sum(pairs, axis=0, keepdims=True)
        act.append(picked(pairs, REACH, True))
    count = jnp.sum(total, axis=1, keepdims=True)
    return count, picked(flags, 2 * REACH, False), jnp.concatenate(act, axis=0)


def stacked_dot(rows, weights, out_ref):
    windows, stacked, width = out_ref.shape
    tile = 512
    frames = stacked * width // weights.shape[1]
    for at in range(0, weights.shape[1], tile):
        part = jnp.dot(rows, weights[:, at : at + tile], preferred_element_type=F32).astype(BF16)
        step, lane = divmod(at, width)
        for w in range(windows):
            out_ref[w, step * frames : (step + 1) * frames, lane : lane + tile] = part[
                w * frames : (w + 1) * frames
            ]


def pred_kernel(low2, ctx, high2, weights, out_ref, rows, sems):
    frames = ctx.shape[0]
    copies = [
        pltpu.make_async_copy(block, rows.at[pl.ds(slot * frames, frames)], sems.at[slot])
        for slot, block in enumerate(
            (low2.at[pl.ds(frames, frames)], ctx, high2.at[pl.ds(frames, frames)])
        )
    ]
    for copy in copies:
        copy.start()
    for copy in copies:
        copy.wait()
    stacked_dot(rows[...], weights, out_ref)


def delta_kernel(
    horizons, windows, core_ref, flags_ref, preds_ref, weights,
    both, low2, high2, low4, high4, both_x, low2_x, high2_x, low4_x, high4_x,
    out_0, out_1, out_2, out_3, loss_ref, codes, code_acc, odd_ctx, odd_pred, blocks, sems,
):
    frames, width = low4.shape
    scale = width ** (-0.5)
    ring, cores = blocks.shape[:2]
    parts = ring * cores
    pred_cols, code_cols = horizons * width // parts, width // parts
    core, place = core_ref[0, 0], core_ref[0, 1]

    def put(sem, block, start, held, slot):
        at = slot * frames
        if not isinstance(slot, int):
            at = pl.multiple_of(at, frames)
        return pltpu.make_async_copy(
            block.at[pl.ds(start, frames)], held.at[pl.ds(at, frames)], sems.at[sem]
        )

    ctx_copies = [
        put(0, low2_x, frames, odd_ctx, 1 - core),
        put(1, both_x, frames, odd_ctx, 2 - core),
        put(2, high2_x, frames, odd_ctx, 3 - core),
    ]
    code_copies = [
        put(3, low4, 0, codes, 1),
        put(4, low2, 0, codes, 3),
        put(5, both, 0, codes, 5),
        put(6, high2, 0, codes, 7),
        put(7, high4, 0, codes, 9),
        put(8, low4_x, 0, codes, 2 - 2 * core),
        put(9, low2_x, 0, codes, 4 - 2 * core),
        put(10, both_x, 0, codes, 6 - 2 * core),
        put(11, high2_x, 0, codes, 8 - 2 * core),
        put(12, high4_x, 0, codes, 10 - 2 * core),
    ]
    for copy in ctx_copies + code_copies:
        copy.start()
    for copy in ctx_copies:
        copy.wait()
    count, near, act = flag_terms(
        horizons, windows, core_ref[0, 2], core_ref[0, 3], flags_ref[...]
    )
    stacked_dot(odd_ctx[frames : 3 * frames], weights, odd_pred)
    for copy in code_copies:
        copy.wait()
    shape = (horizons * frames, frames)
    row = lax.broadcasted_iota(jnp.int32, shape, 0)
    ahead = row % frames + row // frames + 1
    col = lax.broadcasted_iota(jnp.int32, shape, 1)
    here, after = col == ahead, col == ahead - frames
    preds = {-2: preds_ref[0], -1: odd_pred[0], 0: preds_ref[1], 1: odd_pred[1], 2: preds_ref[2]}
    factor = (1.0 / jnp.maximum(count, 1.0)) * scale
    beside = (-2, -1, 1, 2)
    for window in (-2, -1, 1, 2, 0):
        base = (window + 3) * frames
        query = preds[window]
        scores = rows_dot(query, codes[base : base + 5 * frames]) * scale
        block = {
            d: scores[:, (d + 2) * frames : (d + 3) * frames] for d in range(-REACH, REACH + 1)
        }
        positive = jnp.sum(
            jnp.where(here, block[0], 0.0) + jnp.where(after, block[1], 0.0),
            axis=1,
            keepdims=True,
        )
        for d in beside:
            usable = near[window + d + 4 : window + d + 5]
            block[d] = jnp.where(usable > 0, block[d], -1e30)
        top = jnp.maximum(jnp.maximum(block[-2], block[-1]), jnp.maximum(block[1], block[2]))
        top = jnp.maximum(positive, jnp.max(top, axis=1, keepdims=True))
        total = sum(jnp.exp(block[d] - top) for d in beside)
        total = jnp.sum(total, axis=1, keepdims=True)
        log_total = top + jnp.log(jnp.exp(positive - top) + total)
        active = act[:, window + 2 : window + 3]
        weight = factor * active
        pos_coef = weight * (jnp.exp(positive - log_total) - 1.0)
        pos_after = jnp.where(after, pos_coef, 0.0).astype(BF16)
        if window != 0:
            coef = (weight * jnp.exp(block[-window] - log_total)).astype(BF16)
            term = cols_dot(coef, query)
            if window == -1:
                term = term + cols_dot(pos_after, query)
            if window == -2:
                code_acc[...] = term
            else:
                code_acc[...] += term
        else:
            coefs = {d: (weight * jnp.exp(block[d] - log_total)).astype(BF16) for d in beside}
            coefs[0] = jnp.where(here, pos_coef, 0.0).astype(BF16)
            wide = jnp.concatenate([coefs[d] for d in range(-REACH, REACH + 1)], axis=1)
            delta = jnp.dot(
                wide, codes[base : base + 5 * frames], preferred_element_type=F32
            ) + jnp.dot(
                pos_after, codes[base + 3 * frames : base + 4 * frames], preferred_element_type=F32
            )
            delta = delta.astype(BF16)
            for part in range(parts):
                step, at = divmod(part * pred_cols, width)
                blocks[part // cores, part % cores, :, :pred_cols] = delta[
                    step * frames : (step + 1) * frames, at : at + pred_cols
                ]
            code_delta = (code_acc[...] + cols_dot(coefs[0], query)).astype(BF16)
            for part in range(parts):
                blocks[part // cores, part % cores, :, pred_cols:] = code_delta[
                    :, part * code_cols : (part + 1) * code_cols
                ]
            loss = jnp.sum(active * (log_total - positive), axis=0, keepdims=True)
            loss = loss * (1.0 / jnp.maximum(count, 1.0))
            loss_ref[...] = jnp.broadcast_to(loss, loss_ref.shape)
    for back, out in enumerate((out_0, out_1, out_2, out_3)):
        out[...] = blocks[(place + ring - back) % ring]


def term_kernel(
    pred_cols, core_ref, loss_ref, same_0, same_1, same_2, same_3, cross_0, cross_1, cross_2, cross_3,
    rows_same, rows_cross, out_ref, held,
):
    _, frames, lanes_all = same_0.shape
    plane = out_ref.shape[0]
    core, place = core_ref[0, 0], core_ref[0, 1]
    both = ((same_0, same_1, same_2, same_3), (cross_0, cross_1, cross_2, cross_3))
    ring = len(both[0])
    for side, blocks in enumerate(both):
        for spot, block in enumerate(blocks):
            start = pl.multiple_of((place + spot) % ring * frames, frames)
            held[side, pl.ds(start, frames)] = block[core]
    width = rows_same.shape[1] // 2
    rows = 2 * width // ring
    span = rows // plane
    depth = ring * span // 2
    for first, lanes in ((width, slice(0, pred_cols)), (0, slice(pred_cols, lanes_all))):
        for half in range(ring // 2):
            blocks = slice(first + half * rows, first + (half + 1) * rows)
            term = cols_dot(rows_same[:, blocks], held[0, :, lanes])
            term = term + cols_dot(rows_cross[:, blocks], held[1, :, lanes])
            term = term.reshape(2, plane, span // 2, -1)
            term = jnp.concatenate([term[0], term[1]], axis=1).astype(BF16)
            for tile in range(term.shape[2] // 128):
                at = (lanes.start // 128 + tile) * depth + half * span
                out_ref[:, at : at + span] = term[:, :, tile * 128 : (tile + 1) * 128]
    loss = loss_ref[...]
    high = loss.astype(BF16).astype(F32)
    middle = (loss - high).astype(BF16).astype(F32)
    row = lax.broadcasted_iota(jnp.int32, (16, 128), 0)
    terms = jnp.where(row == 0, high, jnp.where(row == 1, middle, loss - high - middle))
    terms = jnp.where(row < 3, terms, 0.0).astype(BF16)
    out_ref[:, out_ref.shape[1] - 16 :] = jnp.broadcast_to(terms[None], (plane, 16, 128))


def sum_kernel(core_ref, terms_ref, out_0, out_1, out_2, out_3, blocks):
    total = terms_ref[0].astype(F32)
    for source in range(1, terms_ref.shape[0]):
        total = total + terms_ref[source].astype(F32)
    place = core_ref[0, 1]
    ring, cores, rows, lanes = blocks.shape
    owned = rows // 2
    depth = ring * cores * owned
    loss = jnp.sum(total[total.shape[0] - 16 :, :1], axis=0, keepdims=True)
    for part in range(ring * cores):
        for tile in range(lanes // 128):
            at = tile * depth + part * owned
            blocks[part // cores, part % cores, :owned, tile * 128 : (tile + 1) * 128] = total[
                at : at + owned
            ]
        blocks[part // cores, part % cores, owned:] = jnp.broadcast_to(loss, (owned, lanes))
    for back, out in enumerate((out_0, out_1, out_2, out_3)):
        out[...] = blocks[(place + ring - back) % ring]


def gather_kernel(
    core_ref, same_0, same_1, same_2, same_3, cross_0, cross_1, cross_2, cross_3,
    loss_ref, pred_ref, proj_ref, held,
):
    core, place = core_ref[0, 0], core_ref[0, 1]
    both = ((same_0, same_1, same_2, same_3), (cross_0, cross_1, cross_2, cross_3))
    ring = len(both[0])
    for side, blocks in enumerate(both):
        for spot, block in enumerate(blocks):
            source = 2 * ((place + spot) % ring) + (core if side == 0 else 1 - core)
            held[source] = block[core]
    parts, rows, lanes = held.shape
    owned, horizons, width = pred_ref.shape
    code_cols = width // parts
    pred_cols = lanes - code_cols
    loss = jnp.zeros((1, 1), F32)
    for part in range(parts):
        block = held[part]
        step, at = divmod(part * pred_cols, width)
        pred_ref[:, step, at : at + pred_cols] = block[:owned, :pred_cols]
        proj_ref[:, part * code_cols : (part + 1) * code_cols] = block[:owned, pred_cols:]
        loss = loss + block[owned : owned + 1, :1]
    loss_ref[...] = loss


def per_device(features, context, predictor, projection, lengths, frame_mask):
    frames, width = features.shape[1], features.shape[2]
    horizons = predictor.shape[1]
    feat, ctx = features[0], context[0]
    windows, recordings = size_of(TM), size_of(DP)
    devices = windows * recordings
    parts, plane = size_of(RING), size_of(PLANE)
    tm = lax.axis_index(TM)
    core = lax.axis_index("core")

    encoded = jnp.dot(feat, projection, preferred_element_type=F32).astype(BF16)
    both = jnp.concatenate([encoded, ctx], axis=0)
    low2, high2 = window_at(both, -2), window_at(both, 2)
    both_x = other_core(both)
    positions = lax.broadcasted_iota(jnp.int32, (1, frames), 1)
    usable = ((frame_mask == 1) & (positions < lengths)).astype(F32)
    usable_x = other_core(usable)
    pair = jnp.concatenate(
        [jnp.where(core == 0, usable, usable_x), jnp.where(core == 0, usable_x, usable)], axis=1
    )
    pair, both_x = lax.optimization_barrier((pair, both_x))
    chips = size_of(CHIPS)
    flags = lax.all_to_all(
        jnp.broadcast_to(pair, (chips, 2 * frames)), CHIPS, 0, 0, tiled=True
    )
    low4, high4 = window_at(encoded, -4), window_at(encoded, 4)
    weights = predictor.reshape(width, horizons * width)
    low2, high2, weights, flags = lax.optimization_barrier((low2, high2, weights, flags))
    low2_x, high2_x = other_core(low2), other_core(high2)
    low4_x, high4_x = other_core(low4), other_core(high4)
    rows_ring = lax.all_gather(jnp.concatenate([feat, ctx], axis=1), "y", tiled=True)

    smem = pl.BlockSpec(memory_space=pltpu.SMEM)
    vmem = pl.BlockSpec(memory_space=pltpu.VMEM)
    anywhere = pl.BlockSpec(memory_space=pl.ANY)
    limit = pltpu.CompilerParams(vmem_limit_bytes=16 * 2**20)

    preds = pl.pallas_call(
        pred_kernel,
        out_shape=jax.ShapeDtypeStruct((3, horizons * frames, width), BF16),
        in_specs=[anywhere] * 3 + [vmem],
        out_specs=vmem,
        scratch_shapes=[pltpu.VMEM((3 * frames, width), BF16), pltpu.SemaphoreType.DMA((3,))],
        compiler_params=limit,
        cost_estimate=pl.CostEstimate(flops=1600000000, bytes_accessed=6500000, transcendentals=0),
    )(low2, ctx, high2, weights)

    rows_cross = other_core(rows_ring)

    pred_cols, code_cols = horizons * width // parts, width // parts
    lanes = pred_cols + code_cols
    core_word = jnp.stack([core, lax.axis_index("y"), lax.axis_index(ALL), tm])
    core_word = core_word.reshape(1, 4).astype(jnp.int32)
    ring = lax.axis_size("y")
    *deltas, loss_part = pl.pallas_call(
        functools.partial(delta_kernel, horizons, windows),
        out_shape=[jax.ShapeDtypeStruct((2, frames, lanes), BF16)] * ring
        + [jax.ShapeDtypeStruct((1, 128), F32)],
        in_specs=[smem] + [vmem] * 3 + [anywhere] * 10,
        out_specs=[vmem] * (ring + 1),
        scratch_shapes=[
            pltpu.VMEM((11 * frames, width), BF16),
            pltpu.VMEM((frames, width), F32),
            pltpu.VMEM((4 * frames, width), BF16),
            pltpu.VMEM((2, horizons * frames, width), BF16),
            pltpu.VMEM((ring, 2, frames, lanes), BF16),
            pltpu.SemaphoreType.DMA((13,)),
        ],
        compiler_params=pltpu.CompilerParams(vmem_limit_bytes=20 * 2**20),
        cost_estimate=pl.CostEstimate(
            flops=4000000000, bytes_accessed=12000000, transcendentals=900000
        ),
    )(
        core_word, flags, preds, weights,
        both, low2, high2, low4, high4, both_x, low2_x, high2_x, low4_x, high4_x,
    )

    _, rows_ring = lax.optimization_barrier((loss_part, rows_ring))
    rows_cross = other_core(rows_ring)
    same = [deltas[0]] + [ring_shift(deltas[step], ("y",), step) for step in range(1, ring)]
    cross = [other_core(block) for block in same]
    terms = pl.pallas_call(
        functools.partial(term_kernel, pred_cols),
        out_shape=jax.ShapeDtypeStruct((plane, width // plane * lanes // 128 + 16, 128), BF16),
        in_specs=[smem] + [vmem] * 11,
        out_specs=vmem,
        scratch_shapes=[pltpu.VMEM((2, ring * frames, lanes), BF16)],
        compiler_params=limit,
        cost_estimate=pl.CostEstimate(flops=1600000000, bytes_accessed=6000000, transcendentals=0),
    )(core_word, loss_part, *same, *cross, rows_ring, rows_cross)

    owned = width // devices
    terms = lax.all_to_all(terms, PLANE, 0, 0, tiled=True)
    block = jax.ShapeDtypeStruct((2, 2 * owned, lanes), F32)
    sums = pl.pallas_call(
        sum_kernel,
        out_shape=[block] * ring,
        in_specs=[smem, vmem],
        out_specs=[vmem] * ring,
        scratch_shapes=[pltpu.VMEM((ring, 2, 2 * owned, lanes), F32)],
    )(core_word, terms)
    same = [sums[0]] + [ring_shift(sums[step], ("y",), step) for step in range(1, ring)]
    cross = [other_core(block) for block in same]
    loss, grad_pred, grad_proj = pl.pallas_call(
        gather_kernel,
        out_shape=(
            jax.ShapeDtypeStruct((1, 1), F32),
            jax.ShapeDtypeStruct((owned, horizons, width), F32),
            jax.ShapeDtypeStruct((owned, width), F32),
        ),
        in_specs=[smem] + [vmem] * 8,
        out_specs=(vmem, vmem, vmem),
        scratch_shapes=[pltpu.VMEM((parts, 2 * owned, lanes), F32)],
    )(core_word, *same, *cross)
    return (loss.reshape(()), grad_pred, grad_proj)


def solution(mesh):
    fine = Mesh(mesh.devices.reshape(4, 2, 8, 2, 2), ALL)
    placed = (P(DP, TM, None), P(DP, TM, None), P(), P(), P(DP, TM), P(DP, TM))
    return jax.shard_map(
        per_device,
        mesh=fine,
        in_specs=placed,
        out_specs=(P(), P(ALL, None, None), P(ALL, None)),
        check_vma=False,
    )
```

```python
import functools

import jax
import jax.numpy as jnp
from jax import lax
from jax.experimental import pallas as pl
from jax.experimental.pallas import tpu as pltpu
from jax.sharding import Mesh, PartitionSpec as P

DP = ("y", "xh")
TM = ("z", "xl", "core")
ALL = DP + TM
PLANE = ("xh", "z", "xl")
RING = ("y", "core")
CHIPS = ("y", "xh", "z", "xl")
F32 = jnp.float32
BF16 = jnp.bfloat16
REACH = 2


def size_of(names):
    size = 1
    for name in names:
        size *= lax.axis_size(name)
    return size


def ring_shift(block, axes, offset):
    size = size_of(axes)
    return lax.ppermute(block, axes, [((i + offset) % size, i) for i in range(size)])


def window_at(block, offset):
    return ring_shift(block, TM, offset)


def other_core(block):
    return lax.ppermute(block, "core", [(0, 1), (1, 0)])


def rows_dot(a, b):
    return lax.dot_general(a, b, (((1,), (1,)), ((), ())), preferred_element_type=F32)


def cols_dot(a, b):
    return lax.dot_general(a, b, (((0,), (0,)), ((), ())), preferred_element_type=F32)


def flag_terms(horizons, windows, device, tm, flags):
    chips, span = flags.shape
    frames = span // 2
    row = lax.broadcasted_iota(jnp.int32, flags.shape, 0)
    lane = lax.broadcasted_iota(jnp.int32, flags.shape, 1)
    last = row % (windows // 2) == windows // 2 - 1
    following = jnp.where(last, 0.0, pltpu.roll(flags, chips - 1, 0))
    slot = lax.broadcasted_iota(jnp.int32, (chips, 16), 1)
    source = lax.broadcasted_iota(jnp.int32, (chips, 16), 0)

    def picked(values, reach, transposed):
        window = slot - reach
        inside = (tm + window >= 0) & (tm + window < windows)
        out = 0.0
        for half in range(2):
            pick = (2 * source + half == device + window) & inside
            pick = jnp.where(pick, 1.0, 0.0).astype(BF16)
            part = values[:, half * frames : (half + 1) * frames].astype(BF16)
            out = out + (cols_dot(part, pick) if transposed else cols_dot(pick, part))
        return out

    total = jnp.zeros((1, span), F32)
    act = []
    for h in range(1, horizons + 1):
        ahead = jnp.where(
            lane < span - h, pltpu.roll(flags, span - h, 1), pltpu.roll(following, span - h, 1)
        )
        pairs = flags * ahead
        total = total + jnp.sum(pairs, axis=0, keepdims=True)
        act.append(picked(pairs, REACH, True))
    count = jnp.sum(total, axis=1, keepdims=True)
    return count, picked(flags, 2 * REACH, False), jnp.concatenate(act, axis=0)


def stacked_dot(rows, weights, out_ref):
    windows, stacked, width = out_ref.shape
    tile = 512
    frames = stacked * width // weights.shape[1]
    for at in range(0, weights.shape[1], tile):
        part = jnp.dot(rows, weights[:, at : at + tile], preferred_element_type=F32).astype(BF16)
        step, lane = divmod(at, width)
        for w in range(windows):
            out_ref[w, step * frames : (step + 1) * frames, lane : lane + tile] = part[
                w * frames : (w + 1) * frames
            ]


def pred_kernel(low2, ctx, high2, weights, out_ref, done_ref, rows, sems):
    frames = ctx.shape[0]
    copies = [
        pltpu.make_async_copy(block, rows.at[pl.ds(slot * frames, frames)], sems.at[slot])
        for slot, block in enumerate(
            (low2.at[pl.ds(frames, frames)], ctx, high2.at[pl.ds(frames, frames)])
        )
    ]
    for copy in copies:
        copy.start()
    for copy in copies:
        copy.wait()
    stacked_dot(rows[...], weights, out_ref)
    done_ref[...] = jnp.zeros_like(done_ref)


def delta_kernel(
    horizons, windows, core_ref, flags_ref, preds_ref, weights,
    both, low2, high2, low4, high4, both_x, low2_x, high2_x, low4_x, high4_x,
    out_0, out_1, out_2, out_3, loss_ref, codes, code_acc, odd_ctx, odd_pred, blocks, sems,
):
    frames, width = low4.shape
    scale = width ** (-0.5)
    ring, cores = blocks.shape[:2]
    parts = ring * cores
    pred_cols, code_cols = horizons * width // parts, width // parts
    core, place = core_ref[0, 0], core_ref[0, 1]

    def put(sem, block, start, held, slot):
        at = slot * frames
        if not isinstance(slot, int):
            at = pl.multiple_of(at, frames)
        return pltpu.make_async_copy(
            block.at[pl.ds(start, frames)], held.at[pl.ds(at, frames)], sems.at[sem]
        )

    ctx_copies = [
        put(0, low2_x, frames, odd_ctx, 1 - core),
        put(1, both_x, frames, odd_ctx, 2 - core),
        put(2, high2_x, frames, odd_ctx, 3 - core),
    ]
    code_copies = [
        put(3, low4, 0, codes, 1),
        put(4, low2, 0, codes, 3),
        put(5, both, 0, codes, 5),
        put(6, high2, 0, codes, 7),
        put(7, high4, 0, codes, 9),
        put(8, low4_x, 0, codes, 2 - 2 * core),
        put(9, low2_x, 0, codes, 4 - 2 * core),
        put(10, both_x, 0, codes, 6 - 2 * core),
        put(11, high2_x, 0, codes, 8 - 2 * core),
        put(12, high4_x, 0, codes, 10 - 2 * core),
    ]
    for copy in ctx_copies + code_copies:
        copy.start()
    for copy in ctx_copies:
        copy.wait()
    count, near, act = flag_terms(
        horizons, windows, core_ref[0, 2], core_ref[0, 3], flags_ref[...]
    )
    stacked_dot(odd_ctx[frames : 3 * frames], weights, odd_pred)
    for copy in code_copies:
        copy.wait()
    shape = (horizons * frames, frames)
    row = lax.broadcasted_iota(jnp.int32, shape, 0)
    ahead = row % frames + row // frames + 1
    col = lax.broadcasted_iota(jnp.int32, shape, 1)
    here, after = col == ahead, col == ahead - frames
    preds = {-2: preds_ref[0], -1: odd_pred[0], 0: preds_ref[1], 1: odd_pred[1], 2: preds_ref[2]}
    factor = (1.0 / jnp.maximum(count, 1.0)) * scale
    beside = (-2, -1, 1, 2)
    for window in (-2, -1, 1, 2, 0):
        base = (window + 3) * frames
        query = preds[window]
        scores = rows_dot(query, codes[base : base + 5 * frames]) * scale
        block = {
            d: scores[:, (d + 2) * frames : (d + 3) * frames] for d in range(-REACH, REACH + 1)
        }
        positive = jnp.sum(
            jnp.where(here, block[0], 0.0) + jnp.where(after, block[1], 0.0),
            axis=1,
            keepdims=True,
        )
        for d in beside:
            usable = near[window + d + 4 : window + d + 5]
            block[d] = jnp.where(usable > 0, block[d], -1e30)
        top = jnp.maximum(jnp.maximum(block[-2], block[-1]), jnp.maximum(block[1], block[2]))
        top = jnp.maximum(positive, jnp.max(top, axis=1, keepdims=True))
        total = sum(jnp.exp(block[d] - top) for d in beside)
        total = jnp.sum(total, axis=1, keepdims=True)
        log_total = top + jnp.log(jnp.exp(positive - top) + total)
        active = act[:, window + 2 : window + 3]
        weight = factor * active
        pos_coef = weight * (jnp.exp(positive - log_total) - 1.0)
        pos_after = jnp.where(after, pos_coef, 0.0).astype(BF16)
        if window != 0:
            coef = (weight * jnp.exp(block[-window] - log_total)).astype(BF16)
            term = cols_dot(coef, query)
            if window == -1:
                term = term + cols_dot(pos_after, query)
            if window == -2:
                code_acc[...] = term
            else:
                code_acc[...] += term
        else:
            coefs = {d: (weight * jnp.exp(block[d] - log_total)).astype(BF16) for d in beside}
            coefs[0] = jnp.where(here, pos_coef, 0.0).astype(BF16)
            wide = jnp.concatenate([coefs[d] for d in range(-REACH, REACH + 1)], axis=1)
            delta = jnp.dot(
                wide, codes[base : base + 5 * frames], preferred_element_type=F32
            ) + jnp.dot(
                pos_after, codes[base + 3 * frames : base + 4 * frames], preferred_element_type=F32
            )
            delta = delta.astype(BF16)
            for part in range(parts):
                step, at = divmod(part * pred_cols, width)
                blocks[part // cores, part % cores, :, :pred_cols] = delta[
                    step * frames : (step + 1) * frames, at : at + pred_cols
                ]
            code_delta = (code_acc[...] + cols_dot(coefs[0], query)).astype(BF16)
            for part in range(parts):
                blocks[part // cores, part % cores, :, pred_cols:] = code_delta[
                    :, part * code_cols : (part + 1) * code_cols
                ]
            loss = jnp.sum(active * (log_total - positive), axis=0, keepdims=True)
            loss = loss * (1.0 / jnp.maximum(count, 1.0))
            loss_ref[...] = jnp.broadcast_to(loss, loss_ref.shape)
    for back, out in enumerate((out_0, out_1, out_2, out_3)):
        out[...] = blocks[(place + ring - back) % ring]


def term_kernel(
    pred_cols, core_ref, loss_ref, same_0, same_1, same_2, same_3, cross_0, cross_1, cross_2, cross_3,
    rows_same, rows_cross, out_ref, held,
):
    _, frames, lanes_all = same_0.shape
    plane = out_ref.shape[0]
    core, place = core_ref[0, 0], core_ref[0, 1]
    both = ((same_0, same_1, same_2, same_3), (cross_0, cross_1, cross_2, cross_3))
    ring = len(both[0])
    for side, blocks in enumerate(both):
        for spot, block in enumerate(blocks):
            start = pl.multiple_of((place + spot) % ring * frames, frames)
            held[side, pl.ds(start, frames)] = block[core]
    width = rows_same.shape[1] // 2
    rows = 2 * width // ring
    span = rows // plane
    depth = ring * span // 2
    for first, lanes in ((width, slice(0, pred_cols)), (0, slice(pred_cols, lanes_all))):
        for half in range(ring // 2):
            blocks = slice(first + half * rows, first + (half + 1) * rows)
            term = cols_dot(rows_same[:, blocks], held[0, :, lanes])
            term = term + cols_dot(rows_cross[:, blocks], held[1, :, lanes])
            term = term.reshape(2, plane, span // 2, -1)
            term = jnp.concatenate([term[0], term[1]], axis=1).astype(BF16)
            for tile in range(term.shape[2] // 128):
                at = (lanes.start // 128 + tile) * depth + half * span
                out_ref[:, at : at + span] = term[:, :, tile * 128 : (tile + 1) * 128]
    loss = loss_ref[...]
    high = loss.astype(BF16).astype(F32)
    middle = (loss - high).astype(BF16).astype(F32)
    row = lax.broadcasted_iota(jnp.int32, (16, 128), 0)
    terms = jnp.where(row == 0, high, jnp.where(row == 1, middle, loss - high - middle))
    terms = jnp.where(row < 3, terms, 0.0).astype(BF16)
    out_ref[:, out_ref.shape[1] - 16 :] = jnp.broadcast_to(terms[None], (plane, 16, 128))


def sum_kernel(core_ref, terms_ref, out_0, out_1, out_2, out_3, blocks):
    total = terms_ref[0].astype(F32)
    for source in range(1, terms_ref.shape[0]):
        total = total + terms_ref[source].astype(F32)
    place = core_ref[0, 1]
    ring, cores, rows, lanes = blocks.shape
    owned = rows // 2
    depth = ring * cores * owned
    loss = jnp.sum(total[total.shape[0] - 16 :, :1], axis=0, keepdims=True)
    for part in range(ring * cores):
        for tile in range(lanes // 128):
            at = tile * depth + part * owned
            blocks[part // cores, part % cores, :owned, tile * 128 : (tile + 1) * 128] = total[
                at : at + owned
            ]
        blocks[part // cores, part % cores, owned:] = jnp.broadcast_to(loss, (owned, lanes))
    for back, out in enumerate((out_0, out_1, out_2, out_3)):
        out[...] = blocks[(place + ring - back) % ring]


def gather_kernel(
    core_ref, same_0, same_1, same_2, same_3, cross_0, cross_1, cross_2, cross_3,
    loss_ref, pred_ref, proj_ref, held,
):
    core, place = core_ref[0, 0], core_ref[0, 1]
    both = ((same_0, same_1, same_2, same_3), (cross_0, cross_1, cross_2, cross_3))
    ring = len(both[0])
    for side, blocks in enumerate(both):
        for spot, block in enumerate(blocks):
            source = 2 * ((place + spot) % ring) + (core if side == 0 else 1 - core)
            held[source] = block[core]
    parts, rows, lanes = held.shape
    owned, horizons, width = pred_ref.shape
    code_cols = width // parts
    pred_cols = lanes - code_cols
    loss = jnp.zeros((1, 1), F32)
    for part in range(parts):
        block = held[part]
        step, at = divmod(part * pred_cols, width)
        pred_ref[:, step, at : at + pred_cols] = block[:owned, :pred_cols]
        proj_ref[:, part * code_cols : (part + 1) * code_cols] = block[:owned, pred_cols:]
        loss = loss + block[owned : owned + 1, :1]
    loss_ref[...] = loss


def per_device(features, context, predictor, projection, lengths, frame_mask):
    frames, width = features.shape[1], features.shape[2]
    horizons = predictor.shape[1]
    feat, ctx = features[0], context[0]
    windows, recordings = size_of(TM), size_of(DP)
    devices = windows * recordings
    parts, plane = size_of(RING), size_of(PLANE)
    tm = lax.axis_index(TM)
    core = lax.axis_index("core")

    encoded = jnp.dot(feat, projection, preferred_element_type=F32).astype(BF16)
    both = jnp.concatenate([encoded, ctx], axis=0)
    low2, high2 = window_at(both, -2), window_at(both, 2)
    both_x = other_core(both)
    positions = lax.broadcasted_iota(jnp.int32, (1, frames), 1)
    usable = ((frame_mask == 1) & (positions < lengths)).astype(F32)
    usable_x = other_core(usable)
    pair = jnp.concatenate(
        [jnp.where(core == 0, usable, usable_x), jnp.where(core == 0, usable_x, usable)], axis=1
    )
    pair, both_x = lax.optimization_barrier((pair, both_x))
    chips = size_of(CHIPS)
    flags = lax.all_to_all(
        jnp.broadcast_to(pair, (chips, 2 * frames)), CHIPS, 0, 0, tiled=True
    )
    low4, high4 = window_at(encoded, -4), window_at(encoded, 4)
    weights = predictor.reshape(width, horizons * width)
    low2, high2, weights, flags = lax.optimization_barrier((low2, high2, weights, flags))
    low2_x, high2_x = other_core(low2), other_core(high2)
    low4_x, high4_x = other_core(low4), other_core(high4)
    rows_ring = lax.all_gather(jnp.concatenate([feat, ctx], axis=1), "y", tiled=True)

    smem = pl.BlockSpec(memory_space=pltpu.SMEM)
    vmem = pl.BlockSpec(memory_space=pltpu.VMEM)
    anywhere = pl.BlockSpec(memory_space=pl.ANY)
    limit = pltpu.CompilerParams(vmem_limit_bytes=10 * 2**20)

    preds, done = pl.pallas_call(
        pred_kernel,
        out_shape=(
            jax.ShapeDtypeStruct((3, horizons * frames, width), BF16),
            jax.ShapeDtypeStruct((1, 128), F32),
        ),
        in_specs=[anywhere] * 3 + [vmem],
        out_specs=(vmem, vmem),
        scratch_shapes=[pltpu.VMEM((3 * frames, width), BF16), pltpu.SemaphoreType.DMA((3,))],
        compiler_params=limit,
        cost_estimate=pl.CostEstimate(flops=1600000000, bytes_accessed=6500000, transcendentals=0),
    )(low2, ctx, high2, weights)

    _, later = lax.optimization_barrier((done, rows_ring))
    rows_cross = other_core(later)

    pred_cols, code_cols = horizons * width // parts, width // parts
    lanes = pred_cols + code_cols
    core_word = jnp.stack([core, lax.axis_index("y"), lax.axis_index(ALL), tm])
    core_word = core_word.reshape(1, 4).astype(jnp.int32)
    ring = lax.axis_size("y")
    *deltas, loss_part = pl.pallas_call(
        functools.partial(delta_kernel, horizons, windows),
        out_shape=[jax.ShapeDtypeStruct((2, frames, lanes), BF16)] * ring
        + [jax.ShapeDtypeStruct((1, 128), F32)],
        in_specs=[smem] + [vmem] * 3 + [anywhere] * 10,
        out_specs=[vmem] * (ring + 1),
        scratch_shapes=[
            pltpu.VMEM((11 * frames, width), BF16),
            pltpu.VMEM((frames, width), F32),
            pltpu.VMEM((4 * frames, width), BF16),
            pltpu.VMEM((2, horizons * frames, width), BF16),
            pltpu.VMEM((ring, 2, frames, lanes), BF16),
            pltpu.SemaphoreType.DMA((13,)),
        ],
        compiler_params=pltpu.CompilerParams(vmem_limit_bytes=16 * 2**20),
        cost_estimate=pl.CostEstimate(
            flops=4000000000, bytes_accessed=12000000, transcendentals=900000
        ),
    )(
        core_word, flags, preds, weights,
        both, low2, high2, low4, high4, both_x, low2_x, high2_x, low4_x, high4_x,
    )

    _, rows_ring = lax.optimization_barrier((loss_part, rows_ring))
    rows_cross = other_core(rows_ring)
    same = [deltas[0]] + [ring_shift(deltas[step], ("y",), step) for step in range(1, ring)]
    cross = [other_core(block) for block in same]
    terms = pl.pallas_call(
        functools.partial(term_kernel, pred_cols),
        out_shape=jax.ShapeDtypeStruct((plane, width // plane * lanes // 128 + 16, 128), BF16),
        in_specs=[smem] + [vmem] * 11,
        out_specs=vmem,
        scratch_shapes=[pltpu.VMEM((2, ring * frames, lanes), BF16)],
        compiler_params=limit,
        cost_estimate=pl.CostEstimate(flops=1600000000, bytes_accessed=6000000, transcendentals=0),
    )(core_word, loss_part, *same, *cross, rows_ring, rows_cross)

    owned = width // devices
    terms = lax.all_to_all(terms, PLANE, 0, 0, tiled=True)
    block = jax.ShapeDtypeStruct((2, 2 * owned, lanes), F32)
    sums = pl.pallas_call(
        sum_kernel,
        out_shape=[block] * ring,
        in_specs=[smem, vmem],
        out_specs=[vmem] * ring,
        scratch_shapes=[pltpu.VMEM((ring, 2, 2 * owned, lanes), F32)],
    )(core_word, terms)
    same = [sums[0]] + [ring_shift(sums[step], ("y",), step) for step in range(1, ring)]
    cross = [other_core(block) for block in same]
    loss, grad_pred, grad_proj = pl.pallas_call(
        gather_kernel,
        out_shape=(
            jax.ShapeDtypeStruct((1, 1), F32),
            jax.ShapeDtypeStruct((owned, horizons, width), F32),
            jax.ShapeDtypeStruct((owned, width), F32),
        ),
        in_specs=[smem] + [vmem] * 8,
        out_specs=(vmem, vmem, vmem),
        scratch_shapes=[pltpu.VMEM((parts, 2 * owned, lanes), F32)],
    )(core_word, *same, *cross)
    return (loss.reshape(()), grad_pred, grad_proj)


def solution(mesh):
    fine = Mesh(mesh.devices.reshape(4, 2, 8, 2, 2), ALL)
    placed = (P(DP, TM, None), P(DP, TM, None), P(), P(), P(DP, TM), P(DP, TM))
    return jax.shard_map(
        per_device,
        mesh=fine,
        in_specs=placed,
        out_specs=(P(), P(ALL, None, None), P(ALL, None)),
        check_vma=False,
    )
```
